32 devices in a mesh: wide: 8 (over y, x, core), narrow: 4 (over z).
Axes of the slice: x: 2, y: 2, z: 4, core: 2. Of those that a mesh axis runs over, the one named last changes fastest.
Arguments:
- tokens: bfloat16 [98304, 768], P(('wide', 'narrow')), may hold values from -6 to 6
- cotangent: bfloat16 [98304, 768], P(('wide', 'narrow')), may hold values from -6 to 6
- segments: int32 [96, 1024], P(('wide', 'narrow')), may hold values from 0 to 7, never falling along the last dimension, each value on 1 to 512 neighbouring positions
- picks: int32 [96, 128], P(('wide', 'narrow')), may hold values from 0 to 1023, as said below
- w_qkv: float32 [768, 2304], P(('wide', 'narrow')), may hold values from -0.21875 to 0.21875
- w_out: float32 [768, 768], P(('wide', 'narrow')), may hold values from -0.625 to 0.625
- w_up: float32 [768, 3072], P(('wide', 'narrow')), may hold values from -0.21875 to 0.21875
- w_down: float32 [3072, 768], P(('wide', 'narrow')), may hold values from -0.109375 to 0.109375
- vectors: float32 [3, 768], P(None, ('wide', 'narrow')), may hold values from -1 to 2.5
- m_qkv: float32 [768, 2304], P(('wide', 'narrow')), may hold values from -0.75 to 0.75
- m_out: float32 [768, 768], P(('wide', 'narrow')), may hold values from -0.75 to 0.75
- m_up: float32 [768, 3072], P(('wide', 'narrow')), may hold values from -0.75 to 0.75
- m_down: float32 [3072, 768], P(('wide', 'narrow')), may hold values from -0.75 to 0.75
- m_vectors: float32 [3, 768], P(None, ('wide', 'narrow')), may hold values from -0.75 to 0.75
- v_qkv: float32 [768, 2304], P(('wide', 'narrow')), may hold values from 0.0012288 to 0.0049152
- v_out: float32 [768, 768], P(('wide', 'narrow')), may hold values from 0.0012288 to 0.0049152
- v_up: float32 [768, 3072], P(('wide', 'narrow')), may hold values from 0.0012288 to 0.0049152
- v_down: float32 [3072, 768], P(('wide', 'narrow')), may hold values from 0.0012288 to 0.0049152
- v_vectors: float32 [3, 768], P(None, ('wide', 'narrow')), may hold values from 0.24576 to 0.98304
Outputs:
- mixed: bfloat16 [98304, 768], P(('wide', 'narrow'))
- input_grad: bfloat16 [98304, 768], P(('wide', 'narrow'))
- grad_norm: float32 [], replicated
- new_qkv: float32 [768, 2304], P(('wide', 'narrow'))
- new_out: float32 [768, 768], P(('wide', 'narrow'))
- new_up: float32 [768, 3072], P(('wide', 'narrow'))
- new_down: float32 [3072, 768], P(('wide', 'narrow'))
- first_qkv: float32 [768, 2304], P(('wide', 'narrow'))
- first_out: float32 [768, 768], P(('wide', 'narrow'))
- first_up: float32 [768, 3072], P(('wide', 'narrow'))
- first_down: float32 [3072, 768], P(('wide', 'narrow'))
- first_vectors: float32 [3, 768], P(None, ('wide', 'narrow'))
- second_qkv: float32 [768, 2304], P(('wide', 'narrow'))
- second_out: float32 [768, 768], P(('wide', 'narrow'))
- second_up: float32 [768, 3072], P(('wide', 'narrow'))
- second_down: float32 [3072, 768], P(('wide', 'narrow'))
- second_vectors: float32 [3, 768], P(None, ('wide', 'narrow'))
The draws below stay inside these ranges and needn't reach their ends.
Inputs may be any that keep to these rules, and one draw needn't show every extreme that they name: `picks`: each row holds 128 distinct positions of its sequence in rising order.
All inputs are finite; a program needn't handle non-finite values.
Results may differ from the reference program's by a relative error of at most 0.012.
The reference program's roundings to bfloat16 on the way count: a program that leaves them out, or rounds other values in their place, can miss the bound.
Values may be sent and summed in bfloat16 or wider, within the bound.
No kernel may reach another device: no remote copies, remote signals or barrier semaphores. Data moves between devices by JAX's collectives and lax.ppermute only.
A program may use at most 192 MiB of HBM per device.

```python
import math
import jax
import jax.numpy as jnp
import numpy as np
from jax import lax

D = 768
FF = 3072
HEADS = 12
HEAD_DIM = 64
LEN = 1024
TOPK = 128
SEQS = 96
TOKENS = 98304
SELECTED = 12288
PARAMS = 7080192


def draw_picks(key, part):
    row_keys = jax.random.split(key, SEQS)

    def one_row(row_key):
        order = jax.random.permutation(row_key, LEN)
        return jnp.nonzero(order < TOPK, size=TOPK)[0].astype(jnp.int32)
    return jax.vmap(one_row)(row_keys)


def draw_vectors(key, part):
    key_gain, key_router = jax.random.split(key, 2)
    along = jnp.arange(D, dtype=jnp.float32) / (D - 1)
    trend = 0.5 + along
    rough = jax.random.uniform(key_gain, (2, D), jnp.float32, 0.8, 1.25)
    gain_rows = trend[None, :] * rough
    router_row = jax.random.truncated_normal(key_router, -4.0, 4.0, (1, D), jnp.float32) * D ** (-0.5)
    return jnp.concatenate([gain_rows, router_row], axis=0)


def block_levels(key, extent, pieces, low, largest):
    loudness = 1.0
    for position, shards_of in pieces:
        heights = jax.random.uniform(jax.random.fold_in(jax.random.fold_in(key, 6), position), (shards_of,), jnp.float32, low / len(pieces), largest / len(pieces))
        loudness = loudness * jnp.repeat(jnp.exp(heights), extent[position] // shards_of).reshape((-1,) + (1,) * (len(extent) - 1 - position))
    return loudness


def length_profile(amount, total, limit, slope):
    loads = [(1 << 20) // math.isqrt(grade ** slope) + 1 for grade in range(2, amount + 1)]
    surplus, given = total - limit - (amount - 1), [1] * (amount - 1)
    while surplus > 0:
        movable = [i for i in range(amount - 1) if given[i] < limit]
        pool, budget = sum([loads[i] for i in movable]), surplus
        for i in movable:
            more = min(limit - given[i], max(1, budget * loads[i] // pool), surplus)
            given[i] = given[i] + more
            surplus = surplus - more
    return np.array([limit] + given)


def ragged(key, count, total, reach, skew):
    if count == 2:
        one = jax.random.randint(key, (), max(1, total - reach), min(reach, total - 1) + 1)
        return jnp.stack([one, total - one])
    lengths = jnp.asarray(length_profile(count, total, reach, skew), jnp.int32)
    twos = (count - 1) // 2
    donor, taker = lengths[1:1 + 2 * twos:2], lengths[2:2 + 2 * twos:2]
    slack = jnp.minimum(donor - 1, reach - taker)
    passed = jax.random.randint(jax.random.fold_in(key, 1), (twos,), 0, 1 << 20) % (slack + 1)
    lengths = lengths.at[1:1 + 2 * twos:2].set(donor - passed).at[2:2 + 2 * twos:2].set(taker + passed)
    return lengths[jax.random.permutation(jax.random.fold_in(key, 2), count)]


def scatter_about(own_key, shape, spread, reach, cuts=(), kind=jnp.bfloat16):
    level = block_levels(own_key, shape, cuts, -0.22, 0.18) if cuts else 1.0
    array = jax.random.normal(own_key, shape, jnp.float32) * spread * level
    return jnp.minimum(jnp.maximum(array, -reach), reach).astype(kind)


def setup_inputs(seed: int = 0) -> dict:
    key_of = jax.random.split(jax.random.key(seed), 20)
    tokens = scatter_about(key_of[0], (TOKENS, D), 1.0, 6.0, ((0, 32),))
    cotangent = scatter_about(key_of[1], (TOKENS, D), 1.0, 6.0, ((0, 32),))
    segments = jax.vmap(lambda own: jnp.searchsorted(jnp.cumsum(ragged(own, 8, LEN, LEN // 2, 2)), jnp.arange(LEN), side="right"))(jax.random.split(key_of[2], SEQS)).reshape((SEQS, LEN)).astype(jnp.int32)
    picks = draw_picks(jax.random.fold_in(key_of[19], 71), 0)
    w_qkv = scatter_about(key_of[4], (D, 3 * D), D ** -0.5, 0.21875, ((0, 32),), jnp.float32)
    w_out = scatter_about(key_of[5], (D, D), (D // 8) ** -0.5, 0.625, ((0, 32),), jnp.float32)
    w_up = scatter_about(key_of[6], (D, FF), D ** -0.5, 0.21875, ((0, 32),), jnp.float32)
    w_down = scatter_about(key_of[7], (FF, D), FF ** -0.5, 0.109375, ((0, 32),), jnp.float32)
    vectors = draw_vectors(jax.random.fold_in(key_of[19], 71), 0)
    m_qkv = scatter_about(key_of[9], (D, 3 * D), (0.0011 * SELECTED ** 0.5), 0.75, ((0, 32),), jnp.float32)
    m_out = scatter_about(key_of[10], (D, D), (0.0011 * SELECTED ** 0.5), 0.75, ((0, 32),), jnp.float32)
    m_up = scatter_about(key_of[11], (D, FF), (0.0011 * SELECTED ** 0.5), 0.75, ((0, 32),), jnp.float32)
    m_down = scatter_about(key_of[12], (FF, D), (0.0011 * SELECTED ** 0.5), 0.75, ((0, 32),), jnp.float32)
    m_vectors = scatter_about(key_of[13], (3, D), (0.0011 * SELECTED ** 0.5), 0.75, ((1, 32),), jnp.float32)
    v_qkv = jnp.clip(jnp.exp(math.log(0.0049152) - 1.3862944 * jax.random.uniform(key_of[14], (D, 3 * D), jnp.float32) ** block_levels(key_of[14], (D, 3 * D), ((0, 32),), -0.2, 0.2)), 0.0012288, 0.0049152)
    v_out = jnp.clip(jnp.exp(math.log(0.0049152) - 1.3862944 * jax.random.uniform(key_of[15], (D, D), jnp.float32) ** block_levels(key_of[15], (D, D), ((0, 32),), -0.2, 0.2)), 0.0012288, 0.0049152)
    v_up = jnp.clip(jnp.exp(math.log(0.0049152) - 1.3862944 * jax.random.uniform(key_of[16], (D, FF), jnp.float32) ** block_levels(key_of[16], (D, FF), ((0, 32),), -0.2, 0.2)), 0.0012288, 0.0049152)
    v_down = jnp.clip(jnp.exp(math.log(0.0049152) - 1.3862944 * jax.random.uniform(key_of[17], (FF, D), jnp.float32) ** block_levels(key_of[17], (FF, D), ((0, 32),), -0.2, 0.2)), 0.0012288, 0.0049152)
    v_vectors = jnp.clip(jnp.exp(math.log(0.98304) - 1.3862944 * jax.random.uniform(key_of[18], (3, D), jnp.float32) ** block_levels(key_of[18], (3, D), ((1, 32),), -0.2, 0.2)), 0.24576, 0.98304)
    return {"tokens": tokens, "cotangent": cotangent, "segments": segments, "picks": picks, "w_qkv": w_qkv, "w_out": w_out, "w_up": w_up, "w_down": w_down, "vectors": vectors, "m_qkv": m_qkv, "m_out": m_out, "m_up": m_up, "m_down": m_down, "m_vectors": m_vectors, "v_qkv": v_qkv, "v_out": v_out, "v_up": v_up, "v_down": v_down, "v_vectors": v_vectors}


@jax.custom_vjp
def low(v):
    return lax.optimization_barrier(v.astype(jnp.bfloat16)).astype(jnp.float32)

@jax.custom_vjp
def low_back(v):
    return v

def low_keep(v):
    return (low(v), None)

def low_pass(kept, grad):
    return (grad,)

def back_keep(v):
    return (v, None)

def back_low(kept, grad):
    return (low(grad),)
low.defvjp(low_keep, low_pass)
low_back.defvjp(back_keep, back_low)
norm_eps = 1e-06
beta_one = 0.9
beta_two = 0.999
adam_eps = 1e-08
learn_rate = 0.03
decay_rate = 0.1
adam_step = 10
limit_scale = 0.01
masked_out = -1e+30
highest = lax.Precision.HIGHEST

def rms_scale(inputs, gain):
    inverse = lax.rsqrt(lax.optimization_barrier(jnp.mean(inputs * inputs, axis=-1, keepdims=True)) + norm_eps)
    return inputs * inverse * gain

def gelu_tanh(inputs):
    return jax.nn.gelu(inputs, approximate=True)

def routed_branch(picked, allowed, weight_set):
    w_qkv, w_out, w_up, w_down, vectors = weight_set
    row_count = picked.shape[0]
    normed = low(rms_scale(picked, vectors[0]))
    projected = low(low_back(jnp.dot(normed, w_qkv, precision=highest)))
    split_heads = projected.reshape(row_count, 3, HEADS, HEAD_DIM)
    queries = split_heads[:, 0]
    keys_all = split_heads[:, 1]
    value_rows = split_heads[:, 2]
    scores = low_back(jnp.einsum('qhd,khd->hqk', queries, keys_all, precision=highest) * HEAD_DIM ** (-0.5))
    scores = jnp.where(allowed[None], scores, masked_out)
    soft_probs = low(jax.nn.softmax(scores, axis=-1))
    attended = jnp.einsum('hqk,khd->qhd', soft_probs, value_rows, precision=highest).reshape(row_count, D)
    attended = low(low_back(attended))
    attn_out = low_back(jnp.dot(attended, w_out, precision=highest))
    middle = picked + attn_out
    normed_two = low(rms_scale(middle, vectors[1]))
    up_proj = low_back(jnp.dot(normed_two, w_up, precision=highest))
    hidden = low(gelu_tanh(up_proj))
    mlp_out = low_back(jnp.dot(hidden, w_down, precision=highest))
    router_logit = lax.optimization_barrier(jnp.sum(picked * vectors[2], axis=-1))
    gating = jax.nn.sigmoid(router_logit)
    return gating[:, None] * (attn_out + mlp_out)

def moment_update(grad_part, first, second):
    first_new = beta_one * first + (1.0 - beta_one) * grad_part
    second_new = beta_two * second + (1.0 - beta_two) * grad_part * grad_part
    return (first_new, second_new)

def adam_update(master, grad_part, first, second):
    first_new, second_new = moment_update(grad_part, first, second)
    first_hat = first_new / (1.0 - beta_one ** adam_step)
    second_hat = second_new / (1.0 - beta_two ** adam_step)
    master_new = master - learn_rate * (first_hat / (jnp.sqrt(second_hat) + adam_eps) + decay_rate * master)
    return (master_new, first_new, second_new)

def reference(tokens, cotangent, segments, picks, w_qkv, w_out, w_up, w_down, vectors, m_qkv, m_out, m_up, m_down, m_vectors, v_qkv, v_out, v_up, v_down, v_vectors):
    per_group = 4
    groups = SEQS // per_group
    seg_groups = segments.reshape(groups, per_group, LEN)
    pick_groups = picks.reshape(groups, per_group, TOPK)
    row_seq = jnp.repeat(jnp.arange(per_group, dtype=jnp.int32), TOPK)
    seq_index = jnp.arange(per_group, dtype=jnp.int32)[:, None]

    def forward(tok_all, *masters):
        weight_set = tuple((low(master) for master in masters))

        def one_group(packed):
            tok_block, seg_block, pick_block = packed
            picked = jnp.take_along_axis(tok_block, pick_block[:, :, None], axis=1).reshape(per_group * TOPK, D)
            seg_sel = jnp.take_along_axis(seg_block, pick_block, axis=1).reshape(-1)
            positions = pick_block.reshape(-1)
            allowed = (row_seq[:, None] == row_seq[None, :]) & (seg_sel[:, None] == seg_sel[None, :]) & (positions[None, :] <= positions[:, None])
            branch_add = routed_branch(picked, allowed, weight_set)
            return tok_block.at[seq_index, pick_block].add(branch_add.reshape(per_group, TOPK, D))
        mixed_rows = lax.map(jax.checkpoint(one_group), (tok_all.reshape(groups, per_group, LEN, D), seg_groups, pick_groups))
        return mixed_rows.reshape(SEQS * LEN, D)
    tok_all32 = tokens.astype(jnp.float32)
    mixed_rows, pull = jax.vjp(forward, tok_all32, w_qkv, w_out, w_up, w_down, vectors)
    grads = pull(cotangent.astype(jnp.float32))
    input_grad = grads[0]
    weight_grads = grads[1:]
    total_sq = jnp.sum(jnp.stack([jnp.sum(grad_part * grad_part) for grad_part in weight_grads]))
    grad_norm = jnp.sqrt(total_sq)
    clip_limit = limit_scale * math.sqrt(PARAMS * SELECTED)
    factor = jnp.minimum(1.0, clip_limit / (grad_norm + 1e-06))
    masters = (w_qkv, w_out, w_up, w_down)
    firsts = (m_qkv, m_out, m_up, m_down)
    seconds = (v_qkv, v_out, v_up, v_down)
    results = [adam_update(masters[index], weight_grads[index] * factor, firsts[index], seconds[index]) for index in range(4)]
    first_vec, second_vec = moment_update(weight_grads[4] * factor, m_vectors, v_vectors)
    return (mixed_rows.astype(jnp.bfloat16), input_grad.astype(jnp.bfloat16), grad_norm, results[0][0], results[1][0], results[2][0], results[3][0], results[0][1], results[1][1], results[2][1], results[3][1], first_vec, results[0][2], results[1][2], results[2][2], results[3][2], second_vec)
```

```python
import functools
import math

import jax
import jax.numpy as jnp
from jax import lax
from jax.experimental import pallas as pl
from jax.experimental.pallas import tpu as pltpu
from jax.sharding import PartitionSpec as P

HEAD_DIM = 64


norm_eps = 1e-06
beta_one = 0.9
beta_two = 0.999
adam_eps = 1e-08
learn_rate = 0.03
decay_rate = 0.1
adam_step = 10
limit_scale = 0.01
masked_out = -1e30


def rms_scale(inputs, gain):
    inverse = lax.rsqrt(jnp.mean(inputs * inputs, axis=-1, keepdims=True) + norm_eps)
    return inputs * inverse * gain


def gelu_tanh(inputs):
    return jax.nn.gelu(inputs, approximate=True)


def contract_rows(left, right):
    return lax.dot_general(
        left, right, (((0,), (0,)), ((), ())), preferred_element_type=jnp.float32
    )


def contract_cols(left, right):
    return lax.dot_general(
        left, right, (((1,), (1,)), ((), ())), preferred_element_type=jnp.float32
    )


def keep_pair(pair):
    return pair


def routed_forward(picked, allowed, weight_set):
    w_qkv, w_out, w_up, w_down, vectors = weight_set
    gain_rows = vectors.astype(jnp.float32)
    row_count, model_width = picked.shape
    head_count = model_width // HEAD_DIM
    normed = rms_scale(picked, gain_rows[0]).astype(jnp.bfloat16)
    projected = jnp.dot(normed, w_qkv, preferred_element_type=jnp.float32).astype(jnp.bfloat16)
    split_heads = projected.reshape(row_count, 3, head_count, HEAD_DIM)
    queries = split_heads[:, 0]
    keys_all = split_heads[:, 1]
    value_rows = split_heads[:, 2]
    scores = jnp.einsum(
        "qhd,khd->hqk", queries, keys_all, preferred_element_type=jnp.float32
    ) * HEAD_DIM ** (-0.5)
    scores = jnp.where(allowed[None], scores, masked_out)
    top_score = jnp.max(scores, axis=-1, keepdims=True)
    log_total = top_score + jnp.log(jnp.sum(jnp.exp(scores - top_score), axis=-1, keepdims=True))
    soft_probs = jnp.exp(scores - log_total)
    probs_low = soft_probs.astype(jnp.bfloat16)
    attended = jnp.einsum("hqk,khd->qhd", probs_low, value_rows, preferred_element_type=jnp.float32)
    attended = attended.reshape(row_count, model_width).astype(jnp.bfloat16)
    attn_out = jnp.dot(attended, w_out, preferred_element_type=jnp.float32)
    middle = picked + attn_out
    normed_two = rms_scale(middle, gain_rows[1]).astype(jnp.bfloat16)
    up_proj = jnp.dot(normed_two, w_up, preferred_element_type=jnp.float32)
    hidden = gelu_tanh(up_proj).astype(jnp.bfloat16)
    mlp_out = jnp.dot(hidden, w_down, preferred_element_type=jnp.float32)
    router_logit = jnp.sum(picked * gain_rows[2], axis=-1)
    gating = jax.nn.sigmoid(router_logit)
    branch_add = gating[:, None] * (attn_out + mlp_out)
    saved = (
        normed,
        split_heads,
        soft_probs,
        probs_low,
        attended,
        attn_out,
        middle,
        normed_two,
        up_proj,
        hidden,
        mlp_out,
        gating,
    )
    return (branch_add, saved)


def routed_backward(picked, weight_set, saved, back_rows, send_mlp):
    w_qkv, w_out, w_up, w_down, vectors = weight_set
    gain_rows = vectors.astype(jnp.float32)
    (
        normed,
        split_heads,
        soft_probs,
        probs_low,
        attended,
        attn_out,
        middle,
        normed_two,
        up_proj,
        hidden,
        mlp_out,
        gating,
    ) = saved
    row_count, model_width = picked.shape
    head_scale = HEAD_DIM ** (-0.5)
    queries = split_heads[:, 0]
    keys_all = split_heads[:, 1]
    value_rows = split_heads[:, 2]
    gate_grad = jnp.sum(back_rows * (attn_out + mlp_out), axis=-1)
    logit_grad = gate_grad * gating * (1.0 - gating)
    branch_grad = gating[:, None] * back_rows
    mlp_low = branch_grad.astype(jnp.bfloat16)
    grad_down = contract_rows(hidden, mlp_low)
    hidden_grad = contract_cols(mlp_low, w_down)
    up_grad = jax.vjp(gelu_tanh, up_proj)[1](hidden_grad)[0].astype(jnp.bfloat16)
    grad_up = contract_rows(normed_two, up_grad)
    mlp_part = send_mlp((grad_up, grad_down))
    normed_two_grad = contract_cols(up_grad, w_up)
    middle_grad, gain_two_grad = jax.vjp(rms_scale, middle, gain_rows[1])[1](normed_two_grad)
    attn_grad = (branch_grad + middle_grad).astype(jnp.bfloat16)
    grad_out = contract_rows(attended, attn_grad)
    attended_grad = (
        contract_cols(attn_grad, w_out).astype(jnp.bfloat16).reshape(row_count, -1, HEAD_DIM)
    )
    value_grad = jnp.einsum(
        "hqk,qhd->khd", probs_low, attended_grad, preferred_element_type=jnp.float32
    )
    probs_grad = jnp.einsum(
        "qhd,khd->hqk", attended_grad, value_rows, preferred_element_type=jnp.float32
    )
    score_grad = soft_probs * (
        probs_grad - jnp.sum(probs_grad * soft_probs, axis=-1, keepdims=True)
    )
    score_low = score_grad.astype(jnp.bfloat16)
    query_grad = (
        jnp.einsum("hqk,khd->qhd", score_low, keys_all, preferred_element_type=jnp.float32)
        * head_scale
    )
    key_grad = (
        jnp.einsum("hqk,qhd->khd", score_low, queries, preferred_element_type=jnp.float32)
        * head_scale
    )
    qkv_grad = (
        jnp.stack([query_grad, key_grad, value_grad], axis=1)
        .reshape(row_count, 3 * model_width)
        .astype(jnp.bfloat16)
    )
    grad_qkv = contract_rows(normed, qkv_grad)
    normed_grad = contract_cols(qkv_grad, w_qkv)
    norm_rows_grad, gain_one_grad = jax.vjp(rms_scale, picked, gain_rows[0])[1](normed_grad)
    router_grad = jnp.sum(logit_grad[:, None] * picked, axis=0)
    picked_grad = back_rows + middle_grad + norm_rows_grad + logit_grad[:, None] * gain_rows[2]
    grad_vectors = jnp.stack([gain_one_grad, gain_two_grad, router_grad], axis=0)
    return (picked_grad, (grad_qkv, grad_out, grad_vectors), mlp_part)


def moment_update(grad_part, first, second):
    first_new = beta_one * first + (1.0 - beta_one) * grad_part
    second_new = beta_two * second + (1.0 - beta_two) * grad_part * grad_part
    return (first_new, second_new)


def adam_update(master, grad_part, first, second):
    first_new, second_new = moment_update(grad_part, first, second)
    first_hat = first_new / (1.0 - beta_one**adam_step)
    second_hat = second_new / (1.0 - beta_two**adam_step)
    master_new = master - learn_rate * (
        first_hat / (jnp.sqrt(second_hat) + adam_eps) + decay_rate * master
    )
    return (master_new, first_new, second_new)


AXES = ("wide", "narrow")


def swap(array, bit):
    count = lax.axis_size("wide") * lax.axis_size("narrow")
    return lax.ppermute(array, AXES, [(i, i ^ bit) for i in range(count)])


def ordered(mine, other, bit, axis):
    low = jnp.where(bit == 0, mine, other)
    high = jnp.where(bit == 0, other, mine)
    return jnp.stack([low, high], axis=axis)


KEEP_L = ((0, 0, 0), (0, 1, 0))
KEEP_R = ((0, 0, 1), (1, 0, 1))
SEND_L = ((1, 0, 0), (1, 1, 0))
SEND_R = ((0, 1, 1), (1, 1, 1))


def half_row(me, flip, core, step):
    block = me ^ (flip[0] * 4 + flip[1] * 2 + core)
    return pl.multiple_of(block * (2 * step) + flip[2] * step, step)


def gather_pieces(shard, lane):
    rows, width = shard.shape
    z_low, z_high = lane & 1, (lane >> 1) & 1
    part = ordered(shard, swap(shard, 2), z_high, 0)
    part = ordered(part, swap(part, 1), z_low, 1)
    left = part[0].reshape(2 * rows, width)
    right = part[1].reshape(2 * rows, width)
    keep_l = jnp.concatenate([left, swap(left, 8)], axis=0)
    keep_r = jnp.concatenate([right, swap(right, 16)], axis=0)
    far_l = swap(keep_l, 16)
    far_r = swap(keep_r, 8)
    own = (keep_l, keep_r, far_l, far_r)
    return own + tuple(swap(piece, 4) for piece in own)


def assemble(pieces, lane):
    two_step, width = pieces[0].shape
    step = two_step // 2

    def body(me_ref, *refs):
        inputs, out, sem = refs[:8], refs[8], refs[9]
        me = me_ref[0]
        copies = []
        for core in range(2):
            for group, flips in enumerate((KEEP_L, KEEP_R, SEND_L, SEND_R)):
                for slot, flip in enumerate(flips):
                    copies.append(
                        pltpu.make_async_copy(
                            inputs[core * 4 + group].at[pl.ds(slot * step, step)],
                            out.at[pl.ds(half_row(me, flip, core, step), step)],
                            sem.at[len(copies)],
                        )
                    )
        for copy in copies:
            copy.start()
        for copy in copies:
            copy.wait()

    return pl.pallas_call(
        body,
        out_shape=jax.ShapeDtypeStruct((16 * step, width), pieces[0].dtype),
        in_specs=[pl.BlockSpec(memory_space=pltpu.SMEM)]
        + [pl.BlockSpec(memory_space=pl.ANY)] * 8,
        out_specs=pl.BlockSpec(memory_space=pltpu.VMEM),
        scratch_shapes=[pltpu.SemaphoreType.DMA((16,))],
        compiler_params=pltpu.CompilerParams(vmem_limit_bytes=24 << 20),
        name="assemble",
    )((lane >> 2).reshape(1), *pieces)


def disassemble(grad, lane):
    rows, width = grad.shape
    step = rows // 16

    def body(me_ref, grad_ref, keep, send, sem):
        me = me_ref[0]
        copies = []
        for core, out in enumerate((keep, send)):
            for slot, flip in enumerate(SEND_L + SEND_R + KEEP_L + KEEP_R):
                copies.append(
                    pltpu.make_async_copy(
                        grad_ref.at[pl.ds(half_row(me, flip, core, step), step)],
                        out.at[slot],
                        sem.at[len(copies)],
                    )
                )
        for copy in copies:
            copy.start()
        for copy in copies:
            copy.wait()

    half = jax.ShapeDtypeStruct((8, step, width), grad.dtype)
    return pl.pallas_call(
        body,
        out_shape=(half, half),
        in_specs=[
            pl.BlockSpec(memory_space=pltpu.SMEM),
            pl.BlockSpec(memory_space=pltpu.VMEM),
        ],
        out_specs=(pl.BlockSpec(memory_space=pl.ANY),) * 2,
        scratch_shapes=[pltpu.SemaphoreType.DMA((16,))],
        compiler_params=pltpu.CompilerParams(vmem_limit_bytes=24 << 20),
        name="disassemble",
    )((lane >> 2).reshape(1), grad)


def scatter_pieces(keep, send, lane):
    f32, bf16 = jnp.float32, jnp.bfloat16
    step, width = keep.shape[1:]
    z_low, z_high = lane & 1, (lane >> 1) & 1
    total = keep.astype(f32) + swap(send, 4).astype(f32)
    left = total[4:6] + swap(total[0:2].astype(bf16), 16).astype(f32)
    right = total[6:8] + swap(total[2:4].astype(bf16), 8).astype(f32)
    low = left[0] + swap(left[1].astype(bf16), 8).astype(f32)
    high = right[0] + swap(right[1].astype(bf16), 16).astype(f32)
    both = jnp.stack([low, high]).reshape(2, 2, step // 2, width)
    first = lax.dynamic_index_in_dim(both, 1 - z_low, 1, keepdims=False).astype(bf16)
    both = lax.dynamic_index_in_dim(both, z_low, 1, keepdims=False) + swap(first, 1).astype(f32)
    second = lax.dynamic_index_in_dim(both, 1 - z_high, 0, keepdims=False).astype(bf16)
    return lax.dynamic_index_in_dim(both, z_high, 0, keepdims=False) + swap(second, 2).astype(f32)


def per_device(
    paired,
    tokens,
    cotangent,
    segments,
    picks,
    w_qkv,
    w_out,
    w_up,
    w_down,
    vectors,
    m_qkv,
    m_out,
    m_up,
    m_down,
    m_vectors,
    v_qkv,
    v_out,
    v_up,
    v_down,
    v_vectors,
):
    f32, bf16 = jnp.float32, jnp.bfloat16
    masters = (w_qkv, w_out, w_up, w_down, vectors)
    devices_all = lax.axis_size("wide") * lax.axis_size("narrow")
    lane = lax.axis_index(AXES)
    seq_count, top_count = picks.shape
    seq_len = segments.shape[1]
    model_width = tokens.shape[1]
    qkv_width = w_qkv.shape[1]
    shard_width = vectors.shape[1]

    low_vec = jnp.broadcast_to(vectors.astype(bf16)[None], (devices_all, 3, shard_width))
    vec_all = lax.all_to_all(low_vec, AXES, 0, 0, tiled=True)
    vec_all = vec_all.transpose(1, 0, 2).reshape(3, model_width)
    chunk_a = jnp.concatenate([w_qkv, w_out], axis=1).astype(bf16)
    chunk_b = w_up.astype(bf16)
    chunk_c = w_down.astype(bf16)
    if paired:
        whole_a, whole_b, whole_c = (
            assemble(gather_pieces(chunk, lane), lane) for chunk in (chunk_a, chunk_b, chunk_c)
        )
    else:
        whole_a, whole_b, whole_c = (
            lax.all_gather(chunk, AXES, axis=0, tiled=True) for chunk in (chunk_a, chunk_b, chunk_c)
        )
    weights = (whole_a[:, :qkv_width], whole_a[:, qkv_width:], whole_b, whole_c, vec_all)

    hot = picks[:, :, None] == jnp.arange(seq_len, dtype=jnp.int32)[None, None, :]
    hot_low = hot.astype(bf16)
    tok_blocks = tokens.reshape(seq_count, seq_len, model_width)
    back_blocks = cotangent.reshape(seq_count, seq_len, model_width)

    def pick(blocks):
        rows = jnp.einsum("skl,sld->skd", hot_low, blocks, preferred_element_type=f32)
        return rows.reshape(-1, model_width)

    def place(blocks, rows):
        rows = rows.astype(bf16).reshape(seq_count, top_count, model_width)
        spread = jnp.einsum("skl,skd->sld", hot_low, rows, preferred_element_type=f32).astype(bf16)
        taken = jnp.any(hot, axis=1)
        return jnp.where(taken[:, :, None], spread, blocks).reshape(-1, model_width)

    picked = pick(tok_blocks)
    back_rows = pick(back_blocks)
    seg_sel = jnp.sum(jnp.where(hot, segments[:, None, :], 0), axis=-1).reshape(-1)
    positions = picks.reshape(-1)
    row_seq = jnp.repeat(jnp.arange(seq_count, dtype=jnp.int32), top_count)
    allowed = (
        (row_seq[:, None] == row_seq[None, :])
        & (seg_sel[:, None] == seg_sel[None, :])
        & (positions[None, :] <= positions[:, None])
    )
    branch_add, saved = routed_forward(picked, allowed, weights)
    mixed_rows = place(tok_blocks, picked + branch_add)
    picked_grad, attn_parts, mlp_parts = routed_backward(
        picked, weights, saved, back_rows, keep_pair
    )
    input_grad = place(back_blocks, picked_grad)
    grads = (
        mlp_parts[1].astype(bf16),
        mlp_parts[0].astype(bf16),
        jnp.concatenate([attn_parts[0], attn_parts[1]], axis=1).astype(bf16),
    )
    if paired:
        grad_c, grad_b, grad_a = (
            scatter_pieces(*disassemble(grad, lane), lane) for grad in grads
        )
    else:
        grad_c, grad_b, grad_a = (
            lax.psum_scatter(grad.astype(f32), AXES, scatter_dimension=0, tiled=True)
            for grad in grads
        )
    vec_parts = attn_parts[2].reshape(3, devices_all, shard_width).transpose(1, 0, 2)
    grad_vec = jnp.sum(lax.all_to_all(vec_parts, AXES, 0, 0, tiled=True), axis=0)
    grad_shards = (grad_a[:, :qkv_width], grad_a[:, qkv_width:], grad_b, grad_c, grad_vec)
    local_sq = sum(jnp.sum(grad_shard * grad_shard) for grad_shard in grad_shards)
    squares = lax.all_to_all(jnp.full((devices_all, 128), local_sq), AXES, 0, 0, tiled=True)
    total_sq = jnp.sum(squares[:, 0])
    grad_norm = jnp.sqrt(total_sq)
    ff_width = w_up.shape[1]
    params_all = 4 * model_width * model_width + 2 * model_width * ff_width + 3 * model_width
    selected_all = seq_count * top_count * devices_all
    clip_limit = limit_scale * math.sqrt(params_all * selected_all)
    factor = jnp.minimum(1.0, clip_limit / (grad_norm + 1e-06))
    firsts = (m_qkv, m_out, m_up, m_down)
    seconds = (v_qkv, v_out, v_up, v_down)
    results = [
        adam_update(masters[index], grad_shards[index] * factor, firsts[index], seconds[index])
        for index in range(4)
    ]
    first_vec, second_vec = moment_update(grad_shards[4] * factor, m_vectors, v_vectors)
    return (
        mixed_rows,
        input_grad,
        grad_norm,
        results[0][0],
        results[1][0],
        results[2][0],
        results[3][0],
        results[0][1],
        results[1][1],
        results[2][1],
        results[3][1],
        first_vec,
        results[0][2],
        results[1][2],
        results[2][2],
        results[3][2],
        second_vec,
    )


def solution(mesh):
    placed = (
        P(("wide", "narrow"), None),
        P(("wide", "narrow"), None),
        P(("wide", "narrow"), None),
        P(("wide", "narrow"), None),
        P(("wide", "narrow"), None),
        P(("wide", "narrow"), None),
        P(("wide", "narrow"), None),
        P(("wide", "narrow"), None),
        P(None, ("wide", "narrow")),
        P(("wide", "narrow"), None),
        P(("wide", "narrow"), None),
        P(("wide", "narrow"), None),
        P(("wide", "narrow"), None),
        P(None, ("wide", "narrow")),
        P(("wide", "narrow"), None),
        P(("wide", "narrow"), None),
        P(("wide", "narrow"), None),
        P(("wide", "narrow"), None),
        P(None, ("wide", "narrow")),
    )
    paired = mesh.shape["wide"] == 8 and mesh.shape["narrow"] == 4
    return jax.shard_map(
        functools.partial(per_device, paired),
        mesh=mesh,
        in_specs=placed,
        out_specs=(
            P(("wide", "narrow"), None),
            P(("wide", "narrow"), None),
            P(),
            P(("wide", "narrow"), None),
            P(("wide", "narrow"), None),
            P(("wide", "narrow"), None),
            P(("wide", "narrow"), None),
            P(("wide", "narrow"), None),
            P(("wide", "narrow"), None),
            P(("wide", "narrow"), None),
            P(("wide", "narrow"), None),
            P(None, ("wide", "narrow")),
            P(("wide", "narrow"), None),
            P(("wide", "narrow"), None),
            P(("wide", "narrow"), None),
            P(("wide", "narrow"), None),
            P(None, ("wide", "narrow")),
        ),
        check_vma=False,
    )
```

```python
import functools
import math

import jax
import jax.numpy as jnp
from jax import lax
from jax.experimental import pallas as pl
from jax.experimental.pallas import tpu as pltpu
from jax.sharding import PartitionSpec as P

HEAD_DIM = 64


norm_eps = 1e-06
beta_one = 0.9
beta_two = 0.999
adam_eps = 1e-08
learn_rate = 0.03
decay_rate = 0.1
adam_step = 10
limit_scale = 0.01
masked_out = -1e30
AXES = ("wide", "narrow")


def moment_update(grad_part, first, second):
    first_new = beta_one * first + (1.0 - beta_one) * grad_part
    second_new = beta_two * second + (1.0 - beta_two) * grad_part * grad_part
    return (first_new, second_new)


def adam_update(master, grad_part, first, second):
    first_new, second_new = moment_update(grad_part, first, second)
    first_hat = first_new / (1.0 - beta_one**adam_step)
    second_hat = second_new / (1.0 - beta_two**adam_step)
    master_new = master - learn_rate * (
        first_hat / (jnp.sqrt(second_hat) + adam_eps) + decay_rate * master
    )
    return (master_new, first_new, second_new)


f32, bf16 = jnp.float32, jnp.bfloat16
PAIR = 2 * HEAD_DIM
head_scale = HEAD_DIM ** (-0.5)
KEEP_L = ((0, 0, 0), (0, 1, 0))
KEEP_R = ((0, 0, 1), (1, 0, 1))
FAR_L = ((1, 0, 0), (1, 1, 0))
FAR_R = ((0, 1, 1), (1, 1, 1))
GROUPS = (KEEP_L, KEEP_R, FAR_L, FAR_R)


def kernel(body, name, outs, args, kinds, scratch=(), limit=24, loose=0):
    spaces = {"s": pltpu.SMEM, "v": pltpu.VMEM, "a": pltpu.HBM}
    held = len(outs) - loose
    return pl.pallas_call(
        body,
        out_shape=[
            jax.ShapeDtypeStruct(*out) if place < held else pltpu.HBM(*out)
            for place, out in enumerate(outs)
        ],
        in_specs=[pl.BlockSpec(memory_space=spaces[kind]) for kind in kinds],
        out_specs=[
            pl.BlockSpec(memory_space=pltpu.VMEM if place < held else pltpu.HBM)
            for place in range(len(outs))
        ],
        scratch_shapes=list(scratch),
        compiler_params=pltpu.CompilerParams(vmem_limit_bytes=limit << 20),
        name=name,
    )(
        *(
            pltpu.with_memory_space_constraint(arg, pltpu.HBM) if kind == "a" else arg
            for arg, kind in zip(args, kinds)
        )
    )


def each_block(pieces):
    for core in range(2):
        for group, flips in enumerate(GROUPS):
            for place, flip in enumerate(flips):
                yield flip[0] * 4 + flip[1] * 2 + core, flip[2], pieces[core * 4 + group].at[place]


def start_all(copies):
    for copy in copies:
        copy.start()


def wait_all(copies):
    for copy in copies:
        copy.wait()


def fetch(pieces, me, sem, base, left, right):
    copies = []
    for flip, half, block in each_block(pieces):
        rows = block.shape[0]
        start = pl.multiple_of((me ^ flip) * rows, rows)
        for target, column, out_column, width in (left, right)[half]:
            copies.append(
                pltpu.make_async_copy(
                    block.at[:, pl.ds(column, width)],
                    target.at[pl.ds(start, rows), pl.ds(out_column, width)],
                    sem.at[base + len(copies)],
                )
            )
    return copies


def dot_nt(left, right):
    return lax.dot_general(left, right, (((1,), (1,)), ((), ())), preferred_element_type=f32)


def dot_tn(left, right):
    return lax.dot_general(left, right, (((0,), (0,)), ((), ())), preferred_element_type=f32)


def dot_nn(left, right):
    return jnp.dot(left, right, preferred_element_type=f32)


def mean_last(array):
    return jnp.mean(array, axis=-1, keepdims=True)


def sum_rows(array):
    return jnp.sum(array, axis=0, keepdims=True)


def head_masks(dtype):
    lanes = lax.broadcasted_iota(jnp.int32, (1, PAIR), 1)
    first = (lanes < HEAD_DIM).astype(f32).astype(dtype)
    return first, (1 - first).astype(dtype)


def two_heads(pair, masks):
    return jnp.concatenate([pair * masks[0], pair * masks[1]], axis=0)


def one_pair(stacked, masks):
    rows = stacked.shape[0] // 2
    return stacked[:rows] * masks[0] + stacked[rows:] * masks[1]


def attend(me, pieces, picked, back_rows, seg_row, seg_col, order):
    rows, width = picked.shape
    seqs = seg_row.shape[0]
    top = rows // seqs
    pairs = width // PAIR
    first = pieces[0].shape[2]
    rest = 3 * width - first
    spare = pieces[1].shape[2] - rest - width

    def body(me_ref, *refs):
        blocks, refs = refs[:8], refs[8:]
        x_ref, dy_ref, seg_row_ref, seg_col_ref, order_ref = refs[:5]
        own_ref, send_ref, df_ref, gate_ref, vec_ref, add_ref, h2_ref = refs[5:12]
        all_ref, out_ref, qkv_out, prob_out = refs[12:16]
        w_qkv, w_out, w_vec, qkv_ref, prob_ref, att_ref, sem = refs[16:]
        vec_copies = fetch(blocks, me_ref[0], sem, 0, (), ((w_vec, rest + width, 0, spare),))
        left = fetch(blocks, me_ref[0], sem, 8, ((w_qkv, 0, 0, first),), ())
        right = fetch(blocks, me_ref[0], sem, 16, (), ((w_qkv, 0, first, rest),))
        out_copies = fetch(blocks, me_ref[0], sem, 24, (), ((w_out, rest, 0, width),))
        start_all(vec_copies + left + right + out_copies)
        wait_all(vec_copies)
        vec = w_vec[...].astype(f32).T[:8]
        vec_ref[...] = vec
        x = x_ref[...].astype(f32)
        h1 = (x * lax.rsqrt(mean_last(x * x) + norm_eps) * vec[0:1]).astype(bf16)
        for copies, start, count in ((left, 0, first), (right, first, rest)):
            wait_all(copies)
            for part in range(start, start + count, 384):
                lanes = pl.ds(part, 384)
                qkv_ref[:, lanes] = dot_nn(h1, w_qkv[:, lanes]).astype(bf16)
        stored = [
            pltpu.make_async_copy(w_qkv, all_ref, sem.at[32]),
            pltpu.make_async_copy(qkv_ref, qkv_out, sem.at[33]),
            pltpu.make_async_copy(w_out, out_ref, sem.at[34]),
        ]
        wait_all(out_copies)
        start_all(stored)
        masks, masks_f = head_masks(bf16), head_masks(f32)
        ordered_pairs = lax.broadcasted_iota(jnp.int32, (top, top), 1) <= lax.broadcasted_iota(
            jnp.int32, (top, top), 0
        )
        for seq in range(seqs):
            here = pl.ds(seq * top, top)
            seen = ordered_pairs & (seg_col_ref[seq] == seg_row_ref[seq])
            hidden = jnp.where(seen, 0.0, masked_out)
            hidden = jnp.concatenate([hidden, hidden], axis=0)
            for pair in range(pairs):
                q, k, v = (
                    qkv_ref[here, pl.ds(part * width + pair * PAIR, PAIR)] for part in range(3)
                )
                scores = dot_nt(two_heads(q, masks), k) * head_scale
                scores = jnp.where(hidden < 0.0, masked_out, scores)
                power = jnp.exp(scores - jnp.max(scores, axis=-1, keepdims=True))
                probs = power / jnp.sum(power, axis=-1, keepdims=True)
                prob_ref[seq * pairs + pair] = probs
                mixed = one_pair(dot_nn(probs.astype(bf16), v), masks_f)
                att_ref[here, pl.ds(pair * PAIR, PAIR)] = mixed.astype(bf16)
            group = pl.ds(seq * pairs, pairs)
            stored.append(
                pltpu.make_async_copy(prob_ref.at[group], prob_out.at[group], sem.at[35 + seq])
            )
            stored[-1].start()
        gate = jax.nn.sigmoid(jnp.sum(x * vec[2:3], axis=-1, keepdims=True))
        gate_ref[...] = jnp.broadcast_to(gate, gate_ref.shape)
        df = (gate * dy_ref[...].astype(f32)).astype(bf16)
        df_ref[...] = df
        added = dot_nn(att_ref[...], w_out[...])
        add_ref[...] = added
        middle = x + added
        h2 = (middle * lax.rsqrt(mean_last(middle * middle) + norm_eps) * vec[1:2]).astype(bf16)
        h2_ref[...] = h2
        for half in range(2):
            lanes = slice(half * (width // 2), (half + 1) * (width // 2))
            send_ref[2 + half] = df[:, lanes]
            send_ref[4 + half] = h2[:, lanes]
        chosen = one_hot_columns(order_ref)
        for place, array in enumerate((h1, att_ref[...])):
            parted = dot_nn(array, chosen).astype(bf16)
            own_ref[place] = parted[:, : width // 2]
            send_ref[place] = parted[:, width // 2 :]
        wait_all(stored)

    outs = [
        ((2, rows, width // 2), bf16),
        ((6, rows, width // 2), bf16),
        ((rows, width), bf16),
        ((rows, 128), f32),
        ((8, width), f32),
        ((rows, width), f32),
        ((rows, width), bf16),
        ((width, 3 * width), bf16),
        ((width, width), bf16),
        ((rows, 3 * width), bf16),
        ((seqs * pairs, 2 * top, top), f32),
    ]
    scratch = [
        pltpu.VMEM((width, 3 * width), bf16),
        pltpu.VMEM((width, width), bf16),
        pltpu.VMEM((width, spare), bf16),
        pltpu.VMEM((rows, 3 * width), bf16),
        pltpu.VMEM((seqs * pairs, 2 * top, top), f32),
        pltpu.VMEM((rows, width), bf16),
        pltpu.SemaphoreType.DMA((35 + seqs,)),
    ]
    args = (me, *pieces, picked, back_rows, seg_row, seg_col, order)
    return kernel(body, "attend", outs, args, "s" + "a" * 8 + "vvvvv", scratch, 26, 4)


def one_hot_columns(order_ref):
    width = order_ref.shape[1]
    chosen = lax.broadcasted_iota(jnp.int32, (width, width), 0) == order_ref[...]
    return chosen.astype(f32).astype(bf16)


def climb(me, pieces, h2, sib, order):
    rows, width = h2.shape
    first = pieces[0].shape[2]
    block = 2 * first // 8

    def body(me_ref, *refs):
        blocks, refs = refs[:8], refs[8:]
        h2_ref, sib_ref, order_ref = refs[:3]
        own_ref, send_ref, far_ref, pair_ref, up_ref, slope_out = refs[3:9]
        w_up, slope_ref, both_ref, sem = refs[9:]
        copies = fetch(
            blocks, me_ref[0], sem, 0, ((w_up, 0, 0, first),), ((w_up, 0, first, first),)
        )
        start_all(copies)
        both_ref[:rows] = h2_ref[...]
        for half in range(2):
            lanes = pl.ds(half * (width // 2), width // 2)
            both_ref[rows:, lanes] = sib_ref[4 + half]
        chosen = one_hot_columns(order_ref)[:, : width // 2]
        parted = dot_nn(both_ref[...], chosen).astype(bf16)
        pair_ref[0] = parted[:rows]
        pair_ref[1] = parted[rows:]
        wait_all(copies)
        stored = [pltpu.make_async_copy(w_up, up_ref, sem.at[16])]
        start_all(stored)
        scale = math.sqrt(2.0 / math.pi)
        for flip in range(8):
            start = pl.multiple_of((me_ref[0] ^ flip) * block, block)
            place = flip // 2
            lanes = pl.ds(place * block, block)
            weights = w_up[:, pl.ds(start, block)]
            u = dot_nn(both_ref[:rows], weights)
            square = u * u
            bent = jnp.tanh(scale * (u + 0.044715 * (square * u)))
            half_up = 0.5 * (1.0 + bent)
            target = send_ref if flip % 2 else own_ref
            target[:, lanes] = (u * half_up).astype(bf16)
            where = (flip % 2) * 4 + place
            slope_ref[where] = half_up + (0.5 * u) * (1.0 - bent * bent) * (
                scale * (1.0 + (3.0 * 0.044715) * square)
            )
            stored.append(
                pltpu.make_async_copy(
                    slope_ref.at[where], slope_out.at[where], sem.at[17 + flip]
                )
            )
            stored[-1].start()
            if flip % 2 == 0:
                u = dot_nn(both_ref[rows:], weights)
                bent = jnp.tanh(scale * (u + 0.044715 * (u * u * u)))
                far_ref[:, lanes] = (0.5 * u * (1.0 + bent)).astype(bf16)
        wait_all(stored)

    outs = [
        ((rows, 4 * block), bf16),
        ((rows, 4 * block), bf16),
        ((rows, 4 * block), bf16),
        ((2, rows, width // 2), bf16),
        ((width, 8 * block), bf16),
        ((8, rows, block), f32),
    ]
    scratch = [
        pltpu.VMEM((width, 8 * block), bf16),
        pltpu.VMEM((8, rows, block), f32),
        pltpu.VMEM((2 * rows, width), bf16),
        pltpu.SemaphoreType.DMA((25,)),
    ]
    args = (me, *pieces, h2, sib, order)
    return kernel(body, "climb", outs, args, "s" + "a" * 8 + "vvv", scratch, 26, 2)


class View:
    def __init__(self, array, columns=None, first=0, lead=None):
        self.array, self.first, self.lead = array, first, lead
        self.columns = columns or array.shape[-1]

    def value(self):
        array = self.array if self.lead is None else self.array[self.lead]
        return array[:, self.first : self.first + self.columns]

    def read(self, ref, first, columns):
        lanes = pl.ds(self.first + first, columns)
        return ref[:, lanes] if self.lead is None else ref[self.lead, :, lanes]


def outer(name, products, split):
    length = products[0][0].columns // 4
    total = sum(product[1].columns for product in products)
    widths = (split, total - split)
    order = ((2, 3), (1, 3), (0, 1), (0, 2))

    def body(*refs):
        ins, outs = refs[: 4 * len(products)], refs[4 * len(products) :]
        base = 0
        for number, product in enumerate(products):
            reads = [
                functools.partial(view.read, ref)
                for view, ref in zip(product, ins[4 * number : 4 * number + 4])
            ]
            columns = product[1].columns
            step = min(768, columns)
            for start in range(0, columns, step):
                for first in range(0, 4 * length, 384):
                    value = dot_tn(reads[0](first, 384), reads[1](start, step))
                    value += dot_tn(reads[2](first, 384), reads[3](start, step))
                    for block in range(first // length, (first + 384) // length):
                        part = value[block * length - first : (block + 1) * length - first]
                        for half in range(2):
                            low = max(base + start, half * split)
                            high = min(base + start + step, split + half * (total - split))
                            if high <= low:
                                continue
                            piece = part[:, low - base - start : high - base - start]
                            out_lanes = pl.ds(low - half * split, high - low)
                            for out in (half, 2 + half):
                                if block in order[out]:
                                    outs[out][order[out].index(block), :, out_lanes] = piece.astype(
                                        outs[out].dtype
                                    )
            base += columns

    outs = [
        ((2, length, widths[out % 2]), bf16 if out < 2 else f32) for out in range(4)
    ]
    args = [view.array for product in products for view in product]
    return kernel(body, name, outs, args, "v" * len(args))


def descend(me, pieces, slope, df):
    rows, width = df.shape
    block = slope.shape[2]

    def body(me_ref, *refs):
        blocks, refs = refs[:8], refs[8:]
        slope_in, df_ref, du_ref, down_ref, w_down, slope_ref, sem = refs
        copies = [[] for _ in range(8)]
        for flip, side, part in each_block(blocks):
            lanes = pl.ds(side * (width // 2), width // 2)
            place = (flip % 2) * 4 + flip // 2
            target = w_down.at[pl.ds(place * block, block), lanes]
            copies[place].append(
                pltpu.make_async_copy(part, target, sem.at[place * 2 + side])
            )
        for place, pair in enumerate(copies):
            pair.append(
                pltpu.make_async_copy(
                    slope_in.at[place], slope_ref.at[place], sem.at[17 + place]
                )
            )
            start_all(pair)
        for place in range(8):
            wait_all(copies[place])
            flip = place % 4 * 2 + place // 4
            start = pl.multiple_of((me_ref[0] ^ flip) * block, block)
            dg = dot_nt(df_ref[...], w_down[pl.ds(place * block, block)])
            du_ref[:, pl.ds(start, block)] = (dg * slope_ref[place]).astype(bf16)
        stored = pltpu.make_async_copy(w_down, down_ref, sem.at[16])
        stored.start()
        stored.wait()

    outs = [((rows, 8 * block), bf16), ((8 * block, width), bf16)]
    scratch = [
        pltpu.VMEM((8 * block, width), bf16),
        pltpu.VMEM((8, rows, block), f32),
        pltpu.SemaphoreType.DMA((25,)),
    ]
    args = (me, *pieces, slope, df)
    return kernel(body, "descend", outs, args, "s" + "a" * 9 + "v", scratch, 24, 1)


def unclimb(w_up, du, picked, added, gate, back_rows, vec):
    rows, width = picked.shape

    def body(up_ref, du_ref, x_ref, add_ref, gate_ref, dy_ref, vec_ref, dm_ref, da_ref, dg_ref):
        dh = dot_nt(du_ref[...], up_ref[...])
        middle = x_ref[...].astype(f32) + add_ref[...]
        inverse = lax.rsqrt(mean_last(middle * middle) + norm_eps)
        unit = middle * inverse
        dg_ref[...] = jnp.broadcast_to(sum_rows(dh * unit), dg_ref.shape)
        scaled = dh * vec_ref[1:2]
        dm = inverse * (scaled - unit * mean_last(scaled * unit))
        dm_ref[...] = dm
        da_ref[...] = (gate_ref[:, 0:1] * dy_ref[...].astype(f32) + dm).astype(bf16)

    outs = [((rows, width), f32), ((rows, width), bf16), ((8, width), f32)]
    args = (w_up, du, picked, added, gate, back_rows, vec)
    return kernel(body, "unclimb", outs, args, "v" * 7)


def unattend(w_out, da, qkv, probs):
    rows, width = da.shape
    top = probs.shape[2]
    seqs, pairs = rows // top, width // PAIR

    def body(out_ref, da_ref, qkv_ref, prob_ref, dqkv_ref, do_ref):
        do_ref[...] = dot_nt(da_ref[...], out_ref[...]).astype(bf16)
        masks, masks_f = head_masks(bf16), head_masks(f32)
        for seq in range(seqs):
            here = pl.ds(seq * top, top)
            for pair in range(pairs):
                lanes = [pl.ds(part * width + pair * PAIR, PAIR) for part in range(3)]
                q, k, v = (qkv_ref[here, part] for part in lanes)
                do = two_heads(do_ref[here, pl.ds(pair * PAIR, PAIR)], masks)
                probs = prob_ref[seq * pairs + pair]
                dprobs = dot_nt(do, v)
                dscores = probs * (dprobs - jnp.sum(dprobs * probs, axis=-1, keepdims=True))
                dscores = dscores.astype(bf16)
                dq = one_pair(dot_nn(dscores, k), masks_f) * head_scale
                dk = dot_tn(dscores, two_heads(q, masks)) * head_scale
                dv = dot_tn(probs.astype(bf16), do)
                for part, value in zip(lanes, (dq, dk, dv)):
                    dqkv_ref[here, part] = value.astype(bf16)

    scratch = [pltpu.VMEM((rows, width), bf16)]
    outs = [((rows, 3 * width), bf16)]
    return kernel(body, "unattend", outs, (w_out, da, qkv, probs), "vvvv", scratch)[0]


def finish_mlp(w_down, own, send, picked, added, gate, back_rows):
    rows, width = picked.shape
    half = w_down.shape[0] // 2

    def body(down_ref, own_ref, send_ref, x_ref, add_ref, gate_ref, dy_ref, *outs):
        new_ref, dlogit_ref, dr_ref = outs
        out = dot_nn(own_ref[:, :half], down_ref[:half])
        out += dot_nn(send_ref[:, :half], down_ref[half:])
        both = add_ref[...] + out
        x = x_ref[...].astype(f32)
        gate = gate_ref[:, 0:1]
        new_ref[...] = (x + gate * both).astype(bf16)
        dlogit = jnp.sum(dy_ref[...].astype(f32) * both, axis=-1, keepdims=True)
        dlogit = dlogit * gate * (1.0 - gate)
        dlogit_ref[...] = jnp.broadcast_to(dlogit, dlogit_ref.shape)
        dr_ref[...] = jnp.broadcast_to(sum_rows(dlogit * x), dr_ref.shape)

    outs = [((rows, width), bf16), ((rows, 128), f32), ((8, width), f32)]
    args = (w_down, own, send, picked, added, gate, back_rows)
    return kernel(body, "finish_mlp", outs, args, "v" * 7)


def finish_rows(w_qkv, dqkv, picked, back_rows, dmiddle, dlogit, vec):
    rows, width = picked.shape

    def body(all_ref, dqkv_ref, x_ref, dy_ref, dm_ref, dlogit_ref, vec_ref, grad_ref, dg_ref):
        dh = dot_nt(dqkv_ref[...], all_ref[...])
        x = x_ref[...].astype(f32)
        inverse = lax.rsqrt(mean_last(x * x) + norm_eps)
        unit = x * inverse
        dg_ref[...] = jnp.broadcast_to(sum_rows(dh * unit), dg_ref.shape)
        scaled = dh * vec_ref[0:1]
        dx = inverse * (scaled - unit * mean_last(scaled * unit))
        grad = dy_ref[...].astype(f32) + dm_ref[...] + dx + dlogit_ref[:, 0:1] * vec_ref[2:3]
        grad_ref[...] = grad.astype(bf16)

    outs = [((rows, width), bf16), ((8, width), f32)]
    args = (w_qkv, dqkv, picked, back_rows, dmiddle, dlogit, vec)
    return kernel(body, "finish_rows", outs, args, "v" * 7)


def join_z(z, own, others, split):
    rows, width = own.shape

    def body(z_ref, *refs):
        ins, left_ref, right_ref, total = refs[:4], *refs[4:]
        for flip, block in enumerate(ins):
            start = pl.multiple_of((z_ref[0] ^ flip) * rows, rows)
            total[pl.ds(start, rows)] = block[...].astype(f32)
        left_ref[...] = total[:, :split].astype(bf16)
        right_ref[...] = total[:, split:].astype(bf16)

    outs = [((4 * rows, split), bf16), ((4 * rows, width - split), bf16)]
    scratch = [pltpu.VMEM((4 * rows, width), f32)]
    return kernel(body, "join_z", outs, (z, own, *others), "svvvv", scratch)


def join_z_pairs(z, left, right, near_l, near_r, others):
    rows, width = left.shape

    def body(z_ref, *refs):
        mine, others, outs = refs[:4], refs[4:7], refs[7:]
        for flip in range(4):
            start = pl.ds(pl.multiple_of((z_ref[0] ^ flip) * rows, rows), rows)
            for place in range(4):
                block = others[flip - 1][place] if flip else mine[place][...]
                outs[place // 2][place % 2, start] = block

    outs = [((2, 4 * rows, width), bf16)] * 2
    args = (z, left, near_l, right, near_r, *others)
    return kernel(body, "join_z_pairs", outs, args, "svvvvvvv")


def add_z_pairs(z, keep_l, keep_r, other_l, other_r):
    pair, rows, width = keep_l.shape
    part = rows // 4

    def body(z_ref, keep_l, keep_r, other_l, other_r, mine, send, total):
        for half, (keep, other) in enumerate(((keep_l, other_l), (keep_r, other_r))):
            for place in range(pair):
                total[half * pair + place] = keep[place] + other[place].astype(f32)
        for flip in range(4):
            start = pl.multiple_of((z_ref[0] ^ flip) * part, part)
            out = (mine, send)[flip % 2]
            out[flip // 2] = total[:, pl.ds(start, part)].astype(out.dtype)

    outs = [((2, 4, part, width), f32), ((2, 4, part, width), bf16)]
    scratch = [pltpu.VMEM((4, rows, width), f32)]
    args = (z, keep_l, keep_r, other_l, other_r)
    return kernel(body, "add_z_pairs", outs, args, "svvvv", scratch)


def add_four(mine, other):
    def body(mine, other, send_l, send_r, keep):
        def total(place):
            return mine[place] + other[place].astype(f32)

        width = mine.shape[2]
        keep[:, :width] = total(0)
        keep[:, width:] = total(2)
        send_l[...] = total(1).astype(bf16)
        send_r[...] = total(3).astype(bf16)

    _, rows, width = mine.shape
    outs = [((rows, width), bf16)] * 2 + [((rows, 2 * width), f32)]
    return kernel(body, "add_four", outs, (mine, other), "vv")


def add_pairs(keep_l, keep_r, other_l, other_r):
    def body(keep_l, keep_r, other_l, other_r, send_l, send_r, left, right):
        for keep, other, send, mine in (
            (keep_l, other_l, send_l, left),
            (keep_r, other_r, send_r, right),
        ):
            send[...] = (keep[1] + other[1].astype(f32)).astype(bf16)
            mine[...] = keep[0] + other[0].astype(f32)

    shapes = [keep_l.shape[1:], keep_r.shape[1:]]
    outs = [(shape, kind) for kind in (bf16, f32) for shape in shapes]
    return kernel(body, "add_pairs", outs, (keep_l, keep_r, other_l, other_r), "vvvv")


def add_split(z, keep_l, keep_r, other_l, other_r):
    rows, split = keep_l.shape
    width = split + keep_r.shape[1]
    part = rows // 4

    def body(z_ref, keep_l, keep_r, other_l, other_r, mine, one, two, three, total):
        total[:, :split] = keep_l[...] + other_l[...].astype(f32)
        total[:, split:] = keep_r[...] + other_r[...].astype(f32)
        for flip, out in enumerate((mine, one, two, three)):
            start = pl.multiple_of((z_ref[0] ^ flip) * part, part)
            out[...] = total[pl.ds(start, part)].astype(out.dtype)

    outs = [((part, width), f32)] + [((part, width), bf16)] * 3
    scratch = [pltpu.VMEM((rows, width), f32)]
    args = (z, keep_l, keep_r, other_l, other_r)
    return kernel(body, "add_split", outs, args, "svvvv", scratch)


def add_next(keep, other):
    def body(keep, other, mine, send):
        mine[...] = keep[0] + other[0].astype(f32)
        send[...] = (keep[1] + other[1].astype(f32)).astype(bf16)

    shape = keep.shape[1:]
    return kernel(body, "add_next", [(shape, f32), (shape, bf16)], (keep, other), "vv")


def settle_halves(keep, other_l, other_r):
    def body(keep, other_l, other_r, grad, square):
        width = other_l.shape[1]
        total = None
        for half, other in enumerate((other_l, other_r)):
            lanes = pl.ds(half * width, width)
            value = keep[:, lanes] + other[...].astype(f32)
            grad[:, lanes] = value
            part = jnp.sum(value * value)
            total = part if total is None else total + part
        square[...] = jnp.full(square.shape, total)

    outs = [(keep.shape, f32), ((8, 128), f32)]
    return kernel(body, "settle_halves", outs, (keep, other_l, other_r), "vvv")


def settle_z(mine, others):
    def body(mine, one, two, three, grad, square):
        value = mine[...] + one[...].astype(f32) + two[...].astype(f32) + three[...].astype(f32)
        grad[...] = value
        square[...] = jnp.full(square.shape, jnp.sum(value * value))

    outs = [(mine.shape, f32), ((8, 128), f32)]
    return kernel(body, "settle_z", outs, (mine, *others), "vvvv")


def update(squares, limit, grads, states, vec_grad, vec_states):
    count = len(grads)

    def body(square_ref, *refs):
        grad_refs, refs = refs[:count], refs[count:]
        state_refs, refs = refs[: 3 * count], refs[3 * count :]
        vec_ref, vec_m, vec_v, norm_ref, out_refs = *refs[:4], refs[4:]
        norm = jnp.sqrt(jnp.sum(square_ref[...], axis=0, keepdims=True)[:, 0:1])
        norm_ref[...] = jnp.broadcast_to(norm, norm_ref.shape)
        factor = jnp.minimum(1.0, limit / (norm + 1e-06))
        for place in range(count):
            w, m, v = (ref[...] for ref in state_refs[3 * place : 3 * place + 3])
            grad = grads[place].read(grad_refs[place], 0, grads[place].columns) * factor
            for ref, value in zip(out_refs[3 * place :], adam_update(w, grad, m, v)):
                ref[...] = value
        first, second = moment_update(vec_ref[...] * factor, vec_m[...], vec_v[...])
        out_refs[-2][...] = first
        out_refs[-1][...] = second

    flat = [array for state in states for array in state]
    outs = [((8, 128), f32)] + [(array.shape, f32) for array in (*flat, *vec_states)]
    args = (squares, *(grad.array for grad in grads), *flat, vec_grad, *vec_states)
    return kernel(body, "update", outs, args, "v" * len(args), (), 32)


class Steps:
    def __init__(self, chain):
        self.chain = chain
        self.result = None
        self.launch(next(chain))

    def launch(self, step):
        self.flips = [flip for _, flip in step]
        self.given = [array for array, _ in step]

    def advance(self, arrays):
        try:
            self.launch(self.chain.send(arrays))
        except StopIteration as stop:
            self.flips, self.given, self.result = (), (), stop.value


def slot(chains, value):
    arrays = [
        [swap(array, flip) for array, flip in zip(chain.given, chain.flips)] for chain in chains
    ]
    arrays, value = lax.optimization_barrier((arrays, value))
    for chain, array in zip(chains, arrays):
        chain.advance(array)
    return value


def ready(chains, value):
    arrays, value = lax.optimization_barrier(([chain.given for chain in chains], value))
    for chain, array in zip(chains, arrays):
        chain.given = array
    return value


def swap(array, bit):
    count = lax.axis_size("wide") * lax.axis_size("narrow")
    return lax.ppermute(array, AXES, [(i, i ^ bit) for i in range(count)])


def exchange(*arrays):
    return (yield [(array, 4) for array in arrays])


def around_z(shard, at_once):
    if at_once:
        return (yield [(shard, flip) for flip in (1, 2, 3)])
    (two,) = yield [(shard, 2)]
    (both,) = yield [(jnp.stack([shard, two]), 1)]
    return both[0], two, both[1]


def gather(shard, z, split, at_once):
    others = yield from around_z(shard, at_once)
    left, right = join_z(z, shard, others, split)
    near_l, near_r = yield [(left, 8), (right, 16)]
    return (yield from spread(jnp.stack([left, near_l]), jnp.stack([right, near_r])))


def gather_pairs(shard, z):
    half = shard.shape[1] // 2
    left, right = shard[:, :half], shard[:, half:]
    near_l, near_r = yield [(left, 8), (right, 16)]
    others = yield from around_z(jnp.stack([left, near_l, right, near_r]), False)
    keep_l, keep_r = join_z_pairs(z, left, right, near_l, near_r, others)
    return (yield from spread(keep_l, keep_r))


def spread(keep_l, keep_r):
    far_l, far_r, *near = yield [(keep_l, 16), (keep_r, 8), (keep_l, 4), (keep_r, 4)]
    far = yield [(far_l, 4), (far_r, 4)]
    return (keep_l, keep_r, far_l, far_r, *near, *far)


def scatter(z, send_l, send_r, keep_l, keep_r):
    other_l, other_r = yield [(send_l, 16), (send_r, 8)]
    send_l, send_r, left, right = add_pairs(keep_l, keep_r, other_l, other_r)
    other_l, other_r = yield [(send_l, 8), (send_r, 16)]
    mine, *sends = add_split(z, left, right, other_l, other_r)
    others = yield [(send, flip + 1) for flip, send in enumerate(sends)]
    return settle_z(mine, others)


def scatter_pairs(z, send_l, send_r, keep_l, keep_r):
    other_l, other_r = yield [(send_l, 16), (send_r, 8)]
    mine, send = add_z_pairs(z, keep_l, keep_r, other_l, other_r)
    (other,) = yield [(send, 1)]
    mine, send = add_next(mine, other)
    (other,) = yield [(send, 2)]
    send_l, send_r, keep = add_four(mine, other)
    other_l, other_r = yield [(send_l, 8), (send_r, 16)]
    return settle_halves(keep, other_l, other_r)


def cut(whole, split):
    blocks = whole.reshape(8, whole.shape[0] // 8, whole.shape[1])
    sides = (blocks[..., :split], blocks[..., split:])
    return tuple(
        jnp.stack([sides[flip[2]][flip[0] * 4 + flip[1] * 2 + core] for flip in flips])
        for core in range(2)
        for flips in GROUPS
    )


def uncut(own, send):
    parts = jnp.stack([array.reshape(array.shape[0], 4, -1) for array in (own, send)], axis=2)
    return parts.reshape(own.shape[0], -1)


def per_device(
    paired,
    tokens,
    cotangent,
    segments,
    picks,
    w_qkv,
    w_out,
    w_up,
    w_down,
    vectors,
    m_qkv,
    m_out,
    m_up,
    m_down,
    m_vectors,
    v_qkv,
    v_out,
    v_up,
    v_down,
    v_vectors,
):
    devices_all = lax.axis_size("wide") * lax.axis_size("narrow")
    lane = lax.axis_index(AXES)
    seq_count, top_count = picks.shape
    seq_len = segments.shape[1]
    model_width = tokens.shape[1]
    qkv_width = w_qkv.shape[1]
    ff_width = w_up.shape[1]
    shard_width = vectors.shape[1]
    split_a, split_b, split_c = 2 * model_width, ff_width // 2, model_width // 2
    z = (lane & 3).reshape(1)
    me = (lane >> 2).reshape(1) if paired else jnp.zeros((1,), jnp.int32)

    turned = jnp.pad(vectors.T, ((0, 0), (0, 125)))
    chunk_a = jnp.concatenate([w_qkv, w_out, turned], axis=1).astype(bf16)
    chunk_b = w_up.astype(bf16)
    chunk_c = w_down.astype(bf16)

    def start(chain, *args):
        return Steps(chain(*args)) if paired else None

    def tick(chains, value):
        return slot(chains, value) if paired else value

    def stage(chains, value):
        return ready(chains, value) if paired else value

    def whole(take, chunk, split):
        if paired:
            return take.result
        return cut(lax.all_gather(chunk, AXES, axis=0, tiled=True), split)

    hot = picks[:, :, None] == jnp.arange(seq_len, dtype=jnp.int32)[None, None, :]
    hot_low = hot.astype(bf16)
    tok_blocks = tokens.reshape(seq_count, seq_len, model_width)
    back_blocks = cotangent.reshape(seq_count, seq_len, model_width)

    def pick(blocks):
        rows = jnp.einsum("skl,sld->skd", hot_low, blocks, preferred_element_type=f32)
        return rows.astype(bf16).reshape(-1, model_width)

    def place(blocks, rows):
        rows = rows.reshape(seq_count, top_count, model_width)
        spread = jnp.einsum("skl,skd->sld", hot_low, rows, preferred_element_type=f32).astype(bf16)
        taken = jnp.any(hot, axis=1)
        return jnp.where(taken[:, :, None], spread, blocks).reshape(-1, model_width)

    take_a = start(gather, chunk_a, z, split_a, True)
    take_c = start(gather_pairs, chunk_c, z)
    picked = pick(tok_blocks)
    back_rows = pick(back_blocks)
    seg_sel = jnp.sum(jnp.where(hot, segments[:, None, :], 0), axis=-1)
    seg_row, seg_col = seg_sel[:, None, :], seg_sel[:, :, None]
    spot = jnp.arange(model_width, dtype=jnp.int32)
    half, eighth = model_width // 2, model_width // 8
    flip = spot % half // eighth * 2 + spot // half
    order = ((me[0] ^ flip) * eighth + spot % eighth)[None]
    inputs = (picked, back_rows, seg_row, seg_col, order, chunk_b)
    inputs = tick([take_a], inputs)
    take_b = start(gather, inputs[-1], z, split_b, False)
    inputs = tick([take_a, take_b, take_c], inputs[:-1])
    inputs = tick([take_a, take_b], inputs)
    inputs = tick([take_a, take_b, take_c], inputs)

    all_a = whole(take_a, chunk_a, split_a)
    picked, back_rows = inputs[:2]
    order = inputs[4]
    state = attend(me, all_a, *inputs)
    state = tick([take_b, take_c], state)
    own, send, df, gate, vec, added, h2, all_qkv, all_out, qkv, probs = state
    early = start(exchange, send)
    h2 = stage([take_c], h2)
    h2 = tick([take_b, early], h2)
    (sib,) = early.result if paired else (send,)
    all_b = whole(take_b, chunk_b, split_b)
    g_own, g_send, g_sib, h2_pair, all_up, slope = climb(me, all_b, h2, sib, order)

    def give(chain, name, products, split):
        if paired:
            return Steps(chain(z, *outer(name, products, split)))
        grads = [dot_tn(uncut(one.value(), far.value()), two.value()) for one, two, far, _ in products]
        grad = jnp.concatenate(grads, axis=1)
        grad = lax.psum_scatter(grad, AXES, scatter_dimension=0, tiled=True)
        return grad, jnp.full((8, 128), jnp.sum(grad * grad))

    df_sib = jnp.concatenate([sib[2], sib[3]], axis=1)
    left_c = View(g_sib) if paired else View(g_send)
    give_c = give(
        scatter_pairs, "outer_c", [(View(g_own), View(df), left_c, View(df_sib))], split_c
    )
    slope = stage([give_c], slope)
    slope = tick([take_c], slope)
    slope = tick([take_c], slope)
    all_c = whole(take_c, chunk_c, split_c)
    du, all_down = descend(me, all_c, slope, df)
    late_u = start(exchange, du)
    du = stage([late_u], du)
    dmiddle, da, dg2 = unclimb(all_up, du, picked, added, gate, back_rows, vec)
    da, dmiddle = tick([late_u, give_c], (da, dmiddle))
    (du_sib,) = late_u.result if paired else (du,)
    views = [View(h2_pair, lead=place) for place in range(2)]
    if not paired:
        cols = h2.reshape(h2.shape[0], 4, 2, -1)
        views = [View(cols[:, :, core].reshape(h2.shape[0], -1)) for core in range(2)]
    give_b = give(
        scatter_pairs, "outer_b", [(views[0], View(du), views[1], View(du_sib))], split_b
    )
    da = stage([give_b, give_c], da)
    dqkv = unattend(all_out, da, qkv, probs)
    late_q = start(exchange, dqkv, da)
    dqkv, dmiddle = tick([late_q], (dqkv, dmiddle))
    dqkv_sib, da_sib = late_q.result if paired else (dqkv, da)
    give_a = give(
        scatter,
        "outer_a",
        [
            (View(own, lead=0), View(dqkv), View(sib, lead=0), View(dqkv_sib)),
            (View(own, lead=1), View(da), View(sib, lead=1), View(da_sib)),
        ],
        split_a,
    )
    g_own, dqkv = stage([give_a], (g_own, dqkv))
    new_rows, dlogit, dr = finish_mlp(
        all_down, g_own, g_send, picked, added, gate, back_rows
    )
    grad_rows, dg1 = finish_rows(all_qkv, dqkv, picked, back_rows, dmiddle, dlogit, vec)
    new_rows, grad_rows, dg1 = tick([give_b, give_c], (new_rows, grad_rows, dg1))
    new_rows = stage([give_b, give_c], new_rows)
    mixed_rows = place(tok_blocks, new_rows)
    grad_vectors = jnp.stack([dg1[0], dg2[0], dr[0]], axis=0)
    vec_parts = grad_vectors.reshape(3, devices_all, shard_width).transpose(1, 0, 2)
    mixed_rows, vec_parts, grad_rows = tick(
        [give_a, give_b, give_c], (mixed_rows, vec_parts, grad_rows)
    )
    grad_rows = stage([give_a, give_b, give_c], grad_rows)
    grad_vec = jnp.sum(lax.all_to_all(vec_parts, AXES, 0, 0, tiled=True), axis=0)
    grad_rows, grad_vec = tick([give_a, give_b, give_c], (grad_rows, grad_vec))
    grad_rows = stage([give_a, give_b], grad_rows)
    input_grad = place(back_blocks, grad_rows)
    input_grad, grad_vec = tick([give_a, give_b], (input_grad, grad_vec))
    if paired:
        give_a, give_b, give_c = give_a.result, give_b.result, give_c.result
    local_sq = give_a[1] + give_b[1] + give_c[1] + jnp.sum(grad_vec * grad_vec)
    squares = jnp.broadcast_to(local_sq[:1], (devices_all, 128))
    squares = lax.all_to_all(squares, AXES, 0, 0, tiled=True)
    params_all = 4 * model_width * model_width + 2 * model_width * ff_width + 3 * model_width
    selected_all = seq_count * top_count * devices_all
    clip_limit = limit_scale * math.sqrt(params_all * selected_all)
    norm, *news = update(
        squares,
        clip_limit,
        [
            View(give_a[0], qkv_width),
            View(give_a[0], model_width, qkv_width),
            View(give_b[0]),
            View(give_c[0]),
        ],
        [
            (w_qkv, m_qkv, v_qkv),
            (w_out, m_out, v_out),
            (w_up, m_up, v_up),
            (w_down, m_down, v_down),
        ],
        grad_vec,
        (m_vectors, v_vectors),
    )
    return (
        mixed_rows,
        input_grad,
        norm[0, 0],
        *news[0:12:3],
        *news[1:12:3],
        news[12],
        *news[2:12:3],
        news[13],
    )


def solution(mesh):
    placed = (
        P(("wide", "narrow"), None),
        P(("wide", "narrow"), None),
        P(("wide", "narrow"), None),
        P(("wide", "narrow"), None),
        P(("wide", "narrow"), None),
        P(("wide", "narrow"), None),
        P(("wide", "narrow"), None),
        P(("wide", "narrow"), None),
        P(None, ("wide", "narrow")),
        P(("wide", "narrow"), None),
        P(("wide", "narrow"), None),
        P(("wide", "narrow"), None),
        P(("wide", "narrow"), None),
        P(None, ("wide", "narrow")),
        P(("wide", "narrow"), None),
        P(("wide", "narrow"), None),
        P(("wide", "narrow"), None),
        P(("wide", "narrow"), None),
        P(None, ("wide", "narrow")),
    )
    paired = mesh.shape["wide"] == 8 and mesh.shape["narrow"] == 4
    return jax.shard_map(
        functools.partial(per_device, paired),
        mesh=mesh,
        in_specs=placed,
        out_specs=(
            P(("wide", "narrow"), None),
            P(("wide", "narrow"), None),
            P(),
            P(("wide", "narrow"), None),
            P(("wide", "narrow"), None),
            P(("wide", "narrow"), None),
            P(("wide", "narrow"), None),
            P(("wide", "narrow"), None),
            P(("wide", "narrow"), None),
            P(("wide", "narrow"), None),
            P(("wide", "narrow"), None),
            P(None, ("wide", "narrow")),
            P(("wide", "narrow"), None),
            P(("wide", "narrow"), None),
            P(("wide", "narrow"), None),
            P(("wide", "narrow"), None),
            P(None, ("wide", "narrow")),
        ),
        check_vma=False,
    )
```

```python
import functools
import math

import jax
import jax.numpy as jnp
from jax import lax
from jax.experimental import pallas as pl
from jax.experimental.pallas import tpu as pltpu
from jax.sharding import PartitionSpec as P

HEAD_DIM = 64


norm_eps = 1e-06
beta_one = 0.9
beta_two = 0.999
adam_eps = 1e-08
learn_rate = 0.03
decay_rate = 0.1
adam_step = 10
limit_scale = 0.01
masked_out = -1e30
AXES = ("wide", "narrow")


def moment_update(grad_part, first, second):
    first_new = beta_one * first + (1.0 - beta_one) * grad_part
    second_new = beta_two * second + (1.0 - beta_two) * grad_part * grad_part
    return (first_new, second_new)


def adam_update(master, grad_part, first, second):
    first_new, second_new = moment_update(grad_part, first, second)
    first_hat = first_new / (1.0 - beta_one**adam_step)
    second_hat = second_new / (1.0 - beta_two**adam_step)
    master_new = master - learn_rate * (
        first_hat / (jnp.sqrt(second_hat) + adam_eps) + decay_rate * master
    )
    return (master_new, first_new, second_new)


f32, bf16 = jnp.float32, jnp.bfloat16
PAIR = 2 * HEAD_DIM
head_scale = HEAD_DIM ** (-0.5)
KEEP_L = ((0, 0, 0), (0, 1, 0))
KEEP_R = ((0, 0, 1), (1, 0, 1))
FAR_L = ((1, 0, 0), (1, 1, 0))
FAR_R = ((0, 1, 1), (1, 1, 1))
GROUPS = (KEEP_L, KEEP_R, FAR_L, FAR_R)


def kernel(body, name, outs, args, kinds, scratch=(), limit=24, loose=0):
    spaces = {"s": pltpu.SMEM, "v": pltpu.VMEM, "h": pltpu.VMEM, "a": pltpu.HBM}
    held = len(outs) - loose
    return pl.pallas_call(
        body,
        out_shape=[
            jax.ShapeDtypeStruct(*out) if place < held else pltpu.HBM(*out)
            for place, out in enumerate(outs)
        ],
        in_specs=[pl.BlockSpec(memory_space=spaces[kind]) for kind in kinds],
        out_specs=[
            pl.BlockSpec(memory_space=pltpu.VMEM if place < held else pltpu.HBM)
            for place in range(len(outs))
        ],
        scratch_shapes=list(scratch),
        compiler_params=pltpu.CompilerParams(vmem_limit_bytes=limit << 20),
        cost_estimate=pl.CostEstimate(flops=1, bytes_accessed=1, transcendentals=0),
        name=name,
    )(
        *(
            pltpu.with_memory_space_constraint(arg, pltpu.HBM) if kind in "ah" else arg
            for arg, kind in zip(args, kinds)
        )
    )


def each_block(pieces):
    for core in range(2):
        for group, flips in enumerate(GROUPS):
            for place, flip in enumerate(flips):
                yield flip[0] * 4 + flip[1] * 2 + core, flip[2], pieces[core * 4 + group].at[place]


def start_all(copies):
    for copy in copies:
        copy.start()


def wait_all(copies):
    for copy in copies:
        copy.wait()


def fetch(pieces, me, sem, base, left, right):
    copies = []
    for flip, half, block in each_block(pieces):
        rows = block.shape[0]
        start = pl.multiple_of((me ^ flip) * rows, rows)
        for target, column, out_column, width in (left, right)[half]:
            copies.append(
                pltpu.make_async_copy(
                    block.at[:, pl.ds(column, width)],
                    target.at[pl.ds(start, rows), pl.ds(out_column, width)],
                    sem.at[base + len(copies)],
                )
            )
    return copies


def dot_nt(left, right):
    return lax.dot_general(left, right, (((1,), (1,)), ((), ())), preferred_element_type=f32)


def dot_tn(left, right):
    return lax.dot_general(left, right, (((0,), (0,)), ((), ())), preferred_element_type=f32)


def dot_nn(left, right):
    return jnp.dot(left, right, preferred_element_type=f32)


def mean_last(array):
    return jnp.mean(array, axis=-1, keepdims=True)


def sum_rows(array):
    return jnp.sum(array, axis=0, keepdims=True)


def head_masks(dtype):
    lanes = lax.broadcasted_iota(jnp.int32, (1, PAIR), 1)
    first = (lanes < HEAD_DIM).astype(f32).astype(dtype)
    return first, (1 - first).astype(dtype)


def two_heads(pair, masks):
    return jnp.concatenate([pair * masks[0], pair * masks[1]], axis=0)


def one_pair(stacked, masks):
    rows = stacked.shape[0] // 2
    return stacked[:rows] * masks[0] + stacked[rows:] * masks[1]


def gather_input(w_qkv, w_out, vectors):
    rows, first = w_qkv.shape
    second = w_out.shape[1]

    def body(qkv_ref, out_ref, vec_ref, chunk_ref, turned):
        chunk_ref[:, :first] = qkv_ref[...].astype(bf16)
        chunk_ref[:, first : first + second] = out_ref[...].astype(bf16)
        turned[...] = jnp.zeros_like(turned)
        turned[:3] = vec_ref[...]
        same = lax.broadcasted_iota(jnp.int32, (rows, rows), 0) == lax.broadcasted_iota(
            jnp.int32, (rows, rows), 1
        )
        columns = dot_nt(same.astype(f32).astype(bf16), turned[...].astype(bf16))
        chunk_ref[:, first + second :] = columns.astype(bf16)

    outs = [((rows, first + second + 128), bf16)]
    scratch = [pltpu.VMEM((128, rows), f32)]
    return kernel(body, "gather_input", outs, (w_qkv, w_out, vectors), "hhh", scratch)[0]


def attend(me, pieces, picked, back_rows, seg_row, seg_col, order):
    rows, width = picked.shape
    seqs = seg_row.shape[0]
    top = rows // seqs
    pairs = width // PAIR
    first = pieces[0].shape[2]
    rest = 3 * width - first
    spare = pieces[1].shape[2] - rest - width

    def body(me_ref, *refs):
        blocks, refs = refs[:8], refs[8:]
        x_ref, dy_ref, seg_row_ref, seg_col_ref, order_ref = refs[:5]
        own_ref, send_ref, df_ref, gate_ref, vec_ref, add_ref, h2_ref = refs[5:12]
        all_ref, out_ref, qkv_out, prob_out = refs[12:16]
        w_qkv, w_out, w_vec, qkv_ref, prob_ref, att_ref, sem = refs[16:]
        vec_copies = fetch(blocks, me_ref[0], sem, 0, (), ((w_vec, rest + width, 0, spare),))
        left = fetch(blocks, me_ref[0], sem, 8, ((w_qkv, 0, 0, first),), ())
        right = fetch(blocks, me_ref[0], sem, 16, (), ((w_qkv, 0, first, rest),))
        out_copies = fetch(blocks, me_ref[0], sem, 24, (), ((w_out, rest, 0, width),))
        start_all(vec_copies + left + right + out_copies)
        wait_all(vec_copies)
        vec = w_vec[...].astype(f32).T[:8]
        vec_ref[...] = vec
        x = x_ref[...].astype(f32)
        h1 = (x * lax.rsqrt(mean_last(x * x) + norm_eps) * vec[0:1]).astype(bf16)
        for copies, start, count in ((left, 0, first), (right, first, rest)):
            wait_all(copies)
            for part in range(start, start + count, 384):
                lanes = pl.ds(part, 384)
                qkv_ref[:, lanes] = dot_nn(h1, w_qkv[:, lanes]).astype(bf16)
        stored = [
            pltpu.make_async_copy(w_qkv, all_ref, sem.at[32]),
            pltpu.make_async_copy(qkv_ref, qkv_out, sem.at[33]),
            pltpu.make_async_copy(w_out, out_ref, sem.at[34]),
        ]
        wait_all(out_copies)
        start_all(stored)
        masks, masks_f = head_masks(bf16), head_masks(f32)
        ordered_pairs = lax.broadcasted_iota(jnp.int32, (top, top), 1) <= lax.broadcasted_iota(
            jnp.int32, (top, top), 0
        )
        for seq in range(seqs):
            here = pl.ds(seq * top, top)
            seen = ordered_pairs & (seg_col_ref[seq] == seg_row_ref[seq])
            hidden = jnp.where(seen, 0.0, masked_out)
            hidden = jnp.concatenate([hidden, hidden], axis=0)
            for pair in range(pairs):
                q, k, v = (
                    qkv_ref[here, pl.ds(part * width + pair * PAIR, PAIR)] for part in range(3)
                )
                scores = dot_nt(two_heads(q, masks), k) * head_scale
                scores = jnp.where(hidden < 0.0, masked_out, scores)
                power = jnp.exp(scores - jnp.max(scores, axis=-1, keepdims=True))
                probs = power / jnp.sum(power, axis=-1, keepdims=True)
                prob_ref[seq * pairs + pair] = probs
                mixed = one_pair(dot_nn(probs.astype(bf16), v), masks_f)
                att_ref[here, pl.ds(pair * PAIR, PAIR)] = mixed.astype(bf16)
            group = pl.ds(seq * pairs, pairs)
            stored.append(
                pltpu.make_async_copy(prob_ref.at[group], prob_out.at[group], sem.at[35 + seq])
            )
            stored[-1].start()
        gate = jax.nn.sigmoid(jnp.sum(x * vec[2:3], axis=-1, keepdims=True))
        gate_ref[...] = jnp.broadcast_to(gate, gate_ref.shape)
        df = (gate * dy_ref[...].astype(f32)).astype(bf16)
        df_ref[...] = df
        added = dot_nn(att_ref[...], w_out[...])
        add_ref[...] = added
        middle = x + added
        h2 = (middle * lax.rsqrt(mean_last(middle * middle) + norm_eps) * vec[1:2]).astype(bf16)
        h2_ref[...] = h2
        for half in range(2):
            lanes = slice(half * (width // 2), (half + 1) * (width // 2))
            send_ref[2 + half] = df[:, lanes]
            send_ref[4 + half] = h2[:, lanes]
        chosen = one_hot_columns(order_ref)
        for place, array in enumerate((h1, att_ref[...])):
            parted = dot_nn(array, chosen).astype(bf16)
            own_ref[place] = parted[:, : width // 2]
            send_ref[place] = parted[:, width // 2 :]
        wait_all(stored)

    outs = [
        ((2, rows, width // 2), bf16),
        ((6, rows, width // 2), bf16),
        ((rows, width), bf16),
        ((rows, 128), f32),
        ((8, width), f32),
        ((rows, width), f32),
        ((rows, width), bf16),
        ((width, 3 * width), bf16),
        ((width, width), bf16),
        ((rows, 3 * width), bf16),
        ((seqs * pairs, 2 * top, top), f32),
    ]
    scratch = [
        pltpu.VMEM((width, 3 * width), bf16),
        pltpu.VMEM((width, width), bf16),
        pltpu.VMEM((width, spare), bf16),
        pltpu.VMEM((rows, 3 * width), bf16),
        pltpu.VMEM((seqs * pairs, 2 * top, top), f32),
        pltpu.VMEM((rows, width), bf16),
        pltpu.SemaphoreType.DMA((35 + seqs,)),
    ]
    args = (me, *pieces, picked, back_rows, seg_row, seg_col, order)
    return kernel(body, "attend", outs, args, "s" + "a" * 8 + "vvvvv", scratch, 26, 4)


def one_hot_columns(order_ref):
    width = order_ref.shape[1]
    chosen = lax.broadcasted_iota(jnp.int32, (width, width), 0) == order_ref[...]
    return chosen.astype(f32).astype(bf16)


def climb(me, pieces, h2, sib, order):
    rows, width = h2.shape
    first = pieces[0].shape[2]
    block = 2 * first // 8

    def body(me_ref, *refs):
        blocks, refs = refs[:8], refs[8:]
        h2_ref, sib_ref, order_ref = refs[:3]
        own_ref, send_ref, far_ref, pair_ref, up_ref, slope_out = refs[3:9]
        w_up, slope_ref, both_ref, sem = refs[9:]
        copies = fetch(
            blocks, me_ref[0], sem, 0, ((w_up, 0, 0, first),), ((w_up, 0, first, first),)
        )
        start_all(copies)
        both_ref[:rows] = h2_ref[...]
        for half in range(2):
            lanes = pl.ds(half * (width // 2), width // 2)
            both_ref[rows:, lanes] = sib_ref[4 + half]
        chosen = one_hot_columns(order_ref)[:, : width // 2]
        parted = dot_nn(both_ref[...], chosen).astype(bf16)
        pair_ref[0] = parted[:rows]
        pair_ref[1] = parted[rows:]
        wait_all(copies)
        stored = [pltpu.make_async_copy(w_up, up_ref, sem.at[16])]
        start_all(stored)
        scale = math.sqrt(2.0 / math.pi)
        for flip in range(8):
            start = pl.multiple_of((me_ref[0] ^ flip) * block, block)
            place = flip // 2
            lanes = pl.ds(place * block, block)
            weights = w_up[:, pl.ds(start, block)]
            u = dot_nn(both_ref[:rows], weights)
            square = u * u
            bent = jnp.tanh(scale * (u + 0.044715 * (square * u)))
            half_up = 0.5 * (1.0 + bent)
            target = send_ref if flip % 2 else own_ref
            target[:, lanes] = (u * half_up).astype(bf16)
            where = (flip % 2) * 4 + place
            slope_ref[where] = half_up + (0.5 * u) * (1.0 - bent * bent) * (
                scale * (1.0 + (3.0 * 0.044715) * square)
            )
            stored.append(
                pltpu.make_async_copy(
                    slope_ref.at[where], slope_out.at[where], sem.at[17 + flip]
                )
            )
            stored[-1].start()
            if flip % 2 == 0:
                u = dot_nn(both_ref[rows:], weights)
                bent = jnp.tanh(scale * (u + 0.044715 * (u * u * u)))
                far_ref[:, lanes] = (0.5 * u * (1.0 + bent)).astype(bf16)
        wait_all(stored)

    outs = [
        ((rows, 4 * block), bf16),
        ((rows, 4 * block), bf16),
        ((rows, 4 * block), bf16),
        ((2, rows, width // 2), bf16),
        ((width, 8 * block), bf16),
        ((8, rows, block), f32),
    ]
    scratch = [
        pltpu.VMEM((width, 8 * block), bf16),
        pltpu.VMEM((8, rows, block), f32),
        pltpu.VMEM((2 * rows, width), bf16),
        pltpu.SemaphoreType.DMA((25,)),
    ]
    args = (me, *pieces, h2, sib, order)
    return kernel(body, "climb", outs, args, "s" + "a" * 8 + "vvv", scratch, 26, 2)


def vector_columns(order, mine, other):
    width = order.shape[1]
    half = width // 2

    def body(order_ref, *refs):
        ins, (left, right, rows) = refs[:6], refs[6:]
        chosen = one_hot_columns(order_ref)[:, :half]
        rows[...] = jnp.zeros_like(rows)
        for place in range(3):
            rows[place : place + 1] = ins[place][0:1] + ins[3 + place][0:1]
        columns = rows[...].T.astype(bf16)
        for part in range(2):
            left[part] = chosen[part * half : (part + 1) * half]
            right[part] = columns[part * half : (part + 1) * half]

    outs = [((2, half, half), bf16), ((2, half, 128), bf16)]
    scratch = [pltpu.VMEM((128, width), f32)]
    args = (order, *mine, *other)
    return kernel(body, "vector_columns", outs, args, "v" * 7, scratch)


class View:
    def __init__(self, array, columns=None, first=0, lead=None):
        self.array, self.first, self.lead = array, first, lead
        self.columns = columns or array.shape[-1]

    def value(self):
        array = self.array if self.lead is None else self.array[self.lead]
        return array[:, self.first : self.first + self.columns]

    def read(self, ref, first, columns):
        lanes = pl.ds(self.first + first, columns)
        return ref[:, lanes] if self.lead is None else ref[self.lead, :, lanes]


def outer(name, products, split):
    length = products[0][0].columns // 4
    total = sum(product[1].columns for product in products)
    widths = (split, total - split)
    order = ((2, 3), (1, 3), (0, 1), (0, 2))

    def body(*refs):
        ins, outs = refs[: 4 * len(products)], refs[4 * len(products) :]
        base = 0
        for number, product in enumerate(products):
            reads = [
                functools.partial(view.read, ref)
                for view, ref in zip(product, ins[4 * number : 4 * number + 4])
            ]
            columns = product[1].columns
            step = min(768, columns)
            for start in range(0, columns, step):
                for first in range(0, 4 * length, 384):
                    value = dot_tn(reads[0](first, 384), reads[1](start, step))
                    value += dot_tn(reads[2](first, 384), reads[3](start, step))
                    for block in range(first // length, (first + 384) // length):
                        part = value[block * length - first : (block + 1) * length - first]
                        for half in range(2):
                            low = max(base + start, half * split)
                            high = min(base + start + step, split + half * (total - split))
                            if high <= low:
                                continue
                            piece = part[:, low - base - start : high - base - start]
                            out_lanes = pl.ds(low - half * split, high - low)
                            for out in (half, 2 + half):
                                if block in order[out]:
                                    outs[out][order[out].index(block), :, out_lanes] = piece.astype(
                                        outs[out].dtype
                                    )
            base += columns

    outs = [
        ((2, length, widths[out % 2]), bf16 if out < 2 else f32) for out in range(4)
    ]
    args = [view.array for product in products for view in product]
    return kernel(body, name, outs, args, "v" * len(args))


def descend(me, pieces, slope, df):
    rows, width = df.shape
    block = slope.shape[2]

    def body(me_ref, *refs):
        blocks, refs = refs[:8], refs[8:]
        slope_in, df_ref, du_ref, down_ref, w_down, slope_ref, sem = refs
        copies = [[] for _ in range(8)]
        for flip, side, part in each_block(blocks):
            lanes = pl.ds(side * (width // 2), width // 2)
            place = (flip % 2) * 4 + flip // 2
            target = w_down.at[pl.ds(place * block, block), lanes]
            copies[place].append(
                pltpu.make_async_copy(part, target, sem.at[place * 2 + side])
            )
        for place, pair in enumerate(copies):
            pair.append(
                pltpu.make_async_copy(
                    slope_in.at[place], slope_ref.at[place], sem.at[17 + place]
                )
            )
            start_all(pair)
        for place in range(8):
            wait_all(copies[place])
            flip = place % 4 * 2 + place // 4
            start = pl.multiple_of((me_ref[0] ^ flip) * block, block)
            dg = dot_nt(df_ref[...], w_down[pl.ds(place * block, block)])
            du_ref[:, pl.ds(start, block)] = (dg * slope_ref[place]).astype(bf16)
        stored = pltpu.make_async_copy(w_down, down_ref, sem.at[16])
        stored.start()
        stored.wait()

    outs = [((rows, 8 * block), bf16), ((8 * block, width), bf16)]
    scratch = [
        pltpu.VMEM((8 * block, width), bf16),
        pltpu.VMEM((8, rows, block), f32),
        pltpu.SemaphoreType.DMA((25,)),
    ]
    args = (me, *pieces, slope, df)
    return kernel(body, "descend", outs, args, "s" + "a" * 9 + "v", scratch, 24, 1)


def unclimb(w_up, du, picked, added, gate, back_rows, vec):
    rows, width = picked.shape

    def body(up_ref, du_ref, x_ref, add_ref, gate_ref, dy_ref, vec_ref, dm_ref, da_ref, dg_ref):
        dh = dot_nt(du_ref[...], up_ref[...])
        middle = x_ref[...].astype(f32) + add_ref[...]
        inverse = lax.rsqrt(mean_last(middle * middle) + norm_eps)
        unit = middle * inverse
        dg_ref[...] = jnp.broadcast_to(sum_rows(dh * unit), dg_ref.shape)
        scaled = dh * vec_ref[1:2]
        dm = inverse * (scaled - unit * mean_last(scaled * unit))
        dm_ref[...] = dm
        da_ref[...] = (gate_ref[:, 0:1] * dy_ref[...].astype(f32) + dm).astype(bf16)

    outs = [((rows, width), f32), ((rows, width), bf16), ((8, width), f32)]
    args = (w_up, du, picked, added, gate, back_rows, vec)
    return kernel(body, "unclimb", outs, args, "v" * 7)


def unattend(w_out, da, qkv, probs):
    rows, width = da.shape
    top = probs.shape[2]
    seqs, pairs = rows // top, width // PAIR

    def body(out_ref, da_ref, qkv_ref, prob_ref, dqkv_ref, do_ref):
        do_ref[...] = dot_nt(da_ref[...], out_ref[...]).astype(bf16)
        masks, masks_f = head_masks(bf16), head_masks(f32)
        for seq in range(seqs):
            here = pl.ds(seq * top, top)
            for pair in range(pairs):
                lanes = [pl.ds(part * width + pair * PAIR, PAIR) for part in range(3)]
                q, k, v = (qkv_ref[here, part] for part in lanes)
                do = two_heads(do_ref[here, pl.ds(pair * PAIR, PAIR)], masks)
                probs = prob_ref[seq * pairs + pair]
                dprobs = dot_nt(do, v)
                dscores = probs * (dprobs - jnp.sum(dprobs * probs, axis=-1, keepdims=True))
                dscores = dscores.astype(bf16)
                dq = one_pair(dot_nn(dscores, k), masks_f) * head_scale
                dk = dot_tn(dscores, two_heads(q, masks)) * head_scale
                dv = dot_tn(probs.astype(bf16), do)
                for part, value in zip(lanes, (dq, dk, dv)):
                    dqkv_ref[here, part] = value.astype(bf16)

    scratch = [pltpu.VMEM((rows, width), bf16)]
    outs = [((rows, 3 * width), bf16)]
    return kernel(body, "unattend", outs, (w_out, da, qkv, probs), "vvvv", scratch)[0]


def finish_mlp(w_down, own, send, picked, added, gate, back_rows):
    rows, width = picked.shape
    half = w_down.shape[0] // 2

    def body(down_ref, own_ref, send_ref, x_ref, add_ref, gate_ref, dy_ref, *outs):
        new_ref, dlogit_ref, dr_ref = outs
        out = dot_nn(own_ref[:, :half], down_ref[:half])
        out += dot_nn(send_ref[:, :half], down_ref[half:])
        both = add_ref[...] + out
        x = x_ref[...].astype(f32)
        gate = gate_ref[:, 0:1]
        new_ref[...] = (x + gate * both).astype(bf16)
        dlogit = jnp.sum(dy_ref[...].astype(f32) * both, axis=-1, keepdims=True)
        dlogit = dlogit * gate * (1.0 - gate)
        dlogit_ref[...] = jnp.broadcast_to(dlogit, dlogit_ref.shape)
        dr_ref[...] = jnp.broadcast_to(sum_rows(dlogit * x), dr_ref.shape)

    outs = [((rows, width), bf16), ((rows, 128), f32), ((8, width), f32)]
    args = (w_down, own, send, picked, added, gate, back_rows)
    return kernel(body, "finish_mlp", outs, args, "v" * 7)


def finish_rows(w_qkv, dqkv, picked, back_rows, dmiddle, dlogit, vec):
    rows, width = picked.shape

    def body(all_ref, dqkv_ref, x_ref, dy_ref, dm_ref, dlogit_ref, vec_ref, grad_ref, dg_ref):
        dh = dot_nt(dqkv_ref[...], all_ref[...])
        x = x_ref[...].astype(f32)
        inverse = lax.rsqrt(mean_last(x * x) + norm_eps)
        unit = x * inverse
        dg_ref[...] = jnp.broadcast_to(sum_rows(dh * unit), dg_ref.shape)
        scaled = dh * vec_ref[0:1]
        dx = inverse * (scaled - unit * mean_last(scaled * unit))
        grad = dy_ref[...].astype(f32) + dm_ref[...] + dx + dlogit_ref[:, 0:1] * vec_ref[2:3]
        grad_ref[...] = grad.astype(bf16)

    outs = [((rows, width), bf16), ((8, width), f32)]
    args = (w_qkv, dqkv, picked, back_rows, dmiddle, dlogit, vec)
    return kernel(body, "finish_rows", outs, args, "v" * 7)


def join_z(z, own, others, split):
    rows, width = own.shape

    def body(z_ref, *refs):
        ins, left_ref, right_ref, total = refs[:4], *refs[4:]
        for flip, block in enumerate(ins):
            start = pl.multiple_of((z_ref[0] ^ flip) * rows, rows)
            total[pl.ds(start, rows)] = block[...].astype(f32)
        left_ref[...] = total[:, :split].astype(bf16)
        right_ref[...] = total[:, split:].astype(bf16)

    outs = [((4 * rows, split), bf16), ((4 * rows, width - split), bf16)]
    scratch = [pltpu.VMEM((4 * rows, width), f32)]
    return kernel(body, "join_z", outs, (z, own, *others), "svvvv", scratch)


def join_z_pairs(z, left, right, near_l, near_r, others):
    rows, width = left.shape

    def body(z_ref, *refs):
        mine, others, outs = refs[:4], refs[4:7], refs[7:]
        for flip in range(4):
            start = pl.ds(pl.multiple_of((z_ref[0] ^ flip) * rows, rows), rows)
            for place in range(4):
                block = others[flip - 1][place] if flip else mine[place][...]
                outs[place // 2][place % 2, start] = block

    outs = [((2, 4 * rows, width), bf16)] * 2
    args = (z, left, near_l, right, near_r, *others)
    return kernel(body, "join_z_pairs", outs, args, "svvvvvvv")


def add_z_pairs(z, keep_l, keep_r, other_l, other_r):
    pair, rows, width = keep_l.shape
    part = rows // 4

    def body(z_ref, keep_l, keep_r, other_l, other_r, mine, send, total):
        for half, (keep, other) in enumerate(((keep_l, other_l), (keep_r, other_r))):
            for place in range(pair):
                total[half * pair + place] = keep[place] + other[place].astype(f32)
        for flip in range(4):
            start = pl.multiple_of((z_ref[0] ^ flip) * part, part)
            out = (mine, send)[flip % 2]
            out[flip // 2] = total[:, pl.ds(start, part)].astype(out.dtype)

    outs = [((2, 4, part, width), f32), ((2, 4, part, width), bf16)]
    scratch = [pltpu.VMEM((4, rows, width), f32)]
    args = (z, keep_l, keep_r, other_l, other_r)
    return kernel(body, "add_z_pairs", outs, args, "svvvv", scratch)


def add_four(mine, other):
    def body(mine, other, send_l, send_r, keep):
        def total(place):
            return mine[place] + other[place].astype(f32)

        width = mine.shape[2]
        keep[:, :width] = total(0)
        keep[:, width:] = total(2)
        send_l[...] = total(1).astype(bf16)
        send_r[...] = total(3).astype(bf16)

    _, rows, width = mine.shape
    outs = [((rows, width), bf16)] * 2 + [((rows, 2 * width), f32)]
    return kernel(body, "add_four", outs, (mine, other), "vv")


def add_pairs(keep_l, keep_r, other_l, other_r):
    def body(keep_l, keep_r, other_l, other_r, send_l, send_r, left, right):
        for keep, other, send, mine in (
            (keep_l, other_l, send_l, left),
            (keep_r, other_r, send_r, right),
        ):
            send[...] = (keep[1] + other[1].astype(f32)).astype(bf16)
            mine[...] = keep[0] + other[0].astype(f32)

    shapes = [keep_l.shape[1:], keep_r.shape[1:]]
    outs = [(shape, kind) for kind in (bf16, f32) for shape in shapes]
    return kernel(body, "add_pairs", outs, (keep_l, keep_r, other_l, other_r), "vvvv")


def add_split(z, keep_l, keep_r, other_l, other_r):
    rows, split = keep_l.shape
    width = split + keep_r.shape[1]
    part = rows // 4

    def body(z_ref, keep_l, keep_r, other_l, other_r, mine, one, two, three, total):
        total[:, :split] = keep_l[...] + other_l[...].astype(f32)
        total[:, split:] = keep_r[...] + other_r[...].astype(f32)
        for flip, out in enumerate((mine, one, two, three)):
            start = pl.multiple_of((z_ref[0] ^ flip) * part, part)
            out[...] = total[pl.ds(start, part)].astype(out.dtype)

    outs = [((part, width), f32)] + [((part, width), bf16)] * 3
    scratch = [pltpu.VMEM((rows, width), f32)]
    args = (z, keep_l, keep_r, other_l, other_r)
    return kernel(body, "add_split", outs, args, "svvvv", scratch)


def add_next(keep, other):
    def body(keep, other, mine, send):
        mine[...] = keep[0] + other[0].astype(f32)
        send[...] = (keep[1] + other[1].astype(f32)).astype(bf16)

    shape = keep.shape[1:]
    return kernel(body, "add_next", [(shape, f32), (shape, bf16)], (keep, other), "vv")


def settle_halves(keep, other_l, other_r):
    def body(keep, other_l, other_r, grad, square):
        width = other_l.shape[1]
        total = None
        for half, other in enumerate((other_l, other_r)):
            lanes = pl.ds(half * width, width)
            value = keep[:, lanes] + other[...].astype(f32)
            grad[:, lanes] = value
            part = jnp.sum(value * value)
            total = part if total is None else total + part
        square[...] = jnp.full(square.shape, total)

    outs = [(keep.shape, f32), ((8, 128), f32)]
    return kernel(body, "settle_halves", outs, (keep, other_l, other_r), "vvv")


def settle_z(mine, others):
    rows, width = mine.shape

    def body(mine, one, two, three, grad, square, last, turned):
        value = mine[...] + one[...].astype(f32) + two[...].astype(f32) + three[...].astype(f32)
        grad[...] = value
        square[...] = jnp.full(square.shape, jnp.sum(value * value))
        turned[...] = jnp.zeros_like(turned)
        turned[:rows] = value[:, width - 128 :]
        last[...] = turned[...].T[:8]

    outs = [(mine.shape, f32), ((8, 128), f32), ((8, 128), f32)]
    scratch = [pltpu.VMEM((128, 128), f32)]
    return kernel(body, "settle_z", outs, (mine, *others), "vvvv", scratch)


def update(squares, limit, grads, states, vec_grad, vec_states):
    count = len(grads)

    def body(square_ref, *refs):
        grad_refs, refs = refs[:count], refs[count:]
        state_refs, refs = refs[: 3 * count], refs[3 * count :]
        vec_ref, vec_m, vec_v, norm_ref, out_refs = *refs[:4], refs[4:]
        norm = jnp.sqrt(jnp.sum(square_ref[...], axis=0, keepdims=True)[:, 0:1])
        norm_ref[...] = jnp.broadcast_to(norm, norm_ref.shape)
        factor = jnp.minimum(1.0, limit / (norm + 1e-06))
        for place in range(count):
            w, m, v = (ref[...] for ref in state_refs[3 * place : 3 * place + 3])
            grad = grads[place].read(grad_refs[place], 0, grads[place].columns) * factor
            for ref, value in zip(out_refs[3 * place :], adam_update(w, grad, m, v)):
                ref[...] = value
        grad = vec_ref[:3, : vec_m.shape[1]] * factor
        first, second = moment_update(grad, vec_m[...], vec_v[...])
        out_refs[-2][...] = first
        out_refs[-1][...] = second

    flat = [array for state in states for array in state]
    outs = [((8, 128), f32)] + [(array.shape, f32) for array in (*flat, *vec_states)]
    args = (squares, *(grad.array for grad in grads), *flat, vec_grad, *vec_states)
    return kernel(body, "update", outs, args, "v" * len(args), (), 32)


class Steps:
    def __init__(self, chain):
        self.chain = chain
        self.result = None
        self.launch(next(chain))

    def launch(self, step):
        self.flips = [flip for _, flip in step]
        self.given = [array for array, _ in step]

    def advance(self, arrays):
        try:
            self.launch(self.chain.send(arrays))
        except StopIteration as stop:
            self.flips, self.given, self.result = (), (), stop.value


def slot(chains, value):
    arrays = [
        [swap(array, flip) for array, flip in zip(chain.given, chain.flips)] for chain in chains
    ]
    arrays, value = lax.optimization_barrier((arrays, value))
    for chain, array in zip(chains, arrays):
        chain.advance(array)
    return value


def ready(chains, value):
    arrays, value = lax.optimization_barrier(([chain.given for chain in chains], value))
    for chain, array in zip(chains, arrays):
        chain.given = array
    return value


def swap(array, bit):
    count = lax.axis_size("wide") * lax.axis_size("narrow")
    return lax.ppermute(array, AXES, [(i, i ^ bit) for i in range(count)])


def exchange(*arrays):
    return (yield [(array, 4) for array in arrays])


def around_z(shard, at_once):
    if at_once:
        return (yield [(shard, flip) for flip in (1, 2, 3)])
    (two,) = yield [(shard, 2)]
    (both,) = yield [(jnp.stack([shard, two]), 1)]
    return both[0], two, both[1]


def gather(shard, z, split, at_once):
    others = yield from around_z(shard, at_once)
    left, right = join_z(z, shard, others, split)
    near_l, near_r = yield [(left, 8), (right, 16)]
    return (yield from spread(jnp.stack([left, near_l]), jnp.stack([right, near_r])))


def gather_pairs(shard, z):
    half = shard.shape[1] // 2
    left, right = shard[:, :half], shard[:, half:]
    near_l, near_r = yield [(left, 8), (right, 16)]
    others = yield from around_z(jnp.stack([left, near_l, right, near_r]), False)
    keep_l, keep_r = join_z_pairs(z, left, right, near_l, near_r, others)
    return (yield from spread(keep_l, keep_r))


def spread(keep_l, keep_r):
    far_l, far_r, *near = yield [(keep_l, 16), (keep_r, 8), (keep_l, 4), (keep_r, 4)]
    far = yield [(far_l, 4), (far_r, 4)]
    return (keep_l, keep_r, far_l, far_r, *near, *far)


def scatter(z, send_l, send_r, keep_l, keep_r):
    other_l, other_r = yield [(send_l, 16), (send_r, 8)]
    send_l, send_r, left, right = add_pairs(keep_l, keep_r, other_l, other_r)
    other_l, other_r = yield [(send_l, 8), (send_r, 16)]
    mine, *sends = add_split(z, left, right, other_l, other_r)
    others = yield [(send, flip + 1) for flip, send in enumerate(sends)]
    return settle_z(mine, others)


def scatter_pairs(z, send_l, send_r, keep_l, keep_r):
    other_l, other_r = yield [(send_l, 16), (send_r, 8)]
    mine, send = add_z_pairs(z, keep_l, keep_r, other_l, other_r)
    (other,) = yield [(send, 1)]
    mine, send = add_next(mine, other)
    (other,) = yield [(send, 2)]
    send_l, send_r, keep = add_four(mine, other)
    other_l, other_r = yield [(send_l, 8), (send_r, 16)]
    return settle_halves(keep, other_l, other_r)


def cut(whole, split):
    blocks = whole.reshape(8, whole.shape[0] // 8, whole.shape[1])
    sides = (blocks[..., :split], blocks[..., split:])
    return tuple(
        jnp.stack([sides[flip[2]][flip[0] * 4 + flip[1] * 2 + core] for flip in flips])
        for core in range(2)
        for flips in GROUPS
    )


def uncut(own, send):
    parts = jnp.stack([array.reshape(array.shape[0], 4, -1) for array in (own, send)], axis=2)
    return parts.reshape(own.shape[0], -1)


def per_device(
    paired,
    tokens,
    cotangent,
    segments,
    picks,
    w_qkv,
    w_out,
    w_up,
    w_down,
    vectors,
    m_qkv,
    m_out,
    m_up,
    m_down,
    m_vectors,
    v_qkv,
    v_out,
    v_up,
    v_down,
    v_vectors,
):
    devices_all = lax.axis_size("wide") * lax.axis_size("narrow")
    lane = lax.axis_index(AXES)
    seq_count, top_count = picks.shape
    seq_len = segments.shape[1]
    model_width = tokens.shape[1]
    qkv_width = w_qkv.shape[1]
    ff_width = w_up.shape[1]
    shard_width = vectors.shape[1]
    split_a, split_b, split_c = 2 * model_width, ff_width // 2, model_width // 2
    z = (lane & 3).reshape(1)
    me = (lane >> 2).reshape(1) if paired else jnp.zeros((1,), jnp.int32)

    chunk_a = gather_input(w_qkv, w_out, vectors)
    chunk_b = w_up.astype(bf16)
    chunk_c = w_down.astype(bf16)

    def start(chain, *args):
        return Steps(chain(*args)) if paired else None

    def tick(chains, value):
        return slot(chains, value) if paired else value

    def stage(chains, value):
        return ready(chains, value) if paired else value

    def whole(take, chunk, split):
        if paired:
            return take.result
        return cut(lax.all_gather(chunk, AXES, axis=0, tiled=True), split)

    hot = picks[:, :, None] == jnp.arange(seq_len, dtype=jnp.int32)[None, None, :]
    hot_low = hot.astype(bf16)
    tok_blocks = tokens.reshape(seq_count, seq_len, model_width)
    back_blocks = cotangent.reshape(seq_count, seq_len, model_width)

    def pick(blocks):
        rows = jnp.einsum("skl,sld->skd", hot_low, blocks, preferred_element_type=f32)
        return rows.astype(bf16).reshape(-1, model_width)

    def place(blocks, rows):
        rows = rows.reshape(seq_count, top_count, model_width)
        spread = jnp.einsum("skl,skd->sld", hot_low, rows, preferred_element_type=f32).astype(bf16)
        taken = jnp.any(hot, axis=1)
        return jnp.where(taken[:, :, None], spread, blocks).reshape(-1, model_width)

    take_a = start(gather, chunk_a, z, split_a, True)
    take_c = start(gather_pairs, chunk_c, z)
    picked = pick(tok_blocks)
    back_rows = pick(back_blocks)
    seg_sel = jnp.sum(jnp.where(hot, segments[:, None, :], 0), axis=-1)
    seg_row, seg_col = seg_sel[:, None, :], seg_sel[:, :, None]
    spot = jnp.arange(model_width, dtype=jnp.int32)
    half, eighth = model_width // 2, model_width // 8
    flip = spot % half // eighth * 2 + spot // half
    order = ((me[0] ^ flip) * eighth + spot % eighth)[None]
    inputs = (picked, back_rows, seg_row, seg_col, order, chunk_b)
    inputs = tick([take_a], inputs)
    take_b = start(gather, inputs[-1], z, split_b, False)
    inputs = tick([take_a, take_b, take_c], inputs[:-1])
    inputs = tick([take_a, take_b], inputs)
    inputs = tick([take_a, take_b, take_c], inputs)

    all_a = whole(take_a, chunk_a, split_a)
    picked, back_rows = inputs[:2]
    order = inputs[4]
    state = attend(me, all_a, *inputs)
    state = tick([take_b, take_c], state)
    own, send, df, gate, vec, added, h2, all_qkv, all_out, qkv, probs = state
    early = start(exchange, send)
    h2 = stage([take_c], h2)
    h2 = tick([take_b, early], h2)
    (sib,) = early.result if paired else (send,)
    all_b = whole(take_b, chunk_b, split_b)
    g_own, g_send, g_sib, h2_pair, all_up, slope = climb(me, all_b, h2, sib, order)

    def give(chain, name, products, split):
        if paired:
            return Steps(chain(z, *outer(name, products, split)))
        grads = [dot_tn(uncut(one.value(), far.value()), two.value()) for one, two, far, _ in products]
        grad = jnp.concatenate(grads, axis=1)
        grad = lax.psum_scatter(grad, AXES, scatter_dimension=0, tiled=True)
        return grad, jnp.full((8, 128), jnp.sum(grad * grad))

    df_sib = jnp.concatenate([sib[2], sib[3]], axis=1)
    left_c = View(g_sib) if paired else View(g_send)
    give_c = give(
        scatter_pairs, "outer_c", [(View(g_own), View(df), left_c, View(df_sib))], split_c
    )
    slope = stage([give_c], slope)
    slope = tick([take_c], slope)
    slope = tick([take_c], slope)
    all_c = whole(take_c, chunk_c, split_c)
    du, all_down = descend(me, all_c, slope, df)
    dmiddle, da, dg2 = unclimb(all_up, du, picked, added, gate, back_rows, vec)
    new_rows, dlogit, dr = finish_mlp(
        all_down, g_own, g_send, picked, added, gate, back_rows
    )
    du, da, dmiddle, new_rows, dlogit = tick([give_c], (du, da, dmiddle, new_rows, dlogit))
    late_u = start(exchange, du)
    dqkv = unattend(all_out, da, qkv, probs)
    dqkv = tick([late_u], dqkv)
    (du_sib,) = late_u.result if paired else (du,)
    late_q = start(exchange, dqkv, da)
    views = [View(h2_pair, lead=place) for place in range(2)]
    if not paired:
        cols = h2.reshape(h2.shape[0], 4, 2, -1)
        views = [View(cols[:, :, core].reshape(h2.shape[0], -1)) for core in range(2)]
    give_b = give(
        scatter_pairs, "outer_b", [(views[0], View(du), views[1], View(du_sib))], split_b
    )
    dqkv = stage([give_b, give_c], dqkv)
    grad_rows, dg1 = finish_rows(all_qkv, dqkv, picked, back_rows, dmiddle, dlogit, vec)
    late_v = start(exchange, dg1, dg2, dr)
    dqkv = stage([late_v], dqkv)
    dqkv = tick([late_q, late_v], dqkv)
    dqkv_sib, da_sib = late_q.result if paired else (dqkv, da)
    products = [
        (View(own, lead=0), View(dqkv), View(sib, lead=0), View(dqkv_sib)),
        (View(own, lead=1), View(da), View(sib, lead=1), View(da_sib)),
    ]
    if paired:
        left, right = vector_columns(order, (dg1, dg2, dr), late_v.result)
        products.append(tuple(View(array, lead=part) for part in range(2) for array in (left, right)))
    give_a = give(scatter, "outer_a", products, split_a)
    grad_rows = stage([give_a], grad_rows)
    grad_rows = tick([give_b, give_c], grad_rows)
    grad_rows, new_rows = stage([give_b, give_c], (grad_rows, new_rows))
    mixed_rows = place(tok_blocks, new_rows)
    grad_rows, mixed_rows = tick([give_a], (grad_rows, mixed_rows))
    grad_rows = stage([give_a], grad_rows)
    grad_rows = tick([give_b, give_c], grad_rows)
    grad_rows = stage([give_b, give_c], grad_rows)
    input_grad = place(back_blocks, grad_rows)
    grad_rows = tick([give_a, give_c], input_grad)
    input_grad = stage([give_a], input_grad)
    input_grad = tick([give_b], input_grad)
    input_grad = tick([give_a, give_b], input_grad)
    if paired:
        give_a, give_b, give_c = give_a.result, give_b.result, give_c.result
        vec_grad = give_a[2]
        local_sq = give_a[1] + give_b[1] + give_c[1]
    else:
        rows = jnp.stack([dg1[0], dg2[0], dr[0]], axis=0)
        rows = lax.psum_scatter(rows, AXES, scatter_dimension=1, tiled=True)
        vec_grad = jnp.pad(rows, ((0, 5), (0, 128 - shard_width)))
        local_sq = give_a[1] + give_b[1] + give_c[1] + jnp.sum(rows * rows)
    squares = jnp.broadcast_to(local_sq[:1], (devices_all, 128))
    squares = lax.all_to_all(squares, AXES, 0, 0, tiled=True)
    params_all = 4 * model_width * model_width + 2 * model_width * ff_width + 3 * model_width
    selected_all = seq_count * top_count * devices_all
    clip_limit = limit_scale * math.sqrt(params_all * selected_all)
    norm, *news = update(
        squares,
        clip_limit,
        [
            View(give_a[0], qkv_width),
            View(give_a[0], model_width, qkv_width),
            View(give_b[0]),
            View(give_c[0]),
        ],
        [
            (w_qkv, m_qkv, v_qkv),
            (w_out, m_out, v_out),
            (w_up, m_up, v_up),
            (w_down, m_down, v_down),
        ],
        vec_grad,
        (m_vectors, v_vectors),
    )
    return (
        mixed_rows,
        input_grad,
        norm[0, 0],
        *news[0:12:3],
        *news[1:12:3],
        news[12],
        *news[2:12:3],
        news[13],
    )


def solution(mesh):
    placed = (
        P(("wide", "narrow"), None),
        P(("wide", "narrow"), None),
        P(("wide", "narrow"), None),
        P(("wide", "narrow"), None),
        P(("wide", "narrow"), None),
        P(("wide", "narrow"), None),
        P(("wide", "narrow"), None),
        P(("wide", "narrow"), None),
        P(None, ("wide", "narrow")),
        P(("wide", "narrow"), None),
        P(("wide", "narrow"), None),
        P(("wide", "narrow"), None),
        P(("wide", "narrow"), None),
        P(None, ("wide", "narrow")),
        P(("wide", "narrow"), None),
        P(("wide", "narrow"), None),
        P(("wide", "narrow"), None),
        P(("wide", "narrow"), None),
        P(None, ("wide", "narrow")),
    )
    paired = mesh.shape["wide"] == 8 and mesh.shape["narrow"] == 4
    return jax.shard_map(
        functools.partial(per_device, paired),
        mesh=mesh,
        in_specs=placed,
        out_specs=(
            P(("wide", "narrow"), None),
            P(("wide", "narrow"), None),
            P(),
            P(("wide", "narrow"), None),
            P(("wide", "narrow"), None),
            P(("wide", "narrow"), None),
            P(("wide", "narrow"), None),
            P(("wide", "narrow"), None),
            P(("wide", "narrow"), None),
            P(("wide", "narrow"), None),
            P(("wide", "narrow"), None),
            P(None, ("wide", "narrow")),
            P(("wide", "narrow"), None),
            P(("wide", "narrow"), None),
            P(("wide", "narrow"), None),
            P(("wide", "narrow"), None),
            P(None, ("wide", "narrow")),
        ),
        check_vma=False,
    )
```

```python
import functools
import math

import jax
import jax.numpy as jnp
from jax import lax
from jax.experimental import pallas as pl
from jax.experimental.pallas import tpu as pltpu
from jax.sharding import PartitionSpec as P

HEAD_DIM = 64


norm_eps = 1e-06
beta_one = 0.9
beta_two = 0.999
adam_eps = 1e-08
learn_rate = 0.03
decay_rate = 0.1
adam_step = 10
limit_scale = 0.01
masked_out = -1e30
AXES = ("wide", "narrow")


def moment_update(grad_part, first, second):
    first_new = beta_one * first + (1.0 - beta_one) * grad_part
    second_new = beta_two * second + (1.0 - beta_two) * grad_part * grad_part
    return (first_new, second_new)


def adam_update(master, grad_part, first, second):
    first_new, second_new = moment_update(grad_part, first, second)
    first_hat = first_new / (1.0 - beta_one**adam_step)
    second_hat = second_new / (1.0 - beta_two**adam_step)
    master_new = master - learn_rate * (
        first_hat / (jnp.sqrt(second_hat) + adam_eps) + decay_rate * master
    )
    return (master_new, first_new, second_new)


f32, bf16 = jnp.float32, jnp.bfloat16
PAIR = 2 * HEAD_DIM
head_scale = HEAD_DIM ** (-0.5)
KEEP_L = ((0, 0, 0), (0, 1, 0))
KEEP_R = ((0, 0, 1), (1, 0, 1))
FAR_L = ((1, 0, 0), (1, 1, 0))
FAR_R = ((0, 1, 1), (1, 1, 1))
GROUPS = (KEEP_L, KEEP_R, FAR_L, FAR_R)
PIECES = "aaaaaaaavv"


def kernel(body, name, outs, args, kinds, scratch=(), limit=24, loose=0):
    spaces = {"s": pltpu.SMEM, "v": pltpu.VMEM, "h": pltpu.VMEM, "a": pltpu.HBM}
    held = len(outs) - loose
    return pl.pallas_call(
        body,
        out_shape=[
            jax.ShapeDtypeStruct(*out) if place < held else pltpu.HBM(*out)
            for place, out in enumerate(outs)
        ],
        in_specs=[pl.BlockSpec(memory_space=spaces[kind]) for kind in kinds],
        out_specs=[
            pl.BlockSpec(memory_space=pltpu.VMEM if place < held else pltpu.HBM)
            for place in range(len(outs))
        ],
        scratch_shapes=list(scratch),
        compiler_params=pltpu.CompilerParams(vmem_limit_bytes=limit << 20),
        cost_estimate=pl.CostEstimate(flops=1, bytes_accessed=1, transcendentals=0),
        name=name,
    )(
        *(
            pltpu.with_memory_space_constraint(arg, pltpu.HBM) if kind in "ah" else arg
            for arg, kind in zip(args, kinds)
        )
    )


def each_block(pieces):
    for core in range(2):
        for group, flips in enumerate(GROUPS):
            for place, flip in enumerate(flips):
                if core == 0 and group < 2:
                    ref = pieces[2 * group + place]
                else:
                    ref = pieces[core * 4 + group + 2].at[place]
                yield flip[0] * 4 + flip[1] * 2 + core, flip[2], ref


def start_all(copies):
    for copy in copies:
        copy.start()


def wait_all(copies):
    for copy in copies:
        copy.wait()


def fetch(pieces, me, sem, base, left, right):
    copies = []
    for flip, half, block in each_block(pieces):
        rows = block.shape[0]
        start = pl.multiple_of((me ^ flip) * rows, rows)
        for target, column, out_column, width in (left, right)[half]:
            copies.append(
                pltpu.make_async_copy(
                    block.at[:, pl.ds(column, width)],
                    target.at[pl.ds(start, rows), pl.ds(out_column, width)],
                    sem.at[base + len(copies)],
                )
            )
    return copies


def dot_nt(left, right):
    return lax.dot_general(left, right, (((1,), (1,)), ((), ())), preferred_element_type=f32)


def dot_tn(left, right):
    return lax.dot_general(left, right, (((0,), (0,)), ((), ())), preferred_element_type=f32)


def dot_nn(left, right):
    return jnp.dot(left, right, preferred_element_type=f32)


def mean_last(array):
    return jnp.mean(array, axis=-1, keepdims=True)


def sum_rows(array):
    return jnp.sum(array, axis=0, keepdims=True)


def head_masks(dtype):
    lanes = lax.broadcasted_iota(jnp.int32, (1, PAIR), 1)
    first = (lanes < HEAD_DIM).astype(f32).astype(dtype)
    return first, (1 - first).astype(dtype)


def two_heads(pair, masks):
    return jnp.concatenate([pair * masks[0], pair * masks[1]], axis=0)


def one_pair(stacked, masks):
    rows = stacked.shape[0] // 2
    return stacked[:rows] * masks[0] + stacked[rows:] * masks[1]


def gather_input(w_qkv, w_out, vectors):
    rows, first = w_qkv.shape
    second = w_out.shape[1]

    def body(qkv_ref, out_ref, vec_ref, chunk_ref, turned):
        chunk_ref[:, :first] = qkv_ref[...].astype(bf16)
        chunk_ref[:, first : first + second] = out_ref[...].astype(bf16)
        turned[...] = jnp.zeros_like(turned)
        turned[:3] = vec_ref[...]
        same = lax.broadcasted_iota(jnp.int32, (rows, rows), 0) == lax.broadcasted_iota(
            jnp.int32, (rows, rows), 1
        )
        columns = dot_nt(same.astype(f32).astype(bf16), turned[...].astype(bf16))
        chunk_ref[:, first + second :] = columns.astype(bf16)

    outs = [((rows, first + second + 128), bf16)]
    scratch = [pltpu.VMEM((128, rows), f32)]
    return kernel(body, "gather_input", outs, (w_qkv, w_out, vectors), "hhh", scratch)[0]


def attend(me, pieces, picked, back_rows, seg_row, seg_col, order):
    rows, width = picked.shape
    seqs = seg_row.shape[0]
    top = rows // seqs
    pairs = width // PAIR
    first = pieces[0].shape[1]
    rest = 3 * width - first
    spare = pieces[2].shape[1] - rest - width

    def body(me_ref, *refs):
        blocks, refs = refs[:10], refs[10:]
        x_ref, dy_ref, seg_row_ref, seg_col_ref, order_ref = refs[:5]
        own_ref, send_ref, df_ref, gate_ref, vec_ref, add_ref, h2_ref = refs[5:12]
        all_ref, out_ref, qkv_out, prob_out = refs[12:16]
        w_qkv, w_out, w_vec, qkv_ref, prob_ref, att_ref, sem = refs[16:]
        vec_copies = fetch(blocks, me_ref[0], sem, 0, (), ((w_vec, rest + width, 0, spare),))
        left = fetch(blocks, me_ref[0], sem, 8, ((w_qkv, 0, 0, first),), ())
        right = fetch(blocks, me_ref[0], sem, 16, (), ((w_qkv, 0, first, rest),))
        out_copies = fetch(blocks, me_ref[0], sem, 24, (), ((w_out, rest, 0, width),))
        start_all(vec_copies + left + right + out_copies)
        wait_all(vec_copies)
        vec = w_vec[...].astype(f32).T[:8]
        vec_ref[...] = vec
        x = x_ref[...].astype(f32)
        h1 = (x * lax.rsqrt(mean_last(x * x) + norm_eps) * vec[0:1]).astype(bf16)
        for copies, start, count in ((left, 0, first), (right, first, rest)):
            wait_all(copies)
            for part in range(start, start + count, 384):
                lanes = pl.ds(part, 384)
                qkv_ref[:, lanes] = dot_nn(h1, w_qkv[:, lanes]).astype(bf16)
        stored = [
            pltpu.make_async_copy(w_qkv, all_ref, sem.at[32]),
            pltpu.make_async_copy(qkv_ref, qkv_out, sem.at[33]),
            pltpu.make_async_copy(w_out, out_ref, sem.at[34]),
        ]
        wait_all(out_copies)
        start_all(stored)
        masks, masks_f = head_masks(bf16), head_masks(f32)
        ordered_pairs = lax.broadcasted_iota(jnp.int32, (top, top), 1) <= lax.broadcasted_iota(
            jnp.int32, (top, top), 0
        )
        for seq in range(seqs):
            here = pl.ds(seq * top, top)
            seen = ordered_pairs & (seg_col_ref[seq] == seg_row_ref[seq])
            hidden = jnp.where(seen, 0.0, masked_out)
            hidden = jnp.concatenate([hidden, hidden], axis=0)
            for pair in range(pairs):
                q, k, v = (
                    qkv_ref[here, pl.ds(part * width + pair * PAIR, PAIR)] for part in range(3)
                )
                scores = dot_nt(two_heads(q, masks), k) * head_scale
                scores = jnp.where(hidden < 0.0, masked_out, scores)
                power = jnp.exp(scores - jnp.max(scores, axis=-1, keepdims=True))
                probs = power / jnp.sum(power, axis=-1, keepdims=True)
                prob_ref[seq * pairs + pair] = probs
                mixed = one_pair(dot_nn(probs.astype(bf16), v), masks_f)
                att_ref[here, pl.ds(pair * PAIR, PAIR)] = mixed.astype(bf16)
            group = pl.ds(seq * pairs, pairs)
            stored.append(
                pltpu.make_async_copy(prob_ref.at[group], prob_out.at[group], sem.at[35 + seq])
            )
            stored[-1].start()
        gate = jax.nn.sigmoid(jnp.sum(x * vec[2:3], axis=-1, keepdims=True))
        gate_ref[...] = jnp.broadcast_to(gate, gate_ref.shape)
        df = (gate * dy_ref[...].astype(f32)).astype(bf16)
        df_ref[...] = df
        added = dot_nn(att_ref[...], w_out[...])
        add_ref[...] = added
        middle = x + added
        h2 = (middle * lax.rsqrt(mean_last(middle * middle) + norm_eps) * vec[1:2]).astype(bf16)
        h2_ref[...] = h2
        for half in range(2):
            lanes = slice(half * (width // 2), (half + 1) * (width // 2))
            send_ref[2 + half] = df[:, lanes]
            send_ref[4 + half] = h2[:, lanes]
        chosen = one_hot_columns(order_ref)
        for place, array in enumerate((h1, att_ref[...])):
            parted = dot_nn(array, chosen).astype(bf16)
            own_ref[place] = parted[:, : width // 2]
            send_ref[place] = parted[:, width // 2 :]
        wait_all(stored)

    outs = [
        ((2, rows, width // 2), bf16),
        ((6, rows, width // 2), bf16),
        ((rows, width), bf16),
        ((rows, 128), f32),
        ((8, width), f32),
        ((rows, width), f32),
        ((rows, width), bf16),
        ((width, 3 * width), bf16),
        ((width, width), bf16),
        ((rows, 3 * width), bf16),
        ((seqs * pairs, 2 * top, top), f32),
    ]
    scratch = [
        pltpu.VMEM((width, 3 * width), bf16),
        pltpu.VMEM((width, width), bf16),
        pltpu.VMEM((width, spare), bf16),
        pltpu.VMEM((rows, 3 * width), bf16),
        pltpu.VMEM((seqs * pairs, 2 * top, top), f32),
        pltpu.VMEM((rows, width), bf16),
        pltpu.SemaphoreType.DMA((35 + seqs,)),
    ]
    args = (me, *pieces, picked, back_rows, seg_row, seg_col, order)
    return kernel(body, "attend", outs, args, "s" + PIECES + "vvvvv", scratch, 26, 4)


def one_hot_columns(order_ref):
    width = order_ref.shape[1]
    chosen = lax.broadcasted_iota(jnp.int32, (width, width), 0) == order_ref[...]
    return chosen.astype(f32).astype(bf16)


def climb(me, pieces, h2, sib, order):
    rows, width = h2.shape
    first = pieces[0].shape[1]
    block = 2 * first // 8

    def body(me_ref, *refs):
        blocks, refs = refs[:10], refs[10:]
        h2_ref, sib_ref, order_ref = refs[:3]
        own_ref, send_ref, far_ref, pair_ref, up_ref, slope_out = refs[3:9]
        w_up, slope_ref, both_ref, sem = refs[9:]
        copies = fetch(
            blocks, me_ref[0], sem, 0, ((w_up, 0, 0, first),), ((w_up, 0, first, first),)
        )
        start_all(copies)
        both_ref[:rows] = h2_ref[...]
        for half in range(2):
            lanes = pl.ds(half * (width // 2), width // 2)
            both_ref[rows:, lanes] = sib_ref[4 + half]
        chosen = one_hot_columns(order_ref)[:, : width // 2]
        parted = dot_nn(both_ref[...], chosen).astype(bf16)
        pair_ref[0] = parted[:rows]
        pair_ref[1] = parted[rows:]
        wait_all(copies)
        stored = [pltpu.make_async_copy(w_up, up_ref, sem.at[16])]
        start_all(stored)
        scale = math.sqrt(2.0 / math.pi)
        for flip in range(8):
            start = pl.multiple_of((me_ref[0] ^ flip) * block, block)
            place = flip // 2
            lanes = pl.ds(place * block, block)
            weights = w_up[:, pl.ds(start, block)]
            u = dot_nn(both_ref[:rows], weights)
            square = u * u
            bent = jnp.tanh(scale * (u + 0.044715 * (square * u)))
            half_up = 0.5 * (1.0 + bent)
            target = send_ref if flip % 2 else own_ref
            target[:, lanes] = (u * half_up).astype(bf16)
            where = (flip % 2) * 4 + place
            slope_ref[where] = half_up + (0.5 * u) * (1.0 - bent * bent) * (
                scale * (1.0 + (3.0 * 0.044715) * square)
            )
            stored.append(
                pltpu.make_async_copy(
                    slope_ref.at[where], slope_out.at[where], sem.at[17 + flip]
                )
            )
            stored[-1].start()
            if flip % 2 == 0:
                u = dot_nn(both_ref[rows:], weights)
                bent = jnp.tanh(scale * (u + 0.044715 * (u * u * u)))
                far_ref[:, lanes] = (0.5 * u * (1.0 + bent)).astype(bf16)
        wait_all(stored)

    outs = [
        ((rows, 4 * block), bf16),
        ((rows, 4 * block), bf16),
        ((rows, 4 * block), bf16),
        ((2, rows, width // 2), bf16),
        ((width, 8 * block), bf16),
        ((8, rows, block), f32),
    ]
    scratch = [
        pltpu.VMEM((width, 8 * block), bf16),
        pltpu.VMEM((8, rows, block), f32),
        pltpu.VMEM((2 * rows, width), bf16),
        pltpu.SemaphoreType.DMA((25,)),
    ]
    args = (me, *pieces, h2, sib, order)
    return kernel(body, "climb", outs, args, "s" + PIECES + "vvv", scratch, 26, 2)


def vector_columns(order, mine, other):
    width = order.shape[1]
    half = width // 2

    def body(order_ref, *refs):
        ins, (left, right, rows) = refs[:6], refs[6:]
        chosen = one_hot_columns(order_ref)[:, :half]
        rows[...] = jnp.zeros_like(rows)
        for place in range(3):
            rows[place : place + 1] = ins[place][0:1] + ins[3 + place][0:1]
        columns = rows[...].T.astype(bf16)
        for part in range(2):
            left[part] = chosen[part * half : (part + 1) * half]
            right[part] = columns[part * half : (part + 1) * half]

    outs = [((2, half, half), bf16), ((2, half, 128), bf16)]
    scratch = [pltpu.VMEM((128, width), f32)]
    args = (order, *mine, *other)
    return kernel(body, "vector_columns", outs, args, "v" * 7, scratch)


class View:
    def __init__(self, array, columns=None, first=0, lead=None):
        self.array, self.first, self.lead = array, first, lead
        self.columns = columns or array.shape[-1]

    def value(self):
        array = self.array if self.lead is None else self.array[self.lead]
        return array[:, self.first : self.first + self.columns]

    def read(self, ref, first, columns):
        lanes = pl.ds(self.first + first, columns)
        return ref[:, lanes] if self.lead is None else ref[self.lead, :, lanes]


def outer(name, products, split):
    length = products[0][0].columns // 4
    total = sum(product[1].columns for product in products)
    widths = (split, total - split)
    order = ((2, 3), (1, 3), (0, 1), (0, 2))

    def body(*refs):
        ins, outs = refs[: 4 * len(products)], refs[4 * len(products) :]
        base = 0
        for number, product in enumerate(products):
            reads = [
                functools.partial(view.read, ref)
                for view, ref in zip(product, ins[4 * number : 4 * number + 4])
            ]
            columns = product[1].columns
            step = min(768, columns)
            for start in range(0, columns, step):
                for first in range(0, 4 * length, 384):
                    value = dot_tn(reads[0](first, 384), reads[1](start, step))
                    value += dot_tn(reads[2](first, 384), reads[3](start, step))
                    for block in range(first // length, (first + 384) // length):
                        part = value[block * length - first : (block + 1) * length - first]
                        for half in range(2):
                            low = max(base + start, half * split)
                            high = min(base + start + step, split + half * (total - split))
                            if high <= low:
                                continue
                            piece = part[:, low - base - start : high - base - start]
                            out_lanes = pl.ds(low - half * split, high - low)
                            for out in (half, 2 + half):
                                if block in order[out]:
                                    outs[out][order[out].index(block), :, out_lanes] = piece.astype(
                                        outs[out].dtype
                                    )
            base += columns

    outs = [
        ((2, length, widths[out % 2]), bf16 if out < 2 else f32) for out in range(4)
    ]
    args = [view.array for product in products for view in product]
    return kernel(body, name, outs, args, "v" * len(args))


def descend(me, pieces, slope, df):
    rows, width = df.shape
    block = slope.shape[2]

    def body(me_ref, *refs):
        blocks, refs = refs[:10], refs[10:]
        slope_in, df_ref, du_ref, down_ref, w_down, slope_ref, sem = refs
        copies = [[] for _ in range(8)]
        for flip, side, part in each_block(blocks):
            lanes = pl.ds(side * (width // 2), width // 2)
            place = (flip % 2) * 4 + flip // 2
            target = w_down.at[pl.ds(place * block, block), lanes]
            copies[place].append(
                pltpu.make_async_copy(part, target, sem.at[place * 2 + side])
            )
        for place, pair in enumerate(copies):
            pair.append(
                pltpu.make_async_copy(
                    slope_in.at[place], slope_ref.at[place], sem.at[17 + place]
                )
            )
            start_all(pair)
        for place in range(8):
            wait_all(copies[place])
            flip = place % 4 * 2 + place // 4
            start = pl.multiple_of((me_ref[0] ^ flip) * block, block)
            dg = dot_nt(df_ref[...], w_down[pl.ds(place * block, block)])
            du_ref[:, pl.ds(start, block)] = (dg * slope_ref[place]).astype(bf16)
        stored = pltpu.make_async_copy(w_down, down_ref, sem.at[16])
        stored.start()
        stored.wait()

    outs = [((rows, 8 * block), bf16), ((8 * block, width), bf16)]
    scratch = [
        pltpu.VMEM((8 * block, width), bf16),
        pltpu.VMEM((8, rows, block), f32),
        pltpu.SemaphoreType.DMA((25,)),
    ]
    args = (me, *pieces, slope, df)
    return kernel(body, "descend", outs, args, "s" + PIECES + "av", scratch, 24, 1)


def unclimb(w_up, du, picked, added, gate, back_rows, vec):
    rows, width = picked.shape

    def body(up_ref, du_ref, x_ref, add_ref, gate_ref, dy_ref, vec_ref, dm_ref, da_ref, dg_ref):
        dh = dot_nt(du_ref[...], up_ref[...])
        middle = x_ref[...].astype(f32) + add_ref[...]
        inverse = lax.rsqrt(mean_last(middle * middle) + norm_eps)
        unit = middle * inverse
        dg_ref[...] = jnp.broadcast_to(sum_rows(dh * unit), dg_ref.shape)
        scaled = dh * vec_ref[1:2]
        dm = inverse * (scaled - unit * mean_last(scaled * unit))
        dm_ref[...] = dm
        da_ref[...] = (gate_ref[:, 0:1] * dy_ref[...].astype(f32) + dm).astype(bf16)

    outs = [((rows, width), f32), ((rows, width), bf16), ((8, width), f32)]
    args = (w_up, du, picked, added, gate, back_rows, vec)
    return kernel(body, "unclimb", outs, args, "v" * 7)


def unattend(w_out, da, qkv, probs):
    rows, width = da.shape
    top = probs.shape[2]
    seqs, pairs = rows // top, width // PAIR

    def body(out_ref, da_ref, qkv_ref, prob_ref, dqkv_ref, do_ref):
        do_ref[...] = dot_nt(da_ref[...], out_ref[...]).astype(bf16)
        masks, masks_f = head_masks(bf16), head_masks(f32)
        for seq in range(seqs):
            here = pl.ds(seq * top, top)
            for pair in range(pairs):
                lanes = [pl.ds(part * width + pair * PAIR, PAIR) for part in range(3)]
                q, k, v = (qkv_ref[here, part] for part in lanes)
                do = two_heads(do_ref[here, pl.ds(pair * PAIR, PAIR)], masks)
                probs = prob_ref[seq * pairs + pair]
                dprobs = dot_nt(do, v)
                dscores = probs * (dprobs - jnp.sum(dprobs * probs, axis=-1, keepdims=True))
                dscores = dscores.astype(bf16)
                dq = one_pair(dot_nn(dscores, k), masks_f) * head_scale
                dk = dot_tn(dscores, two_heads(q, masks)) * head_scale
                dv = dot_tn(probs.astype(bf16), do)
                for part, value in zip(lanes, (dq, dk, dv)):
                    dqkv_ref[here, part] = value.astype(bf16)

    scratch = [pltpu.VMEM((rows, width), bf16)]
    outs = [((rows, 3 * width), bf16)]
    return kernel(body, "unattend", outs, (w_out, da, qkv, probs), "vvvv", scratch)[0]


def finish_mlp(w_down, own, send, picked, added, gate, back_rows):
    rows, width = picked.shape
    half = w_down.shape[0] // 2

    def body(down_ref, own_ref, send_ref, x_ref, add_ref, gate_ref, dy_ref, *outs):
        new_ref, dlogit_ref, dr_ref = outs
        out = dot_nn(own_ref[:, :half], down_ref[:half])
        out += dot_nn(send_ref[:, :half], down_ref[half:])
        both = add_ref[...] + out
        x = x_ref[...].astype(f32)
        gate = gate_ref[:, 0:1]
        new_ref[...] = (x + gate * both).astype(bf16)
        dlogit = jnp.sum(dy_ref[...].astype(f32) * both, axis=-1, keepdims=True)
        dlogit = dlogit * gate * (1.0 - gate)
        dlogit_ref[...] = jnp.broadcast_to(dlogit, dlogit_ref.shape)
        dr_ref[...] = jnp.broadcast_to(sum_rows(dlogit * x), dr_ref.shape)

    outs = [((rows, width), bf16), ((rows, 128), f32), ((8, width), f32)]
    args = (w_down, own, send, picked, added, gate, back_rows)
    return kernel(body, "finish_mlp", outs, args, "v" * 7)


def finish_rows(w_qkv, dqkv, picked, back_rows, dmiddle, dlogit, vec):
    rows, width = picked.shape

    def body(all_ref, dqkv_ref, x_ref, dy_ref, dm_ref, dlogit_ref, vec_ref, grad_ref, dg_ref):
        dh = dot_nt(dqkv_ref[...], all_ref[...])
        x = x_ref[...].astype(f32)
        inverse = lax.rsqrt(mean_last(x * x) + norm_eps)
        unit = x * inverse
        dg_ref[...] = jnp.broadcast_to(sum_rows(dh * unit), dg_ref.shape)
        scaled = dh * vec_ref[0:1]
        dx = inverse * (scaled - unit * mean_last(scaled * unit))
        grad = dy_ref[...].astype(f32) + dm_ref[...] + dx + dlogit_ref[:, 0:1] * vec_ref[2:3]
        grad_ref[...] = grad.astype(bf16)

    outs = [((rows, width), bf16), ((8, width), f32)]
    args = (w_qkv, dqkv, picked, back_rows, dmiddle, dlogit, vec)
    return kernel(body, "finish_rows", outs, args, "v" * 7)


def stack_all(*groups):
    counts = [len(group) for group in groups]

    def body(*refs):
        ins, outs = refs[: sum(counts)], refs[sum(counts) :]
        for out, count in zip(outs, counts):
            for place in range(count):
                out[place] = ins[place][...]
            ins = ins[count:]

    outs = [((len(group), *group[0].shape), group[0].dtype) for group in groups]
    args = [array for group in groups for array in group]
    return kernel(body, "stack_all", outs, args, "v" * len(args))


def pick_flip(refs, flip):
    if flip == 0 or len(refs) == 4:
        return refs[flip]
    return refs[1] if flip == 2 else refs[2].at[flip // 2]


def join_z(z, own, others, split):
    rows, width = own.shape
    count = 1 + len(others)

    def body(z_ref, *refs):
        ins, (left_ref, right_ref, total) = refs[:count], refs[count:]
        for flip in range(4):
            start = pl.multiple_of((z_ref[0] ^ flip) * rows, rows)
            total[pl.ds(start, rows)] = pick_flip(ins, flip)[...].astype(f32)
        left_ref[...] = total[:, :split].astype(bf16)
        right_ref[...] = total[:, split:].astype(bf16)

    outs = [((4 * rows, split), bf16), ((4 * rows, width - split), bf16)]
    scratch = [pltpu.VMEM((4 * rows, width), f32)]
    return kernel(body, "join_z", outs, (z, own, *others), "s" + "v" * count, scratch)


def join_z_pairs(z, mine, others):
    _, rows, width = mine.shape

    def body(z_ref, *refs):
        ins, outs = refs[:3], refs[3:]
        for flip in range(4):
            start = pl.ds(pl.multiple_of((z_ref[0] ^ flip) * rows, rows), rows)
            block = pick_flip(ins, flip)
            for place in range(4):
                outs[place][start] = block[place]

    outs = [((4 * rows, width), bf16)] * 4
    return kernel(body, "join_z_pairs", outs, (z, mine, *others), "svvv")


def add_z_pairs(z, keep_l, keep_r, other_l, other_r):
    pair, rows, width = keep_l.shape
    part = rows // 4

    def body(z_ref, keep_l, keep_r, other_l, other_r, mine, send, total):
        for half, (keep, other) in enumerate(((keep_l, other_l), (keep_r, other_r))):
            for place in range(pair):
                total[half * pair + place] = keep[place] + other[place].astype(f32)
        for flip in range(4):
            start = pl.multiple_of((z_ref[0] ^ flip) * part, part)
            out = (mine, send)[flip % 2]
            out[flip // 2] = total[:, pl.ds(start, part)].astype(out.dtype)

    outs = [((2, 4, part, width), f32), ((2, 4, part, width), bf16)]
    scratch = [pltpu.VMEM((4, rows, width), f32)]
    args = (z, keep_l, keep_r, other_l, other_r)
    return kernel(body, "add_z_pairs", outs, args, "svvvv", scratch)


def add_four(mine, other):
    def body(mine, other, send_l, send_r, keep):
        def total(place):
            return mine[place] + other[place].astype(f32)

        width = mine.shape[2]
        keep[:, :width] = total(0)
        keep[:, width:] = total(2)
        send_l[...] = total(1).astype(bf16)
        send_r[...] = total(3).astype(bf16)

    _, rows, width = mine.shape
    outs = [((rows, width), bf16)] * 2 + [((rows, 2 * width), f32)]
    return kernel(body, "add_four", outs, (mine, other), "vv")


def add_pairs(keep_l, keep_r, other_l, other_r):
    def body(keep_l, keep_r, other_l, other_r, send_l, send_r, left, right):
        for keep, other, send, mine in (
            (keep_l, other_l, send_l, left),
            (keep_r, other_r, send_r, right),
        ):
            send[...] = (keep[1] + other[1].astype(f32)).astype(bf16)
            mine[...] = keep[0] + other[0].astype(f32)

    shapes = [keep_l.shape[1:], keep_r.shape[1:]]
    outs = [(shape, kind) for kind in (bf16, f32) for shape in shapes]
    return kernel(body, "add_pairs", outs, (keep_l, keep_r, other_l, other_r), "vvvv")


def add_split(z, keep_l, keep_r, other_l, other_r):
    rows, split = keep_l.shape
    width = split + keep_r.shape[1]
    part = rows // 4

    def body(z_ref, keep_l, keep_r, other_l, other_r, mine, send, total):
        total[:, :split] = keep_l[...] + other_l[...].astype(f32)
        total[:, split:] = keep_r[...] + other_r[...].astype(f32)
        for flip in range(4):
            start = pl.multiple_of((z_ref[0] ^ flip) * part, part)
            out = (mine, send)[flip % 2]
            out[flip // 2] = total[pl.ds(start, part)].astype(out.dtype)

    outs = [((2, part, width), f32), ((2, part, width), bf16)]
    scratch = [pltpu.VMEM((rows, width), f32)]
    args = (z, keep_l, keep_r, other_l, other_r)
    return kernel(body, "add_split", outs, args, "svvvv", scratch)


def add_next(keep, other):
    def body(keep, other, mine, send):
        mine[...] = keep[0] + other[0].astype(f32)
        send[...] = (keep[1] + other[1].astype(f32)).astype(bf16)

    shape = keep.shape[1:]
    return kernel(body, "add_next", [(shape, f32), (shape, bf16)], (keep, other), "vv")


def settle_halves(keep, other_l, other_r):
    def body(keep, other_l, other_r, grad, square):
        width = other_l.shape[1]
        total = None
        for half, other in enumerate((other_l, other_r)):
            lanes = pl.ds(half * width, width)
            value = keep[:, lanes] + other[...].astype(f32)
            grad[:, lanes] = value
            part = jnp.sum(value * value)
            total = part if total is None else total + part
        square[...] = jnp.full(square.shape, total)

    outs = [(keep.shape, f32), ((8, 128), f32)]
    return kernel(body, "settle_halves", outs, (keep, other_l, other_r), "vvv")


def settle_z(mine, other, squares, devices):
    rows, width = mine.shape

    def body(mine, other, *refs):
        more, (grad, square, last, turned) = refs[: len(squares)], refs[len(squares) :]
        value = mine[...] + other[...].astype(f32)
        grad[...] = value
        total = jnp.sum(value * value)
        for ref in more:
            total = total + ref[0:1, :]
        square[...] = jnp.broadcast_to(total, square.shape)
        turned[...] = jnp.zeros_like(turned)
        turned[:rows] = value[:, width - 128 :]
        last[...] = turned[...].T[:8]

    outs = [(mine.shape, f32), ((devices, 128), f32), ((8, 128), f32)]
    scratch = [pltpu.VMEM((128, 128), f32)]
    args = (mine, other, *squares)
    return kernel(body, "settle_z", outs, args, "v" * len(args), scratch)


def update(squares, limit, grads, states, vec_grad, vec_states):
    count = len(grads)

    def body(square_ref, *refs):
        grad_refs, refs = refs[:count], refs[count:]
        state_refs, refs = refs[: 3 * count], refs[3 * count :]
        vec_ref, vec_m, vec_v, norm_ref, out_refs = *refs[:4], refs[4:]
        norm = jnp.sqrt(jnp.sum(square_ref[...], axis=0, keepdims=True)[:, 0:1])
        norm_ref[...] = norm
        factor = jnp.minimum(1.0, limit / (norm + 1e-06))
        for place in range(count):
            w, m, v = (ref[...] for ref in state_refs[3 * place : 3 * place + 3])
            grad = grads[place].read(grad_refs[place], 0, grads[place].columns) * factor
            for ref, value in zip(out_refs[3 * place :], adam_update(w, grad, m, v)):
                ref[...] = value
        grad = vec_ref[:3, : vec_m.shape[1]] * factor
        first, second = moment_update(grad, vec_m[...], vec_v[...])
        out_refs[-2][...] = first
        out_refs[-1][...] = second

    flat = [array for state in states for array in state]
    outs = [((1, 1), f32)] + [(array.shape, f32) for array in (*flat, *vec_states)]
    args = (squares, *(grad.array for grad in grads), *flat, vec_grad, *vec_states)
    return kernel(body, "update", outs, args, "v" * len(args), (), 32)


class Steps:
    def __init__(self, chain):
        self.chain = chain
        self.result = None
        self.launch(next(chain))

    def launch(self, step):
        self.flips = [flip for _, flip in step]
        self.given = [array for array, _ in step]

    def advance(self, arrays):
        try:
            self.launch(self.chain.send(arrays))
        except StopIteration as stop:
            self.flips, self.given, self.result = (), (), stop.value


def slot(chains, value):
    arrays = [
        [swap(array, flip) for array, flip in zip(chain.given, chain.flips)] for chain in chains
    ]
    arrays, value = lax.optimization_barrier((arrays, value))
    for chain, array in zip(chains, arrays):
        chain.advance(array)
    return value


def ready(chains, value):
    arrays, value = lax.optimization_barrier(([chain.given for chain in chains], value))
    for chain, array in zip(chains, arrays):
        chain.given = array
    return value


def swap(array, bit):
    count = lax.axis_size("wide") * lax.axis_size("narrow")
    return lax.ppermute(array, AXES, [(i, i ^ bit) for i in range(count)])


def exchange(*arrays):
    return (yield [(array, 4) for array in arrays])


def around_z(shard, at_once):
    if at_once:
        return (yield [(shard, flip) for flip in (1, 2, 3)])
    (two,) = yield [(shard, 2)]
    (both,) = yield [(stack_all((shard, two))[0], 1)]
    return two, both


def gather(shard, z, split, at_once):
    others = yield from around_z(shard, at_once)
    left, right = join_z(z, shard, others, split)
    near_l, near_r = yield [(left, 8), (right, 16)]
    return (yield from spread(left, near_l, right, near_r))


def gather_pairs(shard, z):
    half = shard.shape[1] // 2
    left, right = shard[:, :half], shard[:, half:]
    near_l, near_r = yield [(left, 8), (right, 16)]
    mine = jnp.stack([left, near_l, right, near_r])
    others = yield from around_z(mine, False)
    return (yield from spread(*join_z_pairs(z, mine, others)))


def spread(left, near_l, right, near_r):
    keep_l, keep_r = stack_all((left, near_l), (right, near_r))
    far_l, far_r, *near = yield [(keep_l, 16), (keep_r, 8), (keep_l, 4), (keep_r, 4)]
    far = yield [(far_l, 4), (far_r, 4)]
    return (left, near_l, right, near_r, far_l, far_r, *near, *far)


def scatter(z, send_l, send_r, keep_l, keep_r):
    other_l, other_r = yield [(send_l, 16), (send_r, 8)]
    send_l, send_r, left, right = add_pairs(keep_l, keep_r, other_l, other_r)
    other_l, other_r = yield [(send_l, 8), (send_r, 16)]
    mine, send = add_split(z, left, right, other_l, other_r)
    (other,) = yield [(send, 1)]
    mine, send = add_next(mine, other)
    (other,) = yield [(send, 2)]
    return mine, other


def scatter_pairs(z, send_l, send_r, keep_l, keep_r):
    other_l, other_r = yield [(send_l, 16), (send_r, 8)]
    mine, send = add_z_pairs(z, keep_l, keep_r, other_l, other_r)
    (other,) = yield [(send, 1)]
    mine, send = add_next(mine, other)
    (other,) = yield [(send, 2)]
    send_l, send_r, keep = add_four(mine, other)
    other_l, other_r = yield [(send_l, 8), (send_r, 16)]
    return settle_halves(keep, other_l, other_r)


def cut(whole, split):
    blocks = whole.reshape(8, whole.shape[0] // 8, whole.shape[1])
    sides = (blocks[..., :split], blocks[..., split:])
    groups = [
        [sides[flip[2]][flip[0] * 4 + flip[1] * 2 + core] for flip in flips]
        for core in range(2)
        for flips in GROUPS
    ]
    return (*groups[0], *groups[1], *(jnp.stack(group) for group in groups[2:]))


def uncut(own, send):
    parts = jnp.stack([array.reshape(array.shape[0], 4, -1) for array in (own, send)], axis=2)
    return parts.reshape(own.shape[0], -1)


def per_device(
    paired,
    tokens,
    cotangent,
    segments,
    picks,
    w_qkv,
    w_out,
    w_up,
    w_down,
    vectors,
    m_qkv,
    m_out,
    m_up,
    m_down,
    m_vectors,
    v_qkv,
    v_out,
    v_up,
    v_down,
    v_vectors,
):
    devices_all = lax.axis_size("wide") * lax.axis_size("narrow")
    lane = lax.axis_index(AXES)
    seq_count, top_count = picks.shape
    seq_len = segments.shape[1]
    model_width = tokens.shape[1]
    qkv_width = w_qkv.shape[1]
    ff_width = w_up.shape[1]
    shard_width = vectors.shape[1]
    split_a, split_b, split_c = 2 * model_width, ff_width // 2, model_width // 2
    z = (lane & 3).reshape(1)
    me = (lane >> 2).reshape(1) if paired else jnp.zeros((1,), jnp.int32)

    chunk_a = gather_input(w_qkv, w_out, vectors)
    chunk_b = w_up.astype(bf16)
    chunk_c = w_down.astype(bf16)

    def start(chain, *args):
        return Steps(chain(*args)) if paired else None

    def tick(chains, value):
        return slot(chains, value) if paired else value

    def stage(chains, value):
        return ready(chains, value) if paired else value

    def whole(take, chunk, split):
        if paired:
            return take.result
        return cut(lax.all_gather(chunk, AXES, axis=0, tiled=True), split)

    hot = picks[:, :, None] == jnp.arange(seq_len, dtype=jnp.int32)[None, None, :]
    hot_low = hot.astype(bf16)
    tok_blocks = tokens.reshape(seq_count, seq_len, model_width)
    back_blocks = cotangent.reshape(seq_count, seq_len, model_width)

    def pick(blocks):
        rows = jnp.einsum("skl,sld->skd", hot_low, blocks, preferred_element_type=f32)
        return rows.astype(bf16).reshape(-1, model_width)

    def place(blocks, rows):
        rows = rows.reshape(seq_count, top_count, model_width)
        spread = jnp.einsum("skl,skd->sld", hot_low, rows, preferred_element_type=f32).astype(bf16)
        taken = jnp.any(hot, axis=1)
        return jnp.where(taken[:, :, None], spread, blocks).reshape(-1, model_width)

    take_a = start(gather, chunk_a, z, split_a, True)
    take_c = start(gather_pairs, chunk_c, z)
    picked = pick(tok_blocks)
    back_rows = pick(back_blocks)
    seg_sel = jnp.sum(jnp.where(hot, segments[:, None, :], 0), axis=-1)
    seg_row, seg_col = seg_sel[:, None, :], seg_sel[:, :, None]
    spot = jnp.arange(model_width, dtype=jnp.int32)
    half, eighth = model_width // 2, model_width // 8
    flip = spot % half // eighth * 2 + spot // half
    order = ((me[0] ^ flip) * eighth + spot % eighth)[None]
    inputs = (picked, back_rows, seg_row, seg_col, order, chunk_b)
    inputs = tick([take_a, take_c], inputs)
    take_b = start(gather, inputs[-1], z, split_b, False)
    inputs = tick([take_a], inputs[:-1])
    inputs = tick([take_b], inputs)
    inputs = tick([take_b, take_c], inputs)
    inputs = tick([take_a, take_b], inputs)
    inputs = tick([take_a], inputs)

    all_a = whole(take_a, chunk_a, split_a)
    picked, back_rows = inputs[:2]
    order = inputs[4]
    state = attend(me, all_a, *inputs)
    state = tick([take_b, take_c], state)
    own, send, df, gate, vec, added, h2, all_qkv, all_out, qkv, probs = state
    early = start(exchange, send)
    h2 = stage([take_c], h2)
    h2 = tick([take_b, early], h2)
    (sib,) = early.result if paired else (send,)
    all_b = whole(take_b, chunk_b, split_b)
    g_own, g_send, g_sib, h2_pair, all_up, slope = climb(me, all_b, h2, sib, order)

    def give(chain, name, products, split):
        if paired:
            return Steps(chain(z, *outer(name, products, split)))
        grads = [dot_tn(uncut(one.value(), far.value()), two.value()) for one, two, far, _ in products]
        grad = jnp.concatenate(grads, axis=1)
        grad = lax.psum_scatter(grad, AXES, scatter_dimension=0, tiled=True)
        return grad, jnp.full((8, 128), jnp.sum(grad * grad))

    df_sib = jnp.concatenate([sib[2], sib[3]], axis=1)
    left_c = View(g_sib) if paired else View(g_send)
    give_c = give(
        scatter_pairs, "outer_c", [(View(g_own), View(df), left_c, View(df_sib))], split_c
    )
    slope = stage([give_c], slope)
    slope = tick([take_c], slope)
    slope = tick([take_c], slope)
    all_c = whole(take_c, chunk_c, split_c)
    du, all_down = descend(me, all_c, slope, df)
    dmiddle, da, dg2 = unclimb(all_up, du, picked, added, gate, back_rows, vec)
    new_rows, dlogit, dr = finish_mlp(
        all_down, g_own, g_send, picked, added, gate, back_rows
    )
    du, da, dmiddle, new_rows, dlogit = tick([give_c], (du, da, dmiddle, new_rows, dlogit))
    late_u = start(exchange, du)
    dqkv = unattend(all_out, da, qkv, probs)
    dqkv = tick([late_u], dqkv)
    (du_sib,) = late_u.result if paired else (du,)
    late_q = start(exchange, dqkv, da)
    views = [View(h2_pair, lead=place) for place in range(2)]
    if not paired:
        cols = h2.reshape(h2.shape[0], 4, 2, -1)
        views = [View(cols[:, :, core].reshape(h2.shape[0], -1)) for core in range(2)]
    give_b = give(
        scatter_pairs, "outer_b", [(views[0], View(du), views[1], View(du_sib))], split_b
    )
    dqkv = stage([give_b, give_c], dqkv)
    grad_rows, dg1 = finish_rows(all_qkv, dqkv, picked, back_rows, dmiddle, dlogit, vec)
    late_v = start(exchange, dg1, dg2, dr)
    dqkv = stage([late_v], dqkv)
    dqkv = tick([late_q, late_v], dqkv)
    dqkv_sib, da_sib = late_q.result if paired else (dqkv, da)
    products = [
        (View(own, lead=0), View(dqkv), View(sib, lead=0), View(dqkv_sib)),
        (View(own, lead=1), View(da), View(sib, lead=1), View(da_sib)),
    ]
    if paired:
        left, right = vector_columns(order, (dg1, dg2, dr), late_v.result)
        products.append(tuple(View(array, lead=part) for part in range(2) for array in (left, right)))
    give_a = give(scatter, "outer_a", products, split_a)
    grad_rows = stage([give_a], grad_rows)
    grad_rows = tick([give_b, give_c], grad_rows)
    grad_rows, new_rows = stage([give_b, give_c], (grad_rows, new_rows))
    mixed_rows = place(tok_blocks, new_rows)
    grad_rows, mixed_rows = tick([give_a], (grad_rows, mixed_rows))
    grad_rows = stage([give_a], grad_rows)
    grad_rows = tick([give_b, give_c], grad_rows)
    grad_rows = stage([give_b, give_c], grad_rows)
    grad_rows = tick([give_a, give_c], grad_rows)
    grad_rows = stage([give_a], grad_rows)
    input_grad = place(back_blocks, grad_rows)
    input_grad = tick([give_a, give_b], input_grad)
    input_grad = stage([give_a, give_b], input_grad)
    input_grad = tick([give_a, give_b], input_grad)
    if paired:
        (grad_b, square_b), (grad_c, square_c) = give_b.result, give_c.result
        grad_a, squares, vec_grad = settle_z(*give_a.result, (square_b, square_c), devices_all)
    else:
        rows = jnp.stack([dg1[0], dg2[0], dr[0]], axis=0)
        rows = lax.psum_scatter(rows, AXES, scatter_dimension=1, tiled=True)
        vec_grad = jnp.pad(rows, ((0, 5), (0, 128 - shard_width)))
        (grad_a, square_a), (grad_b, square_b), (grad_c, square_c) = give_a, give_b, give_c
        local_sq = square_a + square_b + square_c + jnp.sum(rows * rows)
        squares = jnp.broadcast_to(local_sq[:1], (devices_all, 128))
    squares = lax.all_to_all(squares, AXES, 0, 0, tiled=True)
    params_all = 4 * model_width * model_width + 2 * model_width * ff_width + 3 * model_width
    selected_all = seq_count * top_count * devices_all
    clip_limit = limit_scale * math.sqrt(params_all * selected_all)
    norm, *news = update(
        squares,
        clip_limit,
        [
            View(grad_a, qkv_width),
            View(grad_a, model_width, qkv_width),
            View(grad_b),
            View(grad_c),
        ],
        [
            (w_qkv, m_qkv, v_qkv),
            (w_out, m_out, v_out),
            (w_up, m_up, v_up),
            (w_down, m_down, v_down),
        ],
        vec_grad,
        (m_vectors, v_vectors),
    )
    return (
        mixed_rows,
        input_grad,
        norm[0, 0],
        *news[0:12:3],
        *news[1:12:3],
        news[12],
        *news[2:12:3],
        news[13],
    )


def solution(mesh):
    placed = (
        P(("wide", "narrow"), None),
        P(("wide", "narrow"), None),
        P(("wide", "narrow"), None),
        P(("wide", "narrow"), None),
        P(("wide", "narrow"), None),
        P(("wide", "narrow"), None),
        P(("wide", "narrow"), None),
        P(("wide", "narrow"), None),
        P(None, ("wide", "narrow")),
        P(("wide", "narrow"), None),
        P(("wide", "narrow"), None),
        P(("wide", "narrow"), None),
        P(("wide", "narrow"), None),
        P(None, ("wide", "narrow")),
        P(("wide", "narrow"), None),
        P(("wide", "narrow"), None),
        P(("wide", "narrow"), None),
        P(("wide", "narrow"), None),
        P(None, ("wide", "narrow")),
    )
    paired = mesh.shape["wide"] == 8 and mesh.shape["narrow"] == 4
    return jax.shard_map(
        functools.partial(per_device, paired),
        mesh=mesh,
        in_specs=placed,
        out_specs=(
            P(("wide", "narrow"), None),
            P(("wide", "narrow"), None),
            P(),
            P(("wide", "narrow"), None),
            P(("wide", "narrow"), None),
            P(("wide", "narrow"), None),
            P(("wide", "narrow"), None),
            P(("wide", "narrow"), None),
            P(("wide", "narrow"), None),
            P(("wide", "narrow"), None),
            P(("wide", "narrow"), None),
            P(None, ("wide", "narrow")),
            P(("wide", "narrow"), None),
            P(("wide", "narrow"), None),
            P(("wide", "narrow"), None),
            P(("wide", "narrow"), None),
            P(None, ("wide", "narrow")),
        ),
        check_vma=False,
    )
```

```python
import functools
import math

import jax
import jax.numpy as jnp
from jax import lax
from jax.experimental import pallas as pl
from jax.experimental.pallas import tpu as pltpu
from jax.sharding import PartitionSpec as P

HEAD_DIM = 64


norm_eps = 1e-06
beta_one = 0.9
beta_two = 0.999
adam_eps = 1e-08
learn_rate = 0.03
decay_rate = 0.1
adam_step = 10
limit_scale = 0.01
masked_out = -1e30
AXES = ("wide", "narrow")


def moment_update(grad_part, first, second):
    first_new = beta_one * first + (1.0 - beta_one) * grad_part
    second_new = beta_two * second + (1.0 - beta_two) * grad_part * grad_part
    return (first_new, second_new)


def adam_update(master, grad_part, first, second):
    first_new, second_new = moment_update(grad_part, first, second)
    first_hat = first_new / (1.0 - beta_one**adam_step)
    second_hat = second_new / (1.0 - beta_two**adam_step)
    master_new = master - learn_rate * (
        first_hat / (jnp.sqrt(second_hat) + adam_eps) + decay_rate * master
    )
    return (master_new, first_new, second_new)


f32, bf16 = jnp.float32, jnp.bfloat16
PAIR = 2 * HEAD_DIM
head_scale = HEAD_DIM ** (-0.5)
KEEP_L = ((0, 0, 0), (0, 1, 0))
KEEP_R = ((0, 0, 1), (1, 0, 1))
FAR_L = ((1, 0, 0), (1, 1, 0))
FAR_R = ((0, 1, 1), (1, 1, 1))
GROUPS = (KEEP_L, KEEP_R, FAR_L, FAR_R)
PIECES = "aaaaaaaavv"


def kernel(body, name, outs, args, kinds, scratch=(), limit=24, loose=0):
    spaces = {"s": pltpu.SMEM, "v": pltpu.VMEM, "h": pltpu.VMEM, "a": pltpu.HBM}
    held = len(outs) - loose
    return pl.pallas_call(
        body,
        out_shape=[
            jax.ShapeDtypeStruct(*out) if place < held else pltpu.HBM(*out)
            for place, out in enumerate(outs)
        ],
        in_specs=[pl.BlockSpec(memory_space=spaces[kind]) for kind in kinds],
        out_specs=[
            pl.BlockSpec(memory_space=pltpu.VMEM if place < held else pltpu.HBM)
            for place in range(len(outs))
        ],
        scratch_shapes=list(scratch),
        compiler_params=pltpu.CompilerParams(vmem_limit_bytes=limit << 20),
        cost_estimate=pl.CostEstimate(flops=1, bytes_accessed=1, transcendentals=0),
        name=name,
    )(
        *(
            pltpu.with_memory_space_constraint(arg, pltpu.HBM) if kind in "ah" else arg
            for arg, kind in zip(args, kinds)
        )
    )


def each_block(pieces):
    for core in range(2):
        for group, flips in enumerate(GROUPS):
            for place, flip in enumerate(flips):
                if core == 0 and group < 2:
                    ref = pieces[2 * group + place]
                else:
                    ref = pieces[core * 4 + group + 2].at[place]
                yield flip[0] * 4 + flip[1] * 2 + core, flip[2], ref


def start_all(copies):
    for copy in copies:
        copy.start()


def wait_all(copies):
    for copy in copies:
        copy.wait()


def fetch(pieces, me, sem, base, left, right):
    copies = []
    for flip, half, block in each_block(pieces):
        rows = block.shape[0]
        start = pl.multiple_of((me ^ flip) * rows, rows)
        for target, column, out_column, width in (left, right)[half]:
            copies.append(
                pltpu.make_async_copy(
                    block.at[:, pl.ds(column, width)],
                    target.at[pl.ds(start, rows), pl.ds(out_column, width)],
                    sem.at[base + len(copies)],
                )
            )
    return copies


def dot_nt(left, right):
    return lax.dot_general(left, right, (((1,), (1,)), ((), ())), preferred_element_type=f32)


def dot_tn(left, right):
    return lax.dot_general(left, right, (((0,), (0,)), ((), ())), preferred_element_type=f32)


def dot_nn(left, right):
    return jnp.dot(left, right, preferred_element_type=f32)


def mean_last(array):
    return jnp.mean(array, axis=-1, keepdims=True)


def sum_rows(array):
    return jnp.sum(array, axis=0, keepdims=True)


def head_masks(dtype):
    lanes = lax.broadcasted_iota(jnp.int32, (1, PAIR), 1)
    first = (lanes < HEAD_DIM).astype(f32).astype(dtype)
    return first, (1 - first).astype(dtype)


def two_heads(pair, masks):
    return jnp.concatenate([pair * masks[0], pair * masks[1]], axis=0)


def one_pair(stacked, masks):
    rows = stacked.shape[0] // 2
    return stacked[:rows] * masks[0] + stacked[rows:] * masks[1]


def gather_input(w_qkv, w_out, vectors):
    rows, first = w_qkv.shape
    second = w_out.shape[1]

    def body(qkv_ref, out_ref, vec_ref, chunk_ref, turned):
        chunk_ref[:, :first] = qkv_ref[...].astype(bf16)
        chunk_ref[:, first : first + second] = out_ref[...].astype(bf16)
        turned[...] = jnp.zeros_like(turned)
        turned[:3] = vec_ref[...]
        same = lax.broadcasted_iota(jnp.int32, (rows, rows), 0) == lax.broadcasted_iota(
            jnp.int32, (rows, rows), 1
        )
        columns = dot_nt(same.astype(f32).astype(bf16), turned[...].astype(bf16))
        chunk_ref[:, first + second :] = columns.astype(bf16)

    outs = [((rows, first + second + 128), bf16)]
    scratch = [pltpu.VMEM((128, rows), f32)]
    return kernel(body, "gather_input", outs, (w_qkv, w_out, vectors), "hhh", scratch)[0]


def attend(me, pieces, picked, back_rows, seg_row, seg_col, order):
    rows, width = picked.shape
    seqs = seg_row.shape[0]
    top = rows // seqs
    pairs = width // PAIR
    first = pieces[0].shape[1]
    rest = 3 * width - first
    spare = pieces[2].shape[1] - rest - width

    def body(me_ref, *refs):
        blocks, refs = refs[:10], refs[10:]
        x_ref, dy_ref, seg_row_ref, seg_col_ref, order_ref = refs[:5]
        own_ref, send_ref, df_ref, gate_ref, vec_ref, add_ref, h2_ref = refs[5:12]
        all_ref, out_ref, qkv_out, prob_out = refs[12:16]
        w_qkv, w_out, w_vec, qkv_ref, prob_ref, att_ref, sem = refs[16:]
        vec_copies = fetch(blocks, me_ref[0], sem, 0, (), ((w_vec, rest + width, 0, spare),))
        left = fetch(blocks, me_ref[0], sem, 8, ((w_qkv, 0, 0, first),), ())
        right = fetch(blocks, me_ref[0], sem, 16, (), ((w_qkv, 0, first, rest),))
        out_copies = fetch(blocks, me_ref[0], sem, 24, (), ((w_out, rest, 0, width),))
        start_all(vec_copies + left + right + out_copies)
        wait_all(vec_copies)
        vec = w_vec[...].astype(f32).T[:8]
        vec_ref[...] = vec
        x = x_ref[...].astype(f32)
        h1 = (x * lax.rsqrt(mean_last(x * x) + norm_eps) * vec[0:1]).astype(bf16)
        for copies, start, count in ((left, 0, first), (right, first, rest)):
            wait_all(copies)
            for part in range(start, start + count, 384):
                lanes = pl.ds(part, 384)
                qkv_ref[:, lanes] = dot_nn(h1, w_qkv[:, lanes]).astype(bf16)
        stored = [
            pltpu.make_async_copy(w_qkv, all_ref, sem.at[32]),
            pltpu.make_async_copy(qkv_ref, qkv_out, sem.at[33]),
            pltpu.make_async_copy(w_out, out_ref, sem.at[34]),
        ]
        wait_all(out_copies)
        start_all(stored)
        masks, masks_f = head_masks(bf16), head_masks(f32)
        ordered_pairs = lax.broadcasted_iota(jnp.int32, (top, top), 1) <= lax.broadcasted_iota(
            jnp.int32, (top, top), 0
        )
        for seq in range(seqs):
            here = pl.ds(seq * top, top)
            seen = ordered_pairs & (seg_col_ref[seq] == seg_row_ref[seq])
            hidden = jnp.where(seen, 0.0, masked_out)
            hidden = jnp.concatenate([hidden, hidden], axis=0)
            for pair in range(pairs):
                q, k, v = (
                    qkv_ref[here, pl.ds(part * width + pair * PAIR, PAIR)] for part in range(3)
                )
                scores = dot_nt(two_heads(q, masks), k) * head_scale
                scores = jnp.where(hidden < 0.0, masked_out, scores)
                power = jnp.exp(scores - jnp.max(scores, axis=-1, keepdims=True))
                probs = power / jnp.sum(power, axis=-1, keepdims=True)
                prob_ref[seq * pairs + pair] = probs
                mixed = one_pair(dot_nn(probs.astype(bf16), v), masks_f)
                att_ref[here, pl.ds(pair * PAIR, PAIR)] = mixed.astype(bf16)
            group = pl.ds(seq * pairs, pairs)
            stored.append(
                pltpu.make_async_copy(prob_ref.at[group], prob_out.at[group], sem.at[35 + seq])
            )
            stored[-1].start()
        gate = jax.nn.sigmoid(jnp.sum(x * vec[2:3], axis=-1, keepdims=True))
        gate_ref[...] = jnp.broadcast_to(gate, gate_ref.shape)
        df = (gate * dy_ref[...].astype(f32)).astype(bf16)
        df_ref[...] = df
        added = dot_nn(att_ref[...], w_out[...])
        add_ref[...] = added
        middle = x + added
        h2 = (middle * lax.rsqrt(mean_last(middle * middle) + norm_eps) * vec[1:2]).astype(bf16)
        h2_ref[...] = h2
        for half in range(2):
            lanes = slice(half * (width // 2), (half + 1) * (width // 2))
            send_ref[2 + half] = df[:, lanes]
            send_ref[4 + half] = h2[:, lanes]
        chosen = one_hot_columns(order_ref)
        for place, array in enumerate((h1, att_ref[...])):
            parted = dot_nn(array, chosen).astype(bf16)
            own_ref[place] = parted[:, : width // 2]
            send_ref[place] = parted[:, width // 2 :]
        wait_all(stored)

    outs = [
        ((2, rows, width // 2), bf16),
        ((6, rows, width // 2), bf16),
        ((rows, width), bf16),
        ((rows, 128), f32),
        ((8, width), f32),
        ((rows, width), f32),
        ((rows, width), bf16),
        ((width, 3 * width), bf16),
        ((width, width), bf16),
        ((rows, 3 * width), bf16),
        ((seqs * pairs, 2 * top, top), f32),
    ]
    scratch = [
        pltpu.VMEM((width, 3 * width), bf16),
        pltpu.VMEM((width, width), bf16),
        pltpu.VMEM((width, spare), bf16),
        pltpu.VMEM((rows, 3 * width), bf16),
        pltpu.VMEM((seqs * pairs, 2 * top, top), f32),
        pltpu.VMEM((rows, width), bf16),
        pltpu.SemaphoreType.DMA((35 + seqs,)),
    ]
    args = (me, *pieces, picked, back_rows, seg_row, seg_col, order)
    return kernel(body, "attend", outs, args, "s" + PIECES + "vvvvv", scratch, 26, 4)


def one_hot_columns(order_ref):
    width = order_ref.shape[1]
    chosen = lax.broadcasted_iota(jnp.int32, (width, width), 0) == order_ref[...]
    return chosen.astype(f32).astype(bf16)


def climb(me, pieces, h2, sib, order):
    rows, width = h2.shape
    first = pieces[0].shape[1]
    block = 2 * first // 8

    def body(me_ref, *refs):
        blocks, refs = refs[:10], refs[10:]
        h2_ref, sib_ref, order_ref = refs[:3]
        own_ref, send_ref, far_ref, pair_ref, up_ref, slope_out = refs[3:9]
        w_up, slope_ref, both_ref, sem = refs[9:]
        copies = fetch(
            blocks, me_ref[0], sem, 0, ((w_up, 0, 0, first),), ((w_up, 0, first, first),)
        )
        start_all(copies)
        both_ref[:rows] = h2_ref[...]
        for half in range(2):
            lanes = pl.ds(half * (width // 2), width // 2)
            both_ref[rows:, lanes] = sib_ref[4 + half]
        chosen = one_hot_columns(order_ref)[:, : width // 2]
        parted = dot_nn(both_ref[...], chosen).astype(bf16)
        pair_ref[0] = parted[:rows]
        pair_ref[1] = parted[rows:]
        wait_all(copies)
        stored = [pltpu.make_async_copy(w_up, up_ref, sem.at[16])]
        start_all(stored)
        scale = math.sqrt(2.0 / math.pi)
        for flip in range(8):
            start = pl.multiple_of((me_ref[0] ^ flip) * block, block)
            place = flip // 2
            lanes = pl.ds(place * block, block)
            weights = w_up[:, pl.ds(start, block)]
            u = dot_nn(both_ref[:rows], weights)
            square = u * u
            bent = jnp.tanh(scale * (u + 0.044715 * (square * u)))
            half_up = 0.5 * (1.0 + bent)
            target = send_ref if flip % 2 else own_ref
            target[:, lanes] = (u * half_up).astype(bf16)
            where = (flip % 2) * 4 + place
            slope_ref[where] = half_up + (0.5 * u) * (1.0 - bent * bent) * (
                scale * (1.0 + (3.0 * 0.044715) * square)
            )
            stored.append(
                pltpu.make_async_copy(
                    slope_ref.at[where], slope_out.at[where], sem.at[17 + flip]
                )
            )
            stored[-1].start()
            if flip % 2 == 0:
                u = dot_nn(both_ref[rows:], weights)
                bent = jnp.tanh(scale * (u + 0.044715 * (u * u * u)))
                far_ref[:, lanes] = (0.5 * u * (1.0 + bent)).astype(bf16)
        wait_all(stored)

    outs = [
        ((rows, 4 * block), bf16),
        ((rows, 4 * block), bf16),
        ((rows, 4 * block), bf16),
        ((2, rows, width // 2), bf16),
        ((width, 8 * block), bf16),
        ((8, rows, block), f32),
    ]
    scratch = [
        pltpu.VMEM((width, 8 * block), bf16),
        pltpu.VMEM((8, rows, block), f32),
        pltpu.VMEM((2 * rows, width), bf16),
        pltpu.SemaphoreType.DMA((25,)),
    ]
    args = (me, *pieces, h2, sib, order)
    return kernel(body, "climb", outs, args, "s" + PIECES + "vvv", scratch, 26, 2)


def vector_columns(order, mine, other):
    width = order.shape[1]
    half = width // 2

    def body(order_ref, *refs):
        ins, (left, right, rows) = refs[:6], refs[6:]
        chosen = one_hot_columns(order_ref)[:, :half]
        rows[...] = jnp.zeros_like(rows)
        for place in range(3):
            rows[place : place + 1] = ins[place][0:1] + ins[3 + place][0:1]
        columns = rows[...].T.astype(bf16)
        for part in range(2):
            left[part] = chosen[part * half : (part + 1) * half]
            right[part] = columns[part * half : (part + 1) * half]

    outs = [((2, half, half), bf16), ((2, half, 128), bf16)]
    scratch = [pltpu.VMEM((128, width), f32)]
    args = (order, *mine, *other)
    return kernel(body, "vector_columns", outs, args, "v" * 7, scratch)


class View:
    def __init__(self, array, columns=None, first=0, lead=None):
        self.array, self.first, self.lead = array, first, lead
        self.columns = columns or array.shape[-1]

    def value(self):
        array = self.array if self.lead is None else self.array[self.lead]
        return array[:, self.first : self.first + self.columns]

    def read(self, ref, first, columns):
        lanes = pl.ds(self.first + first, columns)
        return ref[:, lanes] if self.lead is None else ref[self.lead, :, lanes]


def outer(name, products, split):
    length = products[0][0].columns // 4
    total = sum(product[1].columns for product in products)
    widths = (split, total - split)
    order = ((2, 3), (1, 3), (0, 1), (0, 2))

    def body(*refs):
        ins, outs = refs[: 4 * len(products)], refs[4 * len(products) :]
        base = 0
        for number, product in enumerate(products):
            reads = [
                functools.partial(view.read, ref)
                for view, ref in zip(product, ins[4 * number : 4 * number + 4])
            ]
            columns = product[1].columns
            step = min(768, columns)
            for start in range(0, columns, step):
                for first in range(0, 4 * length, 384):
                    value = dot_tn(reads[0](first, 384), reads[1](start, step))
                    value += dot_tn(reads[2](first, 384), reads[3](start, step))
                    for block in range(first // length, (first + 384) // length):
                        part = value[block * length - first : (block + 1) * length - first]
                        for half in range(2):
                            low = max(base + start, half * split)
                            high = min(base + start + step, split + half * (total - split))
                            if high <= low:
                                continue
                            piece = part[:, low - base - start : high - base - start]
                            out_lanes = pl.ds(low - half * split, high - low)
                            for out in (half, 2 + half):
                                if block in order[out]:
                                    outs[out][order[out].index(block), :, out_lanes] = piece.astype(
                                        outs[out].dtype
                                    )
            base += columns

    outs = [
        ((2, length, widths[out % 2]), bf16 if out < 2 else f32) for out in range(4)
    ]
    args = [view.array for product in products for view in product]
    return kernel(body, name, outs, args, "v" * len(args))


def descend(me, pieces, slope, df):
    rows, width = df.shape
    block = slope.shape[2]

    def body(me_ref, *refs):
        blocks, refs = refs[:10], refs[10:]
        slope_in, df_ref, du_ref, down_ref, w_down, slope_ref, sem = refs
        copies = [[] for _ in range(8)]
        for flip, side, part in each_block(blocks):
            lanes = pl.ds(side * (width // 2), width // 2)
            place = (flip % 2) * 4 + flip // 2
            target = w_down.at[pl.ds(place * block, block), lanes]
            copies[place].append(
                pltpu.make_async_copy(part, target, sem.at[place * 2 + side])
            )
        for place, pair in enumerate(copies):
            pair.append(
                pltpu.make_async_copy(
                    slope_in.at[place], slope_ref.at[place], sem.at[17 + place]
                )
            )
            start_all(pair)
        for place in range(8):
            wait_all(copies[place])
            flip = place % 4 * 2 + place // 4
            start = pl.multiple_of((me_ref[0] ^ flip) * block, block)
            dg = dot_nt(df_ref[...], w_down[pl.ds(place * block, block)])
            du_ref[:, pl.ds(start, block)] = (dg * slope_ref[place]).astype(bf16)
        stored = pltpu.make_async_copy(w_down, down_ref, sem.at[16])
        stored.start()
        stored.wait()

    outs = [((rows, 8 * block), bf16), ((8 * block, width), bf16)]
    scratch = [
        pltpu.VMEM((8 * block, width), bf16),
        pltpu.VMEM((8, rows, block), f32),
        pltpu.SemaphoreType.DMA((25,)),
    ]
    args = (me, *pieces, slope, df)
    return kernel(body, "descend", outs, args, "s" + PIECES + "av", scratch, 24, 1)


def unclimb(w_up, du, picked, added, gate, back_rows, vec):
    rows, width = picked.shape

    def body(up_ref, du_ref, x_ref, add_ref, gate_ref, dy_ref, vec_ref, dm_ref, da_ref, dg_ref):
        dh = dot_nt(du_ref[...], up_ref[...])
        middle = x_ref[...].astype(f32) + add_ref[...]
        inverse = lax.rsqrt(mean_last(middle * middle) + norm_eps)
        unit = middle * inverse
        dg_ref[...] = jnp.broadcast_to(sum_rows(dh * unit), dg_ref.shape)
        scaled = dh * vec_ref[1:2]
        dm = inverse * (scaled - unit * mean_last(scaled * unit))
        dm_ref[...] = dm
        da_ref[...] = (gate_ref[:, 0:1] * dy_ref[...].astype(f32) + dm).astype(bf16)

    outs = [((rows, width), f32), ((rows, width), bf16), ((8, width), f32)]
    args = (w_up, du, picked, added, gate, back_rows, vec)
    return kernel(body, "unclimb", outs, args, "v" * 7)


def unattend(w_out, da, qkv, probs):
    rows, width = da.shape
    top = probs.shape[2]
    seqs, pairs = rows // top, width // PAIR

    def body(out_ref, da_ref, qkv_ref, prob_ref, dqkv_ref, do_ref):
        do_ref[...] = dot_nt(da_ref[...], out_ref[...]).astype(bf16)
        masks, masks_f = head_masks(bf16), head_masks(f32)
        for seq in range(seqs):
            here = pl.ds(seq * top, top)
            for pair in range(pairs):
                lanes = [pl.ds(part * width + pair * PAIR, PAIR) for part in range(3)]
                q, k, v = (qkv_ref[here, part] for part in lanes)
                do = two_heads(do_ref[here, pl.ds(pair * PAIR, PAIR)], masks)
                probs = prob_ref[seq * pairs + pair]
                dprobs = dot_nt(do, v)
                dscores = probs * (dprobs - jnp.sum(dprobs * probs, axis=-1, keepdims=True))
                dscores = dscores.astype(bf16)
                dq = one_pair(dot_nn(dscores, k), masks_f) * head_scale
                dk = dot_tn(dscores, two_heads(q, masks)) * head_scale
                dv = dot_tn(probs.astype(bf16), do)
                for part, value in zip(lanes, (dq, dk, dv)):
                    dqkv_ref[here, part] = value.astype(bf16)

    scratch = [pltpu.VMEM((rows, width), bf16)]
    outs = [((rows, 3 * width), bf16)]
    return kernel(body, "unattend", outs, (w_out, da, qkv, probs), "vvvv", scratch)[0]


def finish_mlp(w_down, own, send, picked, added, gate, back_rows):
    rows, width = picked.shape
    half = w_down.shape[0] // 2

    def body(down_ref, own_ref, send_ref, x_ref, add_ref, gate_ref, dy_ref, *outs):
        new_ref, dlogit_ref, dr_ref = outs
        out = dot_nn(own_ref[:, :half], down_ref[:half])
        out += dot_nn(send_ref[:, :half], down_ref[half:])
        both = add_ref[...] + out
        x = x_ref[...].astype(f32)
        gate = gate_ref[:, 0:1]
        new_ref[...] = (x + gate * both).astype(bf16)
        dlogit = jnp.sum(dy_ref[...].astype(f32) * both, axis=-1, keepdims=True)
        dlogit = dlogit * gate * (1.0 - gate)
        dlogit_ref[...] = jnp.broadcast_to(dlogit, dlogit_ref.shape)
        dr_ref[...] = jnp.broadcast_to(sum_rows(dlogit * x), dr_ref.shape)

    outs = [((rows, width), bf16), ((rows, 128), f32), ((8, width), f32)]
    args = (w_down, own, send, picked, added, gate, back_rows)
    return kernel(body, "finish_mlp", outs, args, "v" * 7)


def finish_rows(w_qkv, dqkv, picked, back_rows, dmiddle, dlogit, vec):
    rows, width = picked.shape

    def body(all_ref, dqkv_ref, x_ref, dy_ref, dm_ref, dlogit_ref, vec_ref, grad_ref, dg_ref):
        dh = dot_nt(dqkv_ref[...], all_ref[...])
        x = x_ref[...].astype(f32)
        inverse = lax.rsqrt(mean_last(x * x) + norm_eps)
        unit = x * inverse
        dg_ref[...] = jnp.broadcast_to(sum_rows(dh * unit), dg_ref.shape)
        scaled = dh * vec_ref[0:1]
        dx = inverse * (scaled - unit * mean_last(scaled * unit))
        grad = dy_ref[...].astype(f32) + dm_ref[...] + dx + dlogit_ref[:, 0:1] * vec_ref[2:3]
        grad_ref[...] = grad.astype(bf16)

    outs = [((rows, width), bf16), ((8, width), f32)]
    args = (w_qkv, dqkv, picked, back_rows, dmiddle, dlogit, vec)
    return kernel(body, "finish_rows", outs, args, "v" * 7)


def stack_all(*groups):
    counts = [len(group) for group in groups]

    def body(*refs):
        ins, outs = refs[: sum(counts)], refs[sum(counts) :]
        for out, count in zip(outs, counts):
            for place in range(count):
                out[place] = ins[place][...]
            ins = ins[count:]

    outs = [((len(group), *group[0].shape), group[0].dtype) for group in groups]
    args = [array for group in groups for array in group]
    return kernel(body, "stack_all", outs, args, "v" * len(args))


def pick_flip(refs, flip):
    if flip == 0 or len(refs) == 4:
        return refs[flip]
    return refs[1] if flip == 2 else refs[2].at[flip // 2]


def join_z(z, own, others, split):
    rows, width = own.shape
    count = 1 + len(others)

    def body(z_ref, *refs):
        ins, (left_ref, right_ref, total) = refs[:count], refs[count:]
        for flip in range(4):
            start = pl.multiple_of((z_ref[0] ^ flip) * rows, rows)
            total[pl.ds(start, rows)] = pick_flip(ins, flip)[...].astype(f32)
        left_ref[...] = total[:, :split].astype(bf16)
        right_ref[...] = total[:, split:].astype(bf16)

    outs = [((4 * rows, split), bf16), ((4 * rows, width - split), bf16)]
    scratch = [pltpu.VMEM((4 * rows, width), f32)]
    return kernel(body, "join_z", outs, (z, own, *others), "s" + "v" * count, scratch)


def join_z_pairs(z, mine, others):
    _, rows, width = mine.shape

    def body(z_ref, *refs):
        ins, outs = refs[:3], refs[3:]
        for flip in range(4):
            start = pl.ds(pl.multiple_of((z_ref[0] ^ flip) * rows, rows), rows)
            block = pick_flip(ins, flip)
            for place in range(4):
                outs[place][start] = block[place]

    outs = [((4 * rows, width), bf16)] * 4
    return kernel(body, "join_z_pairs", outs, (z, mine, *others), "svvv")


def add_z_pairs(z, keep_l, keep_r, other_l, other_r):
    pair, rows, width = keep_l.shape
    part = rows // 4

    def body(z_ref, keep_l, keep_r, other_l, other_r, mine, send, total):
        for half, (keep, other) in enumerate(((keep_l, other_l), (keep_r, other_r))):
            for place in range(pair):
                total[half * pair + place] = keep[place] + other[place].astype(f32)
        for flip in range(4):
            start = pl.multiple_of((z_ref[0] ^ flip) * part, part)
            out = (mine, send)[flip % 2]
            out[flip // 2] = total[:, pl.ds(start, part)].astype(out.dtype)

    outs = [((2, 4, part, width), f32), ((2, 4, part, width), bf16)]
    scratch = [pltpu.VMEM((4, rows, width), f32)]
    args = (z, keep_l, keep_r, other_l, other_r)
    return kernel(body, "add_z_pairs", outs, args, "svvvv", scratch)


def add_four(mine, other):
    def body(mine, other, send_l, send_r, keep):
        def total(place):
            return mine[place] + other[place].astype(f32)

        width = mine.shape[2]
        keep[:, :width] = total(0)
        keep[:, width:] = total(2)
        send_l[...] = total(1).astype(bf16)
        send_r[...] = total(3).astype(bf16)

    _, rows, width = mine.shape
    outs = [((rows, width), bf16)] * 2 + [((rows, 2 * width), f32)]
    return kernel(body, "add_four", outs, (mine, other), "vv")


def add_pairs(keep_l, keep_r, other_l, other_r):
    def body(keep_l, keep_r, other_l, other_r, send_l, send_r, left, right):
        for keep, other, send, mine in (
            (keep_l, other_l, send_l, left),
            (keep_r, other_r, send_r, right),
        ):
            send[...] = (keep[1] + other[1].astype(f32)).astype(bf16)
            mine[...] = keep[0] + other[0].astype(f32)

    shapes = [keep_l.shape[1:], keep_r.shape[1:]]
    outs = [(shape, kind) for kind in (bf16, f32) for shape in shapes]
    return kernel(body, "add_pairs", outs, (keep_l, keep_r, other_l, other_r), "vvvv")


def add_split(z, keep_l, keep_r, other_l, other_r):
    rows, split = keep_l.shape
    width = split + keep_r.shape[1]
    part = rows // 4

    def body(z_ref, keep_l, keep_r, other_l, other_r, mine, send, total):
        total[:, :split] = keep_l[...] + other_l[...].astype(f32)
        total[:, split:] = keep_r[...] + other_r[...].astype(f32)
        for flip in range(4):
            start = pl.multiple_of((z_ref[0] ^ flip) * part, part)
            out = (mine, send)[flip % 2]
            out[flip // 2] = total[pl.ds(start, part)].astype(out.dtype)

    outs = [((2, part, width), f32), ((2, part, width), bf16)]
    scratch = [pltpu.VMEM((rows, width), f32)]
    args = (z, keep_l, keep_r, other_l, other_r)
    return kernel(body, "add_split", outs, args, "svvvv", scratch)


def add_next(keep, other):
    def body(keep, other, mine, send):
        mine[...] = keep[0] + other[0].astype(f32)
        send[...] = (keep[1] + other[1].astype(f32)).astype(bf16)

    shape = keep.shape[1:]
    return kernel(body, "add_next", [(shape, f32), (shape, bf16)], (keep, other), "vv")


def settle_halves(keep, other_l, other_r):
    def body(keep, other_l, other_r, grad, square):
        width = other_l.shape[1]
        total = None
        for half, other in enumerate((other_l, other_r)):
            lanes = pl.ds(half * width, width)
            value = keep[:, lanes] + other[...].astype(f32)
            grad[:, lanes] = value
            part = jnp.sum(value * value)
            total = part if total is None else total + part
        square[...] = jnp.full(square.shape, total)

    outs = [(keep.shape, f32), ((8, 128), f32)]
    return kernel(body, "settle_halves", outs, (keep, other_l, other_r), "vvv")


def settle_z(mine, other, squares, devices):
    rows, width = mine.shape

    def body(mine, other, *refs):
        more, (grad, square, last, turned) = refs[: len(squares)], refs[len(squares) :]
        value = mine[...] + other[...].astype(f32)
        grad[...] = value
        total = jnp.sum(value * value)
        for ref in more:
            total = total + ref[0:1, :]
        square[...] = jnp.broadcast_to(total, square.shape)
        turned[...] = jnp.zeros_like(turned)
        turned[:rows] = value[:, width - 128 :]
        last[...] = turned[...].T[:8]

    outs = [(mine.shape, f32), ((devices, 128), f32), ((8, 128), f32)]
    scratch = [pltpu.VMEM((128, 128), f32)]
    args = (mine, other, *squares)
    return kernel(body, "settle_z", outs, args, "v" * len(args), scratch)


def update(squares, limit, grads, states, vec_grad, vec_states):
    count = len(grads)

    def body(square_ref, *refs):
        grad_refs, refs = refs[:count], refs[count:]
        state_refs, refs = refs[: 3 * count], refs[3 * count :]
        vec_ref, vec_m, vec_v, norm_ref, out_refs = *refs[:4], refs[4:]
        norm = jnp.sqrt(jnp.sum(square_ref[...], axis=0, keepdims=True)[:, 0:1])
        norm_ref[...] = jnp.broadcast_to(norm, norm_ref.shape)
        factor = jnp.minimum(1.0, limit / (norm + 1e-06))
        for place in range(count):
            w, m, v = (ref[...] for ref in state_refs[3 * place : 3 * place + 3])
            grad = grads[place].read(grad_refs[place], 0, grads[place].columns) * factor
            for ref, value in zip(out_refs[3 * place :], adam_update(w, grad, m, v)):
                ref[...] = value
        grad = vec_ref[:3, : vec_m.shape[1]] * factor
        first, second = moment_update(grad, vec_m[...], vec_v[...])
        out_refs[-2][...] = first
        out_refs[-1][...] = second

    flat = [array for state in states for array in state]
    outs = [((8, 128), f32)] + [(array.shape, f32) for array in (*flat, *vec_states)]
    args = (squares, *(grad.array for grad in grads), *flat, vec_grad, *vec_states)
    return kernel(body, "update", outs, args, "v" * len(args), (), 32)


class Steps:
    def __init__(self, chain):
        self.chain = chain
        self.result = None
        self.launch(next(chain))

    def launch(self, step):
        self.flips = [flip for _, flip in step]
        self.given = [array for array, _ in step]

    def advance(self, arrays):
        try:
            self.launch(self.chain.send(arrays))
        except StopIteration as stop:
            self.flips, self.given, self.result = (), (), stop.value


def slot(chains, value):
    arrays = [
        [swap(array, flip) for array, flip in zip(chain.given, chain.flips)] for chain in chains
    ]
    arrays, value = lax.optimization_barrier((arrays, value))
    for chain, array in zip(chains, arrays):
        chain.advance(array)
    return value


def ready(chains, value):
    arrays, value = lax.optimization_barrier(([chain.given for chain in chains], value))
    for chain, array in zip(chains, arrays):
        chain.given = array
    return value


def swap(array, bit):
    count = lax.axis_size("wide") * lax.axis_size("narrow")
    return lax.ppermute(array, AXES, [(i, i ^ bit) for i in range(count)])


def exchange(*arrays):
    return (yield [(array, 4) for array in arrays])


def around_z(shard, at_once):
    if at_once:
        return (yield [(shard, flip) for flip in (1, 2, 3)])
    (two,) = yield [(shard, 2)]
    (both,) = yield [(stack_all((shard, two))[0], 1)]
    return two, both


def gather(shard, z, split, at_once):
    others = yield from around_z(shard, at_once)
    left, right = join_z(z, shard, others, split)
    near_l, near_r = yield [(left, 8), (right, 16)]
    return (yield from spread(left, near_l, right, near_r))


def gather_pairs(shard, z):
    half = shard.shape[1] // 2
    left, right = shard[:, :half], shard[:, half:]
    near_l, near_r = yield [(left, 8), (right, 16)]
    mine = jnp.stack([left, near_l, right, near_r])
    others = yield from around_z(mine, False)
    return (yield from spread(*join_z_pairs(z, mine, others)))


def spread(left, near_l, right, near_r):
    keep_l, keep_r = stack_all((left, near_l), (right, near_r))
    far_l, far_r, *near = yield [(keep_l, 16), (keep_r, 8), (keep_l, 4), (keep_r, 4)]
    far = yield [(far_l, 4), (far_r, 4)]
    return (left, near_l, right, near_r, far_l, far_r, *near, *far)


def scatter(z, send_l, send_r, keep_l, keep_r):
    other_l, other_r = yield [(send_l, 16), (send_r, 8)]
    send_l, send_r, left, right = add_pairs(keep_l, keep_r, other_l, other_r)
    other_l, other_r = yield [(send_l, 8), (send_r, 16)]
    mine, send = add_split(z, left, right, other_l, other_r)
    (other,) = yield [(send, 1)]
    mine, send = add_next(mine, other)
    (other,) = yield [(send, 2)]
    return mine, other


def scatter_pairs(z, send_l, send_r, keep_l, keep_r):
    other_l, other_r = yield [(send_l, 16), (send_r, 8)]
    mine, send = add_z_pairs(z, keep_l, keep_r, other_l, other_r)
    (other,) = yield [(send, 1)]
    mine, send = add_next(mine, other)
    (other,) = yield [(send, 2)]
    send_l, send_r, keep = add_four(mine, other)
    other_l, other_r = yield [(send_l, 8), (send_r, 16)]
    return settle_halves(keep, other_l, other_r)


def cut(whole, split):
    blocks = whole.reshape(8, whole.shape[0] // 8, whole.shape[1])
    sides = (blocks[..., :split], blocks[..., split:])
    groups = [
        [sides[flip[2]][flip[0] * 4 + flip[1] * 2 + core] for flip in flips]
        for core in range(2)
        for flips in GROUPS
    ]
    return (*groups[0], *groups[1], *(jnp.stack(group) for group in groups[2:]))


def uncut(own, send):
    parts = jnp.stack([array.reshape(array.shape[0], 4, -1) for array in (own, send)], axis=2)
    return parts.reshape(own.shape[0], -1)


def per_device(
    paired,
    tokens,
    cotangent,
    segments,
    picks,
    w_qkv,
    w_out,
    w_up,
    w_down,
    vectors,
    m_qkv,
    m_out,
    m_up,
    m_down,
    m_vectors,
    v_qkv,
    v_out,
    v_up,
    v_down,
    v_vectors,
):
    devices_all = lax.axis_size("wide") * lax.axis_size("narrow")
    lane = lax.axis_index(AXES)
    seq_count, top_count = picks.shape
    seq_len = segments.shape[1]
    model_width = tokens.shape[1]
    qkv_width = w_qkv.shape[1]
    ff_width = w_up.shape[1]
    shard_width = vectors.shape[1]
    split_a, split_b, split_c = 2 * model_width, ff_width // 2, model_width // 2
    z = (lane & 3).reshape(1)
    me = (lane >> 2).reshape(1) if paired else jnp.zeros((1,), jnp.int32)

    chunk_a = gather_input(w_qkv, w_out, vectors)
    chunk_b = w_up.astype(bf16)
    chunk_c = w_down.astype(bf16)

    def start(chain, *args):
        return Steps(chain(*args)) if paired else None

    def tick(chains, value):
        return slot(chains, value) if paired else value

    def stage(chains, value):
        return ready(chains, value) if paired else value

    def whole(take, chunk, split):
        if paired:
            return take.result
        return cut(lax.all_gather(chunk, AXES, axis=0, tiled=True), split)

    hot = picks[:, :, None] == jnp.arange(seq_len, dtype=jnp.int32)[None, None, :]
    hot_low = hot.astype(bf16)
    tok_blocks = tokens.reshape(seq_count, seq_len, model_width)
    back_blocks = cotangent.reshape(seq_count, seq_len, model_width)

    def pick(blocks):
        rows = jnp.einsum("skl,sld->skd", hot_low, blocks, preferred_element_type=f32)
        return rows.astype(bf16).reshape(-1, model_width)

    def place(blocks, rows):
        rows = rows.reshape(seq_count, top_count, model_width)
        spread = jnp.einsum("skl,skd->sld", hot_low, rows, preferred_element_type=f32).astype(bf16)
        taken = jnp.any(hot, axis=1)
        return jnp.where(taken[:, :, None], spread, blocks).reshape(-1, model_width)

    take_a = start(gather, chunk_a, z, split_a, True)
    take_c = start(gather_pairs, chunk_c, z)
    picked = pick(tok_blocks)
    back_rows = pick(back_blocks)
    seg_sel = jnp.sum(jnp.where(hot, segments[:, None, :], 0), axis=-1)
    seg_row, seg_col = seg_sel[:, None, :], seg_sel[:, :, None]
    spot = jnp.arange(model_width, dtype=jnp.int32)
    half, eighth = model_width // 2, model_width // 8
    flip = spot % half // eighth * 2 + spot // half
    order = ((me[0] ^ flip) * eighth + spot % eighth)[None]
    inputs = (picked, back_rows, seg_row, seg_col, order, chunk_b)
    inputs = tick([take_a, take_c], inputs)
    take_b = start(gather, inputs[-1], z, split_b, False)
    inputs = tick([take_a], inputs[:-1])
    inputs = tick([take_b], inputs)
    inputs = tick([take_b, take_c], inputs)
    inputs = tick([take_a, take_b], inputs)
    inputs = tick([take_a], inputs)

    all_a = whole(take_a, chunk_a, split_a)
    picked, back_rows = inputs[:2]
    order = inputs[4]
    state = attend(me, all_a, *inputs)
    state = tick([take_b, take_c], state)
    own, send, df, gate, vec, added, h2, all_qkv, all_out, qkv, probs = state
    early = start(exchange, send)
    h2 = stage([take_c], h2)
    h2 = tick([take_b, early], h2)
    (sib,) = early.result if paired else (send,)
    all_b = whole(take_b, chunk_b, split_b)
    g_own, g_send, g_sib, h2_pair, all_up, slope = climb(me, all_b, h2, sib, order)

    def give(chain, name, products, split):
        if paired:
            return Steps(chain(z, *outer(name, products, split)))
        grads = [dot_tn(uncut(one.value(), far.value()), two.value()) for one, two, far, _ in products]
        grad = jnp.concatenate(grads, axis=1)
        grad = lax.psum_scatter(grad, AXES, scatter_dimension=0, tiled=True)
        return grad, jnp.full((8, 128), jnp.sum(grad * grad))

    df_sib = jnp.concatenate([sib[2], sib[3]], axis=1)
    left_c = View(g_sib) if paired else View(g_send)
    give_c = give(
        scatter_pairs, "outer_c", [(View(g_own), View(df), left_c, View(df_sib))], split_c
    )
    slope = stage([give_c], slope)
    slope = tick([take_c], slope)
    slope = tick([take_c], slope)
    all_c = whole(take_c, chunk_c, split_c)
    du, all_down = descend(me, all_c, slope, df)
    dmiddle, da, dg2 = unclimb(all_up, du, picked, added, gate, back_rows, vec)
    new_rows, dlogit, dr = finish_mlp(
        all_down, g_own, g_send, picked, added, gate, back_rows
    )
    du, da, dmiddle, new_rows, dlogit = tick([give_c], (du, da, dmiddle, new_rows, dlogit))
    late_u = start(exchange, du)
    dqkv = unattend(all_out, da, qkv, probs)
    dqkv = tick([late_u], dqkv)
    (du_sib,) = late_u.result if paired else (du,)
    late_q = start(exchange, dqkv, da)
    views = [View(h2_pair, lead=place) for place in range(2)]
    if not paired:
        cols = h2.reshape(h2.shape[0], 4, 2, -1)
        views = [View(cols[:, :, core].reshape(h2.shape[0], -1)) for core in range(2)]
    give_b = give(
        scatter_pairs, "outer_b", [(views[0], View(du), views[1], View(du_sib))], split_b
    )
    dqkv = stage([give_b, give_c], dqkv)
    grad_rows, dg1 = finish_rows(all_qkv, dqkv, picked, back_rows, dmiddle, dlogit, vec)
    late_v = start(exchange, dg1, dg2, dr)
    dqkv = stage([late_v], dqkv)
    dqkv = tick([late_q, late_v], dqkv)
    dqkv_sib, da_sib = late_q.result if paired else (dqkv, da)
    products = [
        (View(own, lead=0), View(dqkv), View(sib, lead=0), View(dqkv_sib)),
        (View(own, lead=1), View(da), View(sib, lead=1), View(da_sib)),
    ]
    if paired:
        left, right = vector_columns(order, (dg1, dg2, dr), late_v.result)
        products.append(tuple(View(array, lead=part) for part in range(2) for array in (left, right)))
    give_a = give(scatter, "outer_a", products, split_a)
    grad_rows = stage([give_a], grad_rows)
    grad_rows = tick([give_b, give_c], grad_rows)
    grad_rows, new_rows = stage([give_b, give_c], (grad_rows, new_rows))
    mixed_rows = place(tok_blocks, new_rows)
    grad_rows, mixed_rows = tick([give_a], (grad_rows, mixed_rows))
    grad_rows = stage([give_a], grad_rows)
    grad_rows = tick([give_b, give_c], grad_rows)
    grad_rows = stage([give_b, give_c], grad_rows)
    grad_rows = tick([give_a, give_c], grad_rows)
    grad_rows = stage([give_a], grad_rows)
    input_grad = place(back_blocks, grad_rows)
    input_grad = tick([give_a, give_b], input_grad)
    input_grad = stage([give_a, give_b], input_grad)
    input_grad = tick([give_a, give_b], input_grad)
    if paired:
        (grad_b, square_b), (grad_c, square_c) = give_b.result, give_c.result
        grad_a, squares, vec_grad = settle_z(*give_a.result, (square_b, square_c), devices_all)
    else:
        rows = jnp.stack([dg1[0], dg2[0], dr[0]], axis=0)
        rows = lax.psum_scatter(rows, AXES, scatter_dimension=1, tiled=True)
        vec_grad = jnp.pad(rows, ((0, 5), (0, 128 - shard_width)))
        (grad_a, square_a), (grad_b, square_b), (grad_c, square_c) = give_a, give_b, give_c
        local_sq = square_a + square_b + square_c + jnp.sum(rows * rows)
        squares = jnp.broadcast_to(local_sq[:1], (devices_all, 128))
    squares = lax.all_to_all(squares, AXES, 0, 0, tiled=True)
    params_all = 4 * model_width * model_width + 2 * model_width * ff_width + 3 * model_width
    selected_all = seq_count * top_count * devices_all
    clip_limit = limit_scale * math.sqrt(params_all * selected_all)
    norm, *news = update(
        squares,
        clip_limit,
        [
            View(grad_a, qkv_width),
            View(grad_a, model_width, qkv_width),
            View(grad_b),
            View(grad_c),
        ],
        [
            (w_qkv, m_qkv, v_qkv),
            (w_out, m_out, v_out),
            (w_up, m_up, v_up),
            (w_down, m_down, v_down),
        ],
        vec_grad,
        (m_vectors, v_vectors),
    )
    return (
        mixed_rows,
        input_grad,
        norm[0, 0],
        *news[0:12:3],
        *news[1:12:3],
        news[12],
        *news[2:12:3],
        news[13],
    )


def solution(mesh):
    placed = (
        P(("wide", "narrow"), None),
        P(("wide", "narrow"), None),
        P(("wide", "narrow"), None),
        P(("wide", "narrow"), None),
        P(("wide", "narrow"), None),
        P(("wide", "narrow"), None),
        P(("wide", "narrow"), None),
        P(("wide", "narrow"), None),
        P(None, ("wide", "narrow")),
        P(("wide", "narrow"), None),
        P(("wide", "narrow"), None),
        P(("wide", "narrow"), None),
        P(("wide", "narrow"), None),
        P(None, ("wide", "narrow")),
        P(("wide", "narrow"), None),
        P(("wide", "narrow"), None),
        P(("wide", "narrow"), None),
        P(("wide", "narrow"), None),
        P(None, ("wide", "narrow")),
    )
    paired = mesh.shape["wide"] == 8 and mesh.shape["narrow"] == 4
    return jax.shard_map(
        functools.partial(per_device, paired),
        mesh=mesh,
        in_specs=placed,
        out_specs=(
            P(("wide", "narrow"), None),
            P(("wide", "narrow"), None),
            P(),
            P(("wide", "narrow"), None),
            P(("wide", "narrow"), None),
            P(("wide", "narrow"), None),
            P(("wide", "narrow"), None),
            P(("wide", "narrow"), None),
            P(("wide", "narrow"), None),
            P(("wide", "narrow"), None),
            P(("wide", "narrow"), None),
            P(None, ("wide", "narrow")),
            P(("wide", "narrow"), None),
            P(("wide", "narrow"), None),
            P(("wide", "narrow"), None),
            P(("wide", "narrow"), None),
            P(None, ("wide", "narrow")),
        ),
        check_vma=False,
    )
```

```python
import functools
import math

import jax
import jax.numpy as jnp
from jax import lax
from jax.experimental import pallas as pl
from jax.experimental.pallas import tpu as pltpu
from jax.sharding import PartitionSpec as P

HEAD_DIM = 64


norm_eps = 1e-06
beta_one = 0.9
beta_two = 0.999
adam_eps = 1e-08
learn_rate = 0.03
decay_rate = 0.1
adam_step = 10
limit_scale = 0.01
masked_out = -1e30
AXES = ("wide", "narrow")


def moment_update(grad_part, first, second):
    first_new = beta_one * first + (1.0 - beta_one) * grad_part
    second_new = beta_two * second + (1.0 - beta_two) * grad_part * grad_part
    return (first_new, second_new)


def adam_update(master, grad_part, first, second):
    first_new, second_new = moment_update(grad_part, first, second)
    first_hat = first_new / (1.0 - beta_one**adam_step)
    second_hat = second_new / (1.0 - beta_two**adam_step)
    master_new = master - learn_rate * (
        first_hat / (jnp.sqrt(second_hat) + adam_eps) + decay_rate * master
    )
    return (master_new, first_new, second_new)


f32, bf16 = jnp.float32, jnp.bfloat16
PAIR = 2 * HEAD_DIM
head_scale = HEAD_DIM ** (-0.5)
KEEP_L = ((0, 0, 0), (0, 1, 0))
KEEP_R = ((0, 0, 1), (1, 0, 1))
FAR_L = ((1, 0, 0), (1, 1, 0))
FAR_R = ((0, 1, 1), (1, 1, 1))
GROUPS = (KEEP_L, KEEP_R, FAR_L, FAR_R)


def kernel(body, name, outs, args, kinds, scratch=(), limit=24, loose=0):
    spaces = {"s": pltpu.SMEM, "v": pltpu.VMEM, "h": pltpu.VMEM, "a": pltpu.HBM}
    held = len(outs) - loose
    return pl.pallas_call(
        body,
        out_shape=[
            jax.ShapeDtypeStruct(*out) if place < held else pltpu.HBM(*out)
            for place, out in enumerate(outs)
        ],
        in_specs=[pl.BlockSpec(memory_space=spaces[kind]) for kind in kinds],
        out_specs=[
            pl.BlockSpec(memory_space=pltpu.VMEM if place < held else pltpu.HBM)
            for place in range(len(outs))
        ],
        scratch_shapes=list(scratch),
        compiler_params=pltpu.CompilerParams(vmem_limit_bytes=limit << 20),
        cost_estimate=pl.CostEstimate(flops=1, bytes_accessed=1, transcendentals=0),
        name=name,
    )(
        *(
            pltpu.with_memory_space_constraint(arg, pltpu.HBM) if kind in "ah" else arg
            for arg, kind in zip(args, kinds)
        )
    )


def each_block(pieces):
    for core in range(2):
        for group, flips in enumerate(GROUPS):
            for place, flip in enumerate(flips):
                yield flip[0] * 4 + flip[1] * 2 + core, flip[2], pieces[core * 4 + group].at[place]


def start_all(copies):
    for copy in copies:
        copy.start()


def wait_all(copies):
    for copy in copies:
        copy.wait()


def fetch(pieces, me, sem, base, left, right):
    copies = []
    for flip, half, block in each_block(pieces):
        rows = block.shape[0]
        start = pl.multiple_of((me ^ flip) * rows, rows)
        for target, column, out_column, width in (left, right)[half]:
            copies.append(
                pltpu.make_async_copy(
                    block.at[:, pl.ds(column, width)],
                    target.at[pl.ds(start, rows), pl.ds(out_column, width)],
                    sem.at[base + len(copies)],
                )
            )
    return copies


def dot_nt(left, right):
    return lax.dot_general(left, right, (((1,), (1,)), ((), ())), preferred_element_type=f32)


def dot_tn(left, right):
    return lax.dot_general(left, right, (((0,), (0,)), ((), ())), preferred_element_type=f32)


def dot_nn(left, right):
    return jnp.dot(left, right, preferred_element_type=f32)


def mean_last(array):
    return jnp.mean(array, axis=-1, keepdims=True)


def sum_rows(array):
    return jnp.sum(array, axis=0, keepdims=True)


def head_masks(dtype):
    lanes = lax.broadcasted_iota(jnp.int32, (1, PAIR), 1)
    first = (lanes < HEAD_DIM).astype(f32).astype(dtype)
    return first, (1 - first).astype(dtype)


def two_heads(pair, masks):
    return jnp.concatenate([pair * masks[0], pair * masks[1]], axis=0)


def one_pair(stacked, masks):
    rows = stacked.shape[0] // 2
    return stacked[:rows] * masks[0] + stacked[rows:] * masks[1]


def gather_input(w_qkv, w_out, vectors):
    rows, first = w_qkv.shape
    second = w_out.shape[1]

    def body(qkv_ref, out_ref, vec_ref, chunk_ref, turned):
        chunk_ref[:, :first] = qkv_ref[...].astype(bf16)
        chunk_ref[:, first : first + second] = out_ref[...].astype(bf16)
        turned[...] = jnp.zeros_like(turned)
        turned[:3] = vec_ref[...]
        same = lax.broadcasted_iota(jnp.int32, (rows, rows), 0) == lax.broadcasted_iota(
            jnp.int32, (rows, rows), 1
        )
        columns = dot_nt(same.astype(f32).astype(bf16), turned[...].astype(bf16))
        chunk_ref[:, first + second :] = columns.astype(bf16)

    outs = [((rows, first + second + 128), bf16)]
    scratch = [pltpu.VMEM((128, rows), f32)]
    return kernel(body, "gather_input", outs, (w_qkv, w_out, vectors), "hhh", scratch)[0]


def attend(me, pieces, picked, back_rows, seg_row, seg_col, order):
    rows, width = picked.shape
    seqs = seg_row.shape[0]
    top = rows // seqs
    pairs = width // PAIR
    first = pieces[0].shape[2]
    rest = 3 * width - first
    spare = pieces[1].shape[2] - rest - width

    def body(me_ref, *refs):
        blocks, refs = refs[:8], refs[8:]
        x_ref, dy_ref, seg_row_ref, seg_col_ref, order_ref = refs[:5]
        own_ref, send_ref, df_ref, gate_ref, vec_ref, add_ref, h2_ref = refs[5:12]
        all_ref, out_ref, qkv_out, prob_out = refs[12:16]
        w_qkv, w_out, w_vec, qkv_ref, prob_ref, att_ref, sem = refs[16:]
        vec_copies = fetch(blocks, me_ref[0], sem, 0, (), ((w_vec, rest + width, 0, spare),))
        left = fetch(blocks, me_ref[0], sem, 8, ((w_qkv, 0, 0, first),), ())
        right = fetch(blocks, me_ref[0], sem, 16, (), ((w_qkv, 0, first, rest),))
        out_copies = fetch(blocks, me_ref[0], sem, 24, (), ((w_out, rest, 0, width),))
        start_all(vec_copies + left + right + out_copies)
        wait_all(vec_copies)
        vec = w_vec[...].astype(f32).T[:8]
        vec_ref[...] = vec
        x = x_ref[...].astype(f32)
        h1 = (x * lax.rsqrt(mean_last(x * x) + norm_eps) * vec[0:1]).astype(bf16)
        for copies, start, count in ((left, 0, first), (right, first, rest)):
            wait_all(copies)
            for part in range(start, start + count, 384):
                lanes = pl.ds(part, 384)
                qkv_ref[:, lanes] = dot_nn(h1, w_qkv[:, lanes]).astype(bf16)
        stored = [
            pltpu.make_async_copy(w_qkv, all_ref, sem.at[32]),
            pltpu.make_async_copy(qkv_ref, qkv_out, sem.at[33]),
            pltpu.make_async_copy(w_out, out_ref, sem.at[34]),
        ]
        wait_all(out_copies)
        start_all(stored)
        masks, masks_f = head_masks(bf16), head_masks(f32)
        ordered_pairs = lax.broadcasted_iota(jnp.int32, (top, top), 1) <= lax.broadcasted_iota(
            jnp.int32, (top, top), 0
        )
        for seq in range(seqs):
            here = pl.ds(seq * top, top)
            seen = ordered_pairs & (seg_col_ref[seq] == seg_row_ref[seq])
            hidden = jnp.where(seen, 0.0, masked_out)
            hidden = jnp.concatenate([hidden, hidden], axis=0)
            for pair in range(pairs):
                q, k, v = (
                    qkv_ref[here, pl.ds(part * width + pair * PAIR, PAIR)] for part in range(3)
                )
                scores = dot_nt(two_heads(q, masks), k) * head_scale
                scores = jnp.where(hidden < 0.0, masked_out, scores)
                power = jnp.exp(scores - jnp.max(scores, axis=-1, keepdims=True))
                probs = power / jnp.sum(power, axis=-1, keepdims=True)
                prob_ref[seq * pairs + pair] = probs
                mixed = one_pair(dot_nn(probs.astype(bf16), v), masks_f)
                att_ref[here, pl.ds(pair * PAIR, PAIR)] = mixed.astype(bf16)
            group = pl.ds(seq * pairs, pairs)
            stored.append(
                pltpu.make_async_copy(prob_ref.at[group], prob_out.at[group], sem.at[35 + seq])
            )
            stored[-1].start()
        gate = jax.nn.sigmoid(jnp.sum(x * vec[2:3], axis=-1, keepdims=True))
        gate_ref[...] = jnp.broadcast_to(gate, gate_ref.shape)
        df = (gate * dy_ref[...].astype(f32)).astype(bf16)
        df_ref[...] = df
        added = dot_nn(att_ref[...], w_out[...])
        add_ref[...] = added
        middle = x + added
        h2 = (middle * lax.rsqrt(mean_last(middle * middle) + norm_eps) * vec[1:2]).astype(bf16)
        h2_ref[...] = h2
        for half in range(2):
            lanes = slice(half * (width // 2), (half + 1) * (width // 2))
            send_ref[2 + half] = df[:, lanes]
            send_ref[4 + half] = h2[:, lanes]
        chosen = one_hot_columns(order_ref)
        for place, array in enumerate((h1, att_ref[...])):
            parted = dot_nn(array, chosen).astype(bf16)
            own_ref[place] = parted[:, : width // 2]
            send_ref[place] = parted[:, width // 2 :]
        wait_all(stored)

    outs = [
        ((2, rows, width // 2), bf16),
        ((6, rows, width // 2), bf16),
        ((rows, width), bf16),
        ((rows, 128), f32),
        ((8, width), f32),
        ((rows, width), f32),
        ((rows, width), bf16),
        ((width, 3 * width), bf16),
        ((width, width), bf16),
        ((rows, 3 * width), bf16),
        ((seqs * pairs, 2 * top, top), f32),
    ]
    scratch = [
        pltpu.VMEM((width, 3 * width), bf16),
        pltpu.VMEM((width, width), bf16),
        pltpu.VMEM((width, spare), bf16),
        pltpu.VMEM((rows, 3 * width), bf16),
        pltpu.VMEM((seqs * pairs, 2 * top, top), f32),
        pltpu.VMEM((rows, width), bf16),
        pltpu.SemaphoreType.DMA((35 + seqs,)),
    ]
    args = (me, *pieces, picked, back_rows, seg_row, seg_col, order)
    return kernel(body, "attend", outs, args, "s" + "a" * 8 + "vvvvv", scratch, 26, 4)


def one_hot_columns(order_ref):
    width = order_ref.shape[1]
    chosen = lax.broadcasted_iota(jnp.int32, (width, width), 0) == order_ref[...]
    return chosen.astype(f32).astype(bf16)


def climb(me, pieces, h2, sib, order):
    rows, width = h2.shape
    first = pieces[0].shape[2]
    block = 2 * first // 8

    def body(me_ref, *refs):
        blocks, refs = refs[:8], refs[8:]
        h2_ref, sib_ref, order_ref = refs[:3]
        own_ref, send_ref, far_ref, pair_ref, up_ref, slope_out = refs[3:9]
        w_up, slope_ref, both_ref, sem = refs[9:]
        copies = fetch(
            blocks, me_ref[0], sem, 0, ((w_up, 0, 0, first),), ((w_up, 0, first, first),)
        )
        start_all(copies)
        both_ref[:rows] = h2_ref[...]
        for half in range(2):
            lanes = pl.ds(half * (width // 2), width // 2)
            both_ref[rows:, lanes] = sib_ref[4 + half]
        chosen = one_hot_columns(order_ref)[:, : width // 2]
        parted = dot_nn(both_ref[...], chosen).astype(bf16)
        pair_ref[0] = parted[:rows]
        pair_ref[1] = parted[rows:]
        wait_all(copies)
        stored = [pltpu.make_async_copy(w_up, up_ref, sem.at[16])]
        start_all(stored)
        scale = math.sqrt(2.0 / math.pi)
        for flip in range(8):
            start = pl.multiple_of((me_ref[0] ^ flip) * block, block)
            place = flip // 2
            lanes = pl.ds(place * block, block)
            weights = w_up[:, pl.ds(start, block)]
            u = dot_nn(both_ref[:rows], weights)
            square = u * u
            bent = jnp.tanh(scale * (u + 0.044715 * (square * u)))
            half_up = 0.5 * (1.0 + bent)
            target = send_ref if flip % 2 else own_ref
            target[:, lanes] = (u * half_up).astype(bf16)
            where = (flip % 2) * 4 + place
            slope_ref[where] = half_up + (0.5 * u) * (1.0 - bent * bent) * (
                scale * (1.0 + (3.0 * 0.044715) * square)
            )
            stored.append(
                pltpu.make_async_copy(
                    slope_ref.at[where], slope_out.at[where], sem.at[17 + flip]
                )
            )
            stored[-1].start()
            if flip % 2 == 0:
                u = dot_nn(both_ref[rows:], weights)
                bent = jnp.tanh(scale * (u + 0.044715 * (u * u * u)))
                far_ref[:, lanes] = (0.5 * u * (1.0 + bent)).astype(bf16)
        wait_all(stored)

    outs = [
        ((rows, 4 * block), bf16),
        ((rows, 4 * block), bf16),
        ((rows, 4 * block), bf16),
        ((2, rows, width // 2), bf16),
        ((width, 8 * block), bf16),
        ((8, rows, block), f32),
    ]
    scratch = [
        pltpu.VMEM((width, 8 * block), bf16),
        pltpu.VMEM((8, rows, block), f32),
        pltpu.VMEM((2 * rows, width), bf16),
        pltpu.SemaphoreType.DMA((25,)),
    ]
    args = (me, *pieces, h2, sib, order)
    return kernel(body, "climb", outs, args, "s" + "a" * 8 + "vvv", scratch, 26, 2)


def vector_columns(order, mine, other):
    width = order.shape[1]
    half = width // 2

    def body(order_ref, *refs):
        ins, (left, right, rows) = refs[:6], refs[6:]
        chosen = one_hot_columns(order_ref)[:, :half]
        rows[...] = jnp.zeros_like(rows)
        for place in range(3):
            rows[place : place + 1] = ins[place][0:1] + ins[3 + place][0:1]
        columns = rows[...].T.astype(bf16)
        for part in range(2):
            left[part] = chosen[part * half : (part + 1) * half]
            right[part] = columns[part * half : (part + 1) * half]

    outs = [((2, half, half), bf16), ((2, half, 128), bf16)]
    scratch = [pltpu.VMEM((128, width), f32)]
    args = (order, *mine, *other)
    return kernel(body, "vector_columns", outs, args, "v" * 7, scratch)


class View:
    def __init__(self, array, columns=None, first=0, lead=None):
        self.array, self.first, self.lead = array, first, lead
        self.columns = columns or array.shape[-1]

    def value(self):
        array = self.array if self.lead is None else self.array[self.lead]
        return array[:, self.first : self.first + self.columns]

    def read(self, ref, first, columns):
        lanes = pl.ds(self.first + first, columns)
        return ref[:, lanes] if self.lead is None else ref[self.lead, :, lanes]


def outer(name, products, split):
    length = products[0][0].columns // 4
    total = sum(product[1].columns for product in products)
    widths = (split, total - split)
    order = ((2, 3), (1, 3), (0, 1), (0, 2))

    def body(*refs):
        ins, outs = refs[: 4 * len(products)], refs[4 * len(products) :]
        base = 0
        for number, product in enumerate(products):
            reads = [
                functools.partial(view.read, ref)
                for view, ref in zip(product, ins[4 * number : 4 * number + 4])
            ]
            columns = product[1].columns
            step = min(768, columns)
            for start in range(0, columns, step):
                for first in range(0, 4 * length, 384):
                    value = dot_tn(reads[0](first, 384), reads[1](start, step))
                    value += dot_tn(reads[2](first, 384), reads[3](start, step))
                    for block in range(first // length, (first + 384) // length):
                        part = value[block * length - first : (block + 1) * length - first]
                        for half in range(2):
                            low = max(base + start, half * split)
                            high = min(base + start + step, split + half * (total - split))
                            if high <= low:
                                continue
                            piece = part[:, low - base - start : high - base - start]
                            out_lanes = pl.ds(low - half * split, high - low)
                            for out in (half, 2 + half):
                                if block in order[out]:
                                    outs[out][order[out].index(block), :, out_lanes] = piece.astype(
                                        outs[out].dtype
                                    )
            base += columns

    outs = [
        ((2, length, widths[out % 2]), bf16 if out < 2 else f32) for out in range(4)
    ]
    args = [view.array for product in products for view in product]
    return kernel(body, name, outs, args, "v" * len(args))


def descend(me, pieces, slope, df):
    rows, width = df.shape
    block = slope.shape[2]

    def body(me_ref, *refs):
        blocks, refs = refs[:8], refs[8:]
        slope_in, df_ref, du_ref, down_ref, w_down, slope_ref, sem = refs
        copies = [[] for _ in range(8)]
        for flip, side, part in each_block(blocks):
            lanes = pl.ds(side * (width // 2), width // 2)
            place = (flip % 2) * 4 + flip // 2
            target = w_down.at[pl.ds(place * block, block), lanes]
            copies[place].append(
                pltpu.make_async_copy(part, target, sem.at[place * 2 + side])
            )
        for place, pair in enumerate(copies):
            pair.append(
                pltpu.make_async_copy(
                    slope_in.at[place], slope_ref.at[place], sem.at[17 + place]
                )
            )
            start_all(pair)
        for place in range(8):
            wait_all(copies[place])
            flip = place % 4 * 2 + place // 4
            start = pl.multiple_of((me_ref[0] ^ flip) * block, block)
            dg = dot_nt(df_ref[...], w_down[pl.ds(place * block, block)])
            du_ref[:, pl.ds(start, block)] = (dg * slope_ref[place]).astype(bf16)
        stored = pltpu.make_async_copy(w_down, down_ref, sem.at[16])
        stored.start()
        stored.wait()

    outs = [((rows, 8 * block), bf16), ((8 * block, width), bf16)]
    scratch = [
        pltpu.VMEM((8 * block, width), bf16),
        pltpu.VMEM((8, rows, block), f32),
        pltpu.SemaphoreType.DMA((25,)),
    ]
    args = (me, *pieces, slope, df)
    return kernel(body, "descend", outs, args, "s" + "a" * 9 + "v", scratch, 24, 1)


def unclimb(w_up, du, picked, added, gate, back_rows, vec):
    rows, width = picked.shape

    def body(up_ref, du_ref, x_ref, add_ref, gate_ref, dy_ref, vec_ref, dm_ref, da_ref, dg_ref):
        dh = dot_nt(du_ref[...], up_ref[...])
        middle = x_ref[...].astype(f32) + add_ref[...]
        inverse = lax.rsqrt(mean_last(middle * middle) + norm_eps)
        unit = middle * inverse
        dg_ref[...] = jnp.broadcast_to(sum_rows(dh * unit), dg_ref.shape)
        scaled = dh * vec_ref[1:2]
        dm = inverse * (scaled - unit * mean_last(scaled * unit))
        dm_ref[...] = dm
        da_ref[...] = (gate_ref[:, 0:1] * dy_ref[...].astype(f32) + dm).astype(bf16)

    outs = [((rows, width), f32), ((rows, width), bf16), ((8, width), f32)]
    args = (w_up, du, picked, added, gate, back_rows, vec)
    return kernel(body, "unclimb", outs, args, "v" * 7)


def unattend(w_out, da, qkv, probs):
    rows, width = da.shape
    top = probs.shape[2]
    seqs, pairs = rows // top, width // PAIR

    def body(out_ref, da_ref, qkv_ref, prob_ref, dqkv_ref, do_ref):
        do_ref[...] = dot_nt(da_ref[...], out_ref[...]).astype(bf16)
        masks, masks_f = head_masks(bf16), head_masks(f32)
        for seq in range(seqs):
            here = pl.ds(seq * top, top)
            for pair in range(pairs):
                lanes = [pl.ds(part * width + pair * PAIR, PAIR) for part in range(3)]
                q, k, v = (qkv_ref[here, part] for part in lanes)
                do = two_heads(do_ref[here, pl.ds(pair * PAIR, PAIR)], masks)
                probs = prob_ref[seq * pairs + pair]
                dprobs = dot_nt(do, v)
                dscores = probs * (dprobs - jnp.sum(dprobs * probs, axis=-1, keepdims=True))
                dscores = dscores.astype(bf16)
                dq = one_pair(dot_nn(dscores, k), masks_f) * head_scale
                dk = dot_tn(dscores, two_heads(q, masks)) * head_scale
                dv = dot_tn(probs.astype(bf16), do)
                for part, value in zip(lanes, (dq, dk, dv)):
                    dqkv_ref[here, part] = value.astype(bf16)

    scratch = [pltpu.VMEM((rows, width), bf16)]
    outs = [((rows, 3 * width), bf16)]
    return kernel(body, "unattend", outs, (w_out, da, qkv, probs), "vvvv", scratch)[0]


def finish_mlp(w_down, own, send, picked, added, gate, back_rows):
    rows, width = picked.shape
    half = w_down.shape[0] // 2

    def body(down_ref, own_ref, send_ref, x_ref, add_ref, gate_ref, dy_ref, *outs):
        new_ref, dlogit_ref, dr_ref = outs
        out = dot_nn(own_ref[:, :half], down_ref[:half])
        out += dot_nn(send_ref[:, :half], down_ref[half:])
        both = add_ref[...] + out
        x = x_ref[...].astype(f32)
        gate = gate_ref[:, 0:1]
        new_ref[...] = (x + gate * both).astype(bf16)
        dlogit = jnp.sum(dy_ref[...].astype(f32) * both, axis=-1, keepdims=True)
        dlogit = dlogit * gate * (1.0 - gate)
        dlogit_ref[...] = jnp.broadcast_to(dlogit, dlogit_ref.shape)
        dr_ref[...] = jnp.broadcast_to(sum_rows(dlogit * x), dr_ref.shape)

    outs = [((rows, width), bf16), ((rows, 128), f32), ((8, width), f32)]
    args = (w_down, own, send, picked, added, gate, back_rows)
    return kernel(body, "finish_mlp", outs, args, "v" * 7)


def finish_rows(w_qkv, dqkv, picked, back_rows, dmiddle, dlogit, vec):
    rows, width = picked.shape

    def body(all_ref, dqkv_ref, x_ref, dy_ref, dm_ref, dlogit_ref, vec_ref, grad_ref, dg_ref):
        dh = dot_nt(dqkv_ref[...], all_ref[...])
        x = x_ref[...].astype(f32)
        inverse = lax.rsqrt(mean_last(x * x) + norm_eps)
        unit = x * inverse
        dg_ref[...] = jnp.broadcast_to(sum_rows(dh * unit), dg_ref.shape)
        scaled = dh * vec_ref[0:1]
        dx = inverse * (scaled - unit * mean_last(scaled * unit))
        grad = dy_ref[...].astype(f32) + dm_ref[...] + dx + dlogit_ref[:, 0:1] * vec_ref[2:3]
        grad_ref[...] = grad.astype(bf16)

    outs = [((rows, width), bf16), ((8, width), f32)]
    args = (w_qkv, dqkv, picked, back_rows, dmiddle, dlogit, vec)
    return kernel(body, "finish_rows", outs, args, "v" * 7)


def join_z(z, own, others, split):
    rows, width = own.shape

    def body(z_ref, *refs):
        ins, left_ref, right_ref, total = refs[:4], *refs[4:]
        for flip, block in enumerate(ins):
            start = pl.multiple_of((z_ref[0] ^ flip) * rows, rows)
            total[pl.ds(start, rows)] = block[...].astype(f32)
        left_ref[...] = total[:, :split].astype(bf16)
        right_ref[...] = total[:, split:].astype(bf16)

    outs = [((4 * rows, split), bf16), ((4 * rows, width - split), bf16)]
    scratch = [pltpu.VMEM((4 * rows, width), f32)]
    return kernel(body, "join_z", outs, (z, own, *others), "svvvv", scratch)


def join_z_pairs(z, left, right, near_l, near_r, others):
    rows, width = left.shape

    def body(z_ref, *refs):
        mine, others, outs = refs[:4], refs[4:7], refs[7:]
        for flip in range(4):
            start = pl.ds(pl.multiple_of((z_ref[0] ^ flip) * rows, rows), rows)
            for place in range(4):
                block = others[flip - 1][place] if flip else mine[place][...]
                outs[place // 2][place % 2, start] = block

    outs = [((2, 4 * rows, width), bf16)] * 2
    args = (z, left, near_l, right, near_r, *others)
    return kernel(body, "join_z_pairs", outs, args, "svvvvvvv")


def add_z_pairs(z, keep_l, keep_r, other_l, other_r):
    pair, rows, width = keep_l.shape
    part = rows // 4

    def body(z_ref, keep_l, keep_r, other_l, other_r, mine, send, total):
        for half, (keep, other) in enumerate(((keep_l, other_l), (keep_r, other_r))):
            for place in range(pair):
                total[half * pair + place] = keep[place] + other[place].astype(f32)
        for flip in range(4):
            start = pl.multiple_of((z_ref[0] ^ flip) * part, part)
            out = (mine, send)[flip % 2]
            out[flip // 2] = total[:, pl.ds(start, part)].astype(out.dtype)

    outs = [((2, 4, part, width), f32), ((2, 4, part, width), bf16)]
    scratch = [pltpu.VMEM((4, rows, width), f32)]
    args = (z, keep_l, keep_r, other_l, other_r)
    return kernel(body, "add_z_pairs", outs, args, "svvvv", scratch)


def add_four(mine, other):
    def body(mine, other, send_l, send_r, keep):
        def total(place):
            return mine[place] + other[place].astype(f32)

        width = mine.shape[2]
        keep[:, :width] = total(0)
        keep[:, width:] = total(2)
        send_l[...] = total(1).astype(bf16)
        send_r[...] = total(3).astype(bf16)

    _, rows, width = mine.shape
    outs = [((rows, width), bf16)] * 2 + [((rows, 2 * width), f32)]
    return kernel(body, "add_four", outs, (mine, other), "vv")


def add_pairs(keep_l, keep_r, other_l, other_r):
    def body(keep_l, keep_r, other_l, other_r, send_l, send_r, left, right):
        for keep, other, send, mine in (
            (keep_l, other_l, send_l, left),
            (keep_r, other_r, send_r, right),
        ):
            send[...] = (keep[1] + other[1].astype(f32)).astype(bf16)
            mine[...] = keep[0] + other[0].astype(f32)

    shapes = [keep_l.shape[1:], keep_r.shape[1:]]
    outs = [(shape, kind) for kind in (bf16, f32) for shape in shapes]
    return kernel(body, "add_pairs", outs, (keep_l, keep_r, other_l, other_r), "vvvv")


def add_split(z, keep_l, keep_r, other_l, other_r):
    rows, split = keep_l.shape
    width = split + keep_r.shape[1]
    part = rows // 4

    def body(z_ref, keep_l, keep_r, other_l, other_r, mine, send, total):
        total[:, :split] = keep_l[...] + other_l[...].astype(f32)
        total[:, split:] = keep_r[...] + other_r[...].astype(f32)
        for flip in range(4):
            start = pl.multiple_of((z_ref[0] ^ flip) * part, part)
            out = (mine, send)[flip % 2]
            out[flip // 2] = total[pl.ds(start, part)].astype(out.dtype)

    outs = [((2, part, width), f32), ((2, part, width), bf16)]
    scratch = [pltpu.VMEM((rows, width), f32)]
    args = (z, keep_l, keep_r, other_l, other_r)
    return kernel(body, "add_split", outs, args, "svvvv", scratch)


def add_next(keep, other):
    def body(keep, other, mine, send):
        mine[...] = keep[0] + other[0].astype(f32)
        send[...] = (keep[1] + other[1].astype(f32)).astype(bf16)

    shape = keep.shape[1:]
    return kernel(body, "add_next", [(shape, f32), (shape, bf16)], (keep, other), "vv")


def settle_halves(keep, other_l, other_r):
    def body(keep, other_l, other_r, grad, square):
        width = other_l.shape[1]
        total = None
        for half, other in enumerate((other_l, other_r)):
            lanes = pl.ds(half * width, width)
            value = keep[:, lanes] + other[...].astype(f32)
            grad[:, lanes] = value
            part = jnp.sum(value * value)
            total = part if total is None else total + part
        square[...] = jnp.full(square.shape, total)

    outs = [(keep.shape, f32), ((8, 128), f32)]
    return kernel(body, "settle_halves", outs, (keep, other_l, other_r), "vvv")


def settle_z(mine, other):
    rows, width = mine.shape

    def body(mine, other, grad, square, last, turned):
        value = mine[...] + other[...].astype(f32)
        grad[...] = value
        square[...] = jnp.full(square.shape, jnp.sum(value * value))
        turned[...] = jnp.zeros_like(turned)
        turned[:rows] = value[:, width - 128 :]
        last[...] = turned[...].T[:8]

    outs = [(mine.shape, f32), ((8, 128), f32), ((8, 128), f32)]
    scratch = [pltpu.VMEM((128, 128), f32)]
    return kernel(body, "settle_z", outs, (mine, other), "vv", scratch)


def update(squares, limit, grads, states, vec_grad, vec_states):
    count = len(grads)

    def body(square_ref, *refs):
        grad_refs, refs = refs[:count], refs[count:]
        state_refs, refs = refs[: 3 * count], refs[3 * count :]
        vec_ref, vec_m, vec_v, norm_ref, out_refs = *refs[:4], refs[4:]
        norm = jnp.sqrt(jnp.sum(square_ref[...], axis=0, keepdims=True)[:, 0:1])
        norm_ref[...] = jnp.broadcast_to(norm, norm_ref.shape)
        factor = jnp.minimum(1.0, limit / (norm + 1e-06))
        for place in range(count):
            w, m, v = (ref[...] for ref in state_refs[3 * place : 3 * place + 3])
            grad = grads[place].read(grad_refs[place], 0, grads[place].columns) * factor
            for ref, value in zip(out_refs[3 * place :], adam_update(w, grad, m, v)):
                ref[...] = value
        grad = vec_ref[:3, : vec_m.shape[1]] * factor
        first, second = moment_update(grad, vec_m[...], vec_v[...])
        out_refs[-2][...] = first
        out_refs[-1][...] = second

    flat = [array for state in states for array in state]
    outs = [((8, 128), f32)] + [(array.shape, f32) for array in (*flat, *vec_states)]
    args = (squares, *(grad.array for grad in grads), *flat, vec_grad, *vec_states)
    return kernel(body, "update", outs, args, "v" * len(args), (), 32)


class Steps:
    def __init__(self, chain):
        self.chain = chain
        self.result = None
        self.launch(next(chain))

    def launch(self, step):
        self.flips = [flip for _, flip in step]
        self.given = [array for array, _ in step]

    def advance(self, arrays):
        try:
            self.launch(self.chain.send(arrays))
        except StopIteration as stop:
            self.flips, self.given, self.result = (), (), stop.value


def slot(chains, value):
    arrays = [
        [swap(array, flip) for array, flip in zip(chain.given, chain.flips)] for chain in chains
    ]
    arrays, value = lax.optimization_barrier((arrays, value))
    for chain, array in zip(chains, arrays):
        chain.advance(array)
    return value


def ready(chains, value):
    arrays, value = lax.optimization_barrier(([chain.given for chain in chains], value))
    for chain, array in zip(chains, arrays):
        chain.given = array
    return value


def swap(array, bit):
    count = lax.axis_size("wide") * lax.axis_size("narrow")
    return lax.ppermute(array, AXES, [(i, i ^ bit) for i in range(count)])


def exchange(*arrays):
    return (yield [(array, 4) for array in arrays])


def around_z(shard, at_once):
    if at_once:
        return (yield [(shard, flip) for flip in (1, 2, 3)])
    (two,) = yield [(shard, 2)]
    (both,) = yield [(jnp.stack([shard, two]), 1)]
    return both[0], two, both[1]


def gather(shard, z, split, at_once):
    others = yield from around_z(shard, at_once)
    left, right = join_z(z, shard, others, split)
    near_l, near_r = yield [(left, 8), (right, 16)]
    return (yield from spread(jnp.stack([left, near_l]), jnp.stack([right, near_r])))


def gather_pairs(shard, z):
    half = shard.shape[1] // 2
    left, right = shard[:, :half], shard[:, half:]
    near_l, near_r = yield [(left, 8), (right, 16)]
    others = yield from around_z(jnp.stack([left, near_l, right, near_r]), False)
    keep_l, keep_r = join_z_pairs(z, left, right, near_l, near_r, others)
    return (yield from spread(keep_l, keep_r))


def spread(keep_l, keep_r):
    far_l, far_r, *near = yield [(keep_l, 16), (keep_r, 8), (keep_l, 4), (keep_r, 4)]
    far = yield [(far_l, 4), (far_r, 4)]
    return (keep_l, keep_r, far_l, far_r, *near, *far)


def scatter(z, send_l, send_r, keep_l, keep_r):
    other_l, other_r = yield [(send_l, 16), (send_r, 8)]
    send_l, send_r, left, right = add_pairs(keep_l, keep_r, other_l, other_r)
    other_l, other_r = yield [(send_l, 8), (send_r, 16)]
    mine, send = add_split(z, left, right, other_l, other_r)
    (other,) = yield [(send, 1)]
    mine, send = add_next(mine, other)
    (other,) = yield [(send, 2)]
    return settle_z(mine, other)


def scatter_pairs(z, send_l, send_r, keep_l, keep_r):
    other_l, other_r = yield [(send_l, 16), (send_r, 8)]
    mine, send = add_z_pairs(z, keep_l, keep_r, other_l, other_r)
    (other,) = yield [(send, 1)]
    mine, send = add_next(mine, other)
    (other,) = yield [(send, 2)]
    send_l, send_r, keep = add_four(mine, other)
    other_l, other_r = yield [(send_l, 8), (send_r, 16)]
    return settle_halves(keep, other_l, other_r)


def cut(whole, split):
    blocks = whole.reshape(8, whole.shape[0] // 8, whole.shape[1])
    sides = (blocks[..., :split], blocks[..., split:])
    return tuple(
        jnp.stack([sides[flip[2]][flip[0] * 4 + flip[1] * 2 + core] for flip in flips])
        for core in range(2)
        for flips in GROUPS
    )


def uncut(own, send):
    parts = jnp.stack([array.reshape(array.shape[0], 4, -1) for array in (own, send)], axis=2)
    return parts.reshape(own.shape[0], -1)


def per_device(
    paired,
    tokens,
    cotangent,
    segments,
    picks,
    w_qkv,
    w_out,
    w_up,
    w_down,
    vectors,
    m_qkv,
    m_out,
    m_up,
    m_down,
    m_vectors,
    v_qkv,
    v_out,
    v_up,
    v_down,
    v_vectors,
):
    devices_all = lax.axis_size("wide") * lax.axis_size("narrow")
    lane = lax.axis_index(AXES)
    seq_count, top_count = picks.shape
    seq_len = segments.shape[1]
    model_width = tokens.shape[1]
    qkv_width = w_qkv.shape[1]
    ff_width = w_up.shape[1]
    shard_width = vectors.shape[1]
    split_a, split_b, split_c = 2 * model_width, ff_width // 2, model_width // 2
    z = (lane & 3).reshape(1)
    me = (lane >> 2).reshape(1) if paired else jnp.zeros((1,), jnp.int32)

    chunk_a = gather_input(w_qkv, w_out, vectors)
    chunk_b = w_up.astype(bf16)
    chunk_c = w_down.astype(bf16)

    def start(chain, *args):
        return Steps(chain(*args)) if paired else None

    def tick(chains, value):
        return slot(chains, value) if paired else value

    def stage(chains, value):
        return ready(chains, value) if paired else value

    def whole(take, chunk, split):
        if paired:
            return take.result
        return cut(lax.all_gather(chunk, AXES, axis=0, tiled=True), split)

    hot = picks[:, :, None] == jnp.arange(seq_len, dtype=jnp.int32)[None, None, :]
    hot_low = hot.astype(bf16)
    tok_blocks = tokens.reshape(seq_count, seq_len, model_width)
    back_blocks = cotangent.reshape(seq_count, seq_len, model_width)

    def pick(blocks):
        rows = jnp.einsum("skl,sld->skd", hot_low, blocks, preferred_element_type=f32)
        return rows.astype(bf16).reshape(-1, model_width)

    def place(blocks, rows):
        rows = rows.reshape(seq_count, top_count, model_width)
        spread = jnp.einsum("skl,skd->sld", hot_low, rows, preferred_element_type=f32).astype(bf16)
        taken = jnp.any(hot, axis=1)
        return jnp.where(taken[:, :, None], spread, blocks).reshape(-1, model_width)

    take_a = start(gather, chunk_a, z, split_a, True)
    take_c = start(gather_pairs, chunk_c, z)
    picked = pick(tok_blocks)
    back_rows = pick(back_blocks)
    seg_sel = jnp.sum(jnp.where(hot, segments[:, None, :], 0), axis=-1)
    seg_row, seg_col = seg_sel[:, None, :], seg_sel[:, :, None]
    spot = jnp.arange(model_width, dtype=jnp.int32)
    half, eighth = model_width // 2, model_width // 8
    flip = spot % half // eighth * 2 + spot // half
    order = ((me[0] ^ flip) * eighth + spot % eighth)[None]
    inputs = (picked, back_rows, seg_row, seg_col, order, chunk_b)
    inputs = tick([take_a], inputs)
    take_b = start(gather, inputs[-1], z, split_b, False)
    inputs = tick([take_a, take_b, take_c], inputs[:-1])
    inputs = tick([take_a, take_b], inputs)
    inputs = tick([take_a, take_b, take_c], inputs)

    all_a = whole(take_a, chunk_a, split_a)
    picked, back_rows = inputs[:2]
    order = inputs[4]
    state = attend(me, all_a, *inputs)
    state = tick([take_b, take_c], state)
    own, send, df, gate, vec, added, h2, all_qkv, all_out, qkv, probs = state
    early = start(exchange, send)
    h2 = stage([take_c], h2)
    h2 = tick([take_b, early], h2)
    (sib,) = early.result if paired else (send,)
    all_b = whole(take_b, chunk_b, split_b)
    g_own, g_send, g_sib, h2_pair, all_up, slope = climb(me, all_b, h2, sib, order)

    def give(chain, name, products, split):
        if paired:
            return Steps(chain(z, *outer(name, products, split)))
        grads = [dot_tn(uncut(one.value(), far.value()), two.value()) for one, two, far, _ in products]
        grad = jnp.concatenate(grads, axis=1)
        grad = lax.psum_scatter(grad, AXES, scatter_dimension=0, tiled=True)
        return grad, jnp.full((8, 128), jnp.sum(grad * grad))

    df_sib = jnp.concatenate([sib[2], sib[3]], axis=1)
    left_c = View(g_sib) if paired else View(g_send)
    give_c = give(
        scatter_pairs, "outer_c", [(View(g_own), View(df), left_c, View(df_sib))], split_c
    )
    slope = stage([give_c], slope)
    slope = tick([take_c], slope)
    slope = tick([take_c], slope)
    all_c = whole(take_c, chunk_c, split_c)
    du, all_down = descend(me, all_c, slope, df)
    dmiddle, da, dg2 = unclimb(all_up, du, picked, added, gate, back_rows, vec)
    new_rows, dlogit, dr = finish_mlp(
        all_down, g_own, g_send, picked, added, gate, back_rows
    )
    du, da, dmiddle, new_rows, dlogit = tick([give_c], (du, da, dmiddle, new_rows, dlogit))
    late_u = start(exchange, du)
    dqkv = unattend(all_out, da, qkv, probs)
    dqkv = tick([late_u], dqkv)
    (du_sib,) = late_u.result if paired else (du,)
    late_q = start(exchange, dqkv, da)
    views = [View(h2_pair, lead=place) for place in range(2)]
    if not paired:
        cols = h2.reshape(h2.shape[0], 4, 2, -1)
        views = [View(cols[:, :, core].reshape(h2.shape[0], -1)) for core in range(2)]
    give_b = give(
        scatter_pairs, "outer_b", [(views[0], View(du), views[1], View(du_sib))], split_b
    )
    dqkv = stage([give_b, give_c], dqkv)
    grad_rows, dg1 = finish_rows(all_qkv, dqkv, picked, back_rows, dmiddle, dlogit, vec)
    late_v = start(exchange, dg1, dg2, dr)
    dqkv = stage([late_v], dqkv)
    dqkv = tick([late_q, late_v], dqkv)
    dqkv_sib, da_sib = late_q.result if paired else (dqkv, da)
    products = [
        (View(own, lead=0), View(dqkv), View(sib, lead=0), View(dqkv_sib)),
        (View(own, lead=1), View(da), View(sib, lead=1), View(da_sib)),
    ]
    if paired:
        left, right = vector_columns(order, (dg1, dg2, dr), late_v.result)
        products.append(tuple(View(array, lead=part) for part in range(2) for array in (left, right)))
    give_a = give(scatter, "outer_a", products, split_a)
    grad_rows = stage([give_a], grad_rows)
    grad_rows = tick([give_b, give_c], grad_rows)
    grad_rows, new_rows = stage([give_b, give_c], (grad_rows, new_rows))
    mixed_rows = place(tok_blocks, new_rows)
    grad_rows, mixed_rows = tick([give_a], (grad_rows, mixed_rows))
    grad_rows = stage([give_a], grad_rows)
    grad_rows = tick([give_b, give_c], grad_rows)
    grad_rows = stage([give_b, give_c], grad_rows)
    grad_rows = tick([give_a, give_c], grad_rows)
    grad_rows = stage([give_a], grad_rows)
    input_grad = place(back_blocks, grad_rows)
    input_grad = tick([give_a, give_b], input_grad)
    input_grad = stage([give_a, give_b], input_grad)
    input_grad = tick([give_a, give_b], input_grad)
    if paired:
        give_a, give_b, give_c = give_a.result, give_b.result, give_c.result
        vec_grad = give_a[2]
        local_sq = give_a[1] + give_b[1] + give_c[1]
    else:
        rows = jnp.stack([dg1[0], dg2[0], dr[0]], axis=0)
        rows = lax.psum_scatter(rows, AXES, scatter_dimension=1, tiled=True)
        vec_grad = jnp.pad(rows, ((0, 5), (0, 128 - shard_width)))
        local_sq = give_a[1] + give_b[1] + give_c[1] + jnp.sum(rows * rows)
    squares = jnp.broadcast_to(local_sq[:1], (devices_all, 128))
    squares = lax.all_to_all(squares, AXES, 0, 0, tiled=True)
    params_all = 4 * model_width * model_width + 2 * model_width * ff_width + 3 * model_width
    selected_all = seq_count * top_count * devices_all
    clip_limit = limit_scale * math.sqrt(params_all * selected_all)
    norm, *news = update(
        squares,
        clip_limit,
        [
            View(give_a[0], qkv_width),
            View(give_a[0], model_width, qkv_width),
            View(give_b[0]),
            View(give_c[0]),
        ],
        [
            (w_qkv, m_qkv, v_qkv),
            (w_out, m_out, v_out),
            (w_up, m_up, v_up),
            (w_down, m_down, v_down),
        ],
        vec_grad,
        (m_vectors, v_vectors),
    )
    return (
        mixed_rows,
        input_grad,
        norm[0, 0],
        *news[0:12:3],
        *news[1:12:3],
        news[12],
        *news[2:12:3],
        news[13],
    )


def solution(mesh):
    placed = (
        P(("wide", "narrow"), None),
        P(("wide", "narrow"), None),
        P(("wide", "narrow"), None),
        P(("wide", "narrow"), None),
        P(("wide", "narrow"), None),
        P(("wide", "narrow"), None),
        P(("wide", "narrow"), None),
        P(("wide", "narrow"), None),
        P(None, ("wide", "narrow")),
        P(("wide", "narrow"), None),
        P(("wide", "narrow"), None),
        P(("wide", "narrow"), None),
        P(("wide", "narrow"), None),
        P(None, ("wide", "narrow")),
        P(("wide", "narrow"), None),
        P(("wide", "narrow"), None),
        P(("wide", "narrow"), None),
        P(("wide", "narrow"), None),
        P(None, ("wide", "narrow")),
    )
    paired = mesh.shape["wide"] == 8 and mesh.shape["narrow"] == 4
    return jax.shard_map(
        functools.partial(per_device, paired),
        mesh=mesh,
        in_specs=placed,
        out_specs=(
            P(("wide", "narrow"), None),
            P(("wide", "narrow"), None),
            P(),
            P(("wide", "narrow"), None),
            P(("wide", "narrow"), None),
            P(("wide", "narrow"), None),
            P(("wide", "narrow"), None),
            P(("wide", "narrow"), None),
            P(("wide", "narrow"), None),
            P(("wide", "narrow"), None),
            P(("wide", "narrow"), None),
            P(None, ("wide", "narrow")),
            P(("wide", "narrow"), None),
            P(("wide", "narrow"), None),
            P(("wide", "narrow"), None),
            P(("wide", "narrow"), None),
            P(None, ("wide", "narrow")),
        ),
        check_vma=False,
    )
```

```python
import functools
import math

import jax
import jax.numpy as jnp
from jax import lax
from jax.experimental import pallas as pl
from jax.experimental.pallas import tpu as pltpu
from jax.sharding import PartitionSpec as P

HEAD_DIM = 64


norm_eps = 1e-06
beta_one = 0.9
beta_two = 0.999
adam_eps = 1e-08
learn_rate = 0.03
decay_rate = 0.1
adam_step = 10
limit_scale = 0.01
masked_out = -1e30
AXES = ("wide", "narrow")


def moment_update(grad_part, first, second):
    first_new = beta_one * first + (1.0 - beta_one) * grad_part
    second_new = beta_two * second + (1.0 - beta_two) * grad_part * grad_part
    return (first_new, second_new)


def adam_update(master, grad_part, first, second):
    first_new, second_new = moment_update(grad_part, first, second)
    first_hat = first_new / (1.0 - beta_one**adam_step)
    second_hat = second_new / (1.0 - beta_two**adam_step)
    master_new = master - learn_rate * (
        first_hat / (jnp.sqrt(second_hat) + adam_eps) + decay_rate * master
    )
    return (master_new, first_new, second_new)


f32, bf16 = jnp.float32, jnp.bfloat16
PAIR = 2 * HEAD_DIM
head_scale = HEAD_DIM ** (-0.5)
KEEP_L = ((0, 0, 0), (0, 1, 0))
KEEP_R = ((0, 0, 1), (1, 0, 1))
FAR_L = ((1, 0, 0), (1, 1, 0))
FAR_R = ((0, 1, 1), (1, 1, 1))
GROUPS = (KEEP_L, KEEP_R, FAR_L, FAR_R)
PIECES = "aaaaaaaavv"


def kernel(body, name, outs, args, kinds, scratch=(), limit=24, loose=0):
    spaces = {"s": pltpu.SMEM, "v": pltpu.VMEM, "h": pltpu.VMEM, "a": pltpu.HBM}
    held = len(outs) - loose
    return pl.pallas_call(
        body,
        out_shape=[
            jax.ShapeDtypeStruct(*out) if place < held else pltpu.HBM(*out)
            for place, out in enumerate(outs)
        ],
        in_specs=[pl.BlockSpec(memory_space=spaces[kind]) for kind in kinds],
        out_specs=[
            pl.BlockSpec(memory_space=pltpu.VMEM if place < held else pltpu.HBM)
            for place in range(len(outs))
        ],
        scratch_shapes=list(scratch),
        compiler_params=pltpu.CompilerParams(vmem_limit_bytes=limit << 20),
        cost_estimate=pl.CostEstimate(flops=1, bytes_accessed=1, transcendentals=0),
        name=name,
    )(
        *(
            pltpu.with_memory_space_constraint(arg, pltpu.HBM) if kind in "ah" else arg
            for arg, kind in zip(args, kinds)
        )
    )


def each_block(pieces):
    for core in range(2):
        for group, flips in enumerate(GROUPS):
            for place, flip in enumerate(flips):
                if core == 0 and group < 2:
                    ref = pieces[2 * group + place]
                else:
                    ref = pieces[core * 4 + group + 2].at[place]
                yield flip[0] * 4 + flip[1] * 2 + core, flip[2], ref


def start_all(copies):
    for copy in copies:
        copy.start()


def wait_all(copies):
    for copy in copies:
        copy.wait()


def fetch(pieces, me, sem, base, left, right):
    copies = []
    for flip, half, block in each_block(pieces):
        rows = block.shape[0]
        start = pl.multiple_of((me ^ flip) * rows, rows)
        for target, column, out_column, width in (left, right)[half]:
            copies.append(
                pltpu.make_async_copy(
                    block.at[:, pl.ds(column, width)],
                    target.at[pl.ds(start, rows), pl.ds(out_column, width)],
                    sem.at[base + len(copies)],
                )
            )
    return copies


def dot_nt(left, right):
    return lax.dot_general(left, right, (((1,), (1,)), ((), ())), preferred_element_type=f32)


def dot_tn(left, right):
    return lax.dot_general(left, right, (((0,), (0,)), ((), ())), preferred_element_type=f32)


def dot_nn(left, right):
    return jnp.dot(left, right, preferred_element_type=f32)


def mean_last(array):
    return jnp.mean(array, axis=-1, keepdims=True)


def sum_rows(array):
    return jnp.sum(array, axis=0, keepdims=True)


def head_masks(dtype):
    lanes = lax.broadcasted_iota(jnp.int32, (1, PAIR), 1)
    first = (lanes < HEAD_DIM).astype(f32).astype(dtype)
    return first, (1 - first).astype(dtype)


def two_heads(pair, masks):
    return jnp.concatenate([pair * masks[0], pair * masks[1]], axis=0)


def one_pair(stacked, masks):
    rows = stacked.shape[0] // 2
    return stacked[:rows] * masks[0] + stacked[rows:] * masks[1]


def gather_input(w_qkv, w_out, vectors):
    rows, first = w_qkv.shape
    second = w_out.shape[1]

    def body(qkv_ref, out_ref, vec_ref, chunk_ref, turned):
        chunk_ref[:, :first] = qkv_ref[...].astype(bf16)
        chunk_ref[:, first : first + second] = out_ref[...].astype(bf16)
        turned[...] = jnp.zeros_like(turned)
        turned[:3] = vec_ref[...]
        same = lax.broadcasted_iota(jnp.int32, (rows, rows), 0) == lax.broadcasted_iota(
            jnp.int32, (rows, rows), 1
        )
        columns = dot_nt(same.astype(f32).astype(bf16), turned[...].astype(bf16))
        chunk_ref[:, first + second :] = columns.astype(bf16)

    outs = [((rows, first + second + 128), bf16)]
    scratch = [pltpu.VMEM((128, rows), f32)]
    return kernel(body, "gather_input", outs, (w_qkv, w_out, vectors), "hhh", scratch)[0]


def attend(me, pieces, picked, back_rows, seg_row, seg_col, order):
    rows, width = picked.shape
    seqs = seg_row.shape[0]
    top = rows // seqs
    pairs = width // PAIR
    first = pieces[0].shape[1]
    rest = 3 * width - first
    spare = pieces[2].shape[1] - rest - width

    def body(me_ref, *refs):
        blocks, refs = refs[:10], refs[10:]
        x_ref, dy_ref, seg_row_ref, seg_col_ref, order_ref = refs[:5]
        own_ref, send_ref, df_ref, gate_ref, vec_ref, add_ref, h2_ref = refs[5:12]
        all_ref, out_ref, qkv_out, prob_out = refs[12:16]
        w_qkv, w_out, w_vec, qkv_ref, prob_ref, att_ref, sem = refs[16:]
        vec_copies = fetch(blocks, me_ref[0], sem, 0, (), ((w_vec, rest + width, 0, spare),))
        left = fetch(blocks, me_ref[0], sem, 8, ((w_qkv, 0, 0, first),), ())
        right = fetch(blocks, me_ref[0], sem, 16, (), ((w_qkv, 0, first, rest),))
        out_copies = fetch(blocks, me_ref[0], sem, 24, (), ((w_out, rest, 0, width),))
        start_all(vec_copies + left + right + out_copies)
        wait_all(vec_copies)
        vec = w_vec[...].astype(f32).T[:8]
        vec_ref[...] = vec
        x = x_ref[...].astype(f32)
        h1 = (x * lax.rsqrt(mean_last(x * x) + norm_eps) * vec[0:1]).astype(bf16)
        for copies, start, count in ((left, 0, first), (right, first, rest)):
            wait_all(copies)
            for part in range(start, start + count, 384):
                lanes = pl.ds(part, 384)
                qkv_ref[:, lanes] = dot_nn(h1, w_qkv[:, lanes]).astype(bf16)
        stored = [
            pltpu.make_async_copy(w_qkv, all_ref, sem.at[32]),
            pltpu.make_async_copy(qkv_ref, qkv_out, sem.at[33]),
            pltpu.make_async_copy(w_out, out_ref, sem.at[34]),
        ]
        wait_all(out_copies)
        start_all(stored)
        masks, masks_f = head_masks(bf16), head_masks(f32)
        ordered_pairs = lax.broadcasted_iota(jnp.int32, (top, top), 1) <= lax.broadcasted_iota(
            jnp.int32, (top, top), 0
        )
        for seq in range(seqs):
            here = pl.ds(seq * top, top)
            seen = ordered_pairs & (seg_col_ref[seq] == seg_row_ref[seq])
            hidden = jnp.where(seen, 0.0, masked_out)
            hidden = jnp.concatenate([hidden, hidden], axis=0)
            for pair in range(pairs):
                q, k, v = (
                    qkv_ref[here, pl.ds(part * width + pair * PAIR, PAIR)] for part in range(3)
                )
                scores = dot_nt(two_heads(q, masks), k) * head_scale
                scores = jnp.where(hidden < 0.0, masked_out, scores)
                power = jnp.exp(scores - jnp.max(scores, axis=-1, keepdims=True))
                probs = power / jnp.sum(power, axis=-1, keepdims=True)
                prob_ref[seq * pairs + pair] = probs
                mixed = one_pair(dot_nn(probs.astype(bf16), v), masks_f)
                att_ref[here, pl.ds(pair * PAIR, PAIR)] = mixed.astype(bf16)
            group = pl.ds(seq * pairs, pairs)
            stored.append(
                pltpu.make_async_copy(prob_ref.at[group], prob_out.at[group], sem.at[35 + seq])
            )
            stored[-1].start()
        gate = jax.nn.sigmoid(jnp.sum(x * vec[2:3], axis=-1, keepdims=True))
        gate_ref[...] = jnp.broadcast_to(gate, gate_ref.shape)
        df = (gate * dy_ref[...].astype(f32)).astype(bf16)
        df_ref[...] = df
        added = dot_nn(att_ref[...], w_out[...])
        add_ref[...] = added
        middle = x + added
        h2 = (middle * lax.rsqrt(mean_last(middle * middle) + norm_eps) * vec[1:2]).astype(bf16)
        h2_ref[...] = h2
        for half in range(2):
            lanes = slice(half * (width // 2), (half + 1) * (width // 2))
            send_ref[2 + half] = df[:, lanes]
            send_ref[4 + half] = h2[:, lanes]
        chosen = one_hot_columns(order_ref)
        for place, array in enumerate((h1, att_ref[...])):
            parted = dot_nn(array, chosen).astype(bf16)
            own_ref[place] = parted[:, : width // 2]
            send_ref[place] = parted[:, width // 2 :]
        wait_all(stored)

    outs = [
        ((2, rows, width // 2), bf16),
        ((6, rows, width // 2), bf16),
        ((rows, width), bf16),
        ((rows, 128), f32),
        ((8, width), f32),
        ((rows, width), f32),
        ((rows, width), bf16),
        ((width, 3 * width), bf16),
        ((width, width), bf16),
        ((rows, 3 * width), bf16),
        ((seqs * pairs, 2 * top, top), f32),
    ]
    scratch = [
        pltpu.VMEM((width, 3 * width), bf16),
        pltpu.VMEM((width, width), bf16),
        pltpu.VMEM((width, spare), bf16),
        pltpu.VMEM((rows, 3 * width), bf16),
        pltpu.VMEM((seqs * pairs, 2 * top, top), f32),
        pltpu.VMEM((rows, width), bf16),
        pltpu.SemaphoreType.DMA((35 + seqs,)),
    ]
    args = (me, *pieces, picked, back_rows, seg_row, seg_col, order)
    return kernel(body, "attend", outs, args, "s" + PIECES + "vvvvv", scratch, 26, 4)


def one_hot_columns(order_ref):
    width = order_ref.shape[1]
    chosen = lax.broadcasted_iota(jnp.int32, (width, width), 0) == order_ref[...]
    return chosen.astype(f32).astype(bf16)


def climb(me, pieces, h2, sib, order):
    rows, width = h2.shape
    first = pieces[0].shape[1]
    block = 2 * first // 8

    def body(me_ref, *refs):
        blocks, refs = refs[:10], refs[10:]
        h2_ref, sib_ref, order_ref = refs[:3]
        own_ref, send_ref, far_ref, pair_ref, up_ref, slope_out = refs[3:9]
        w_up, slope_ref, both_ref, sem = refs[9:]
        copies = fetch(
            blocks, me_ref[0], sem, 0, ((w_up, 0, 0, first),), ((w_up, 0, first, first),)
        )
        start_all(copies)
        both_ref[:rows] = h2_ref[...]
        for half in range(2):
            lanes = pl.ds(half * (width // 2), width // 2)
            both_ref[rows:, lanes] = sib_ref[4 + half]
        chosen = one_hot_columns(order_ref)[:, : width // 2]
        parted = dot_nn(both_ref[...], chosen).astype(bf16)
        pair_ref[0] = parted[:rows]
        pair_ref[1] = parted[rows:]
        wait_all(copies)
        stored = [pltpu.make_async_copy(w_up, up_ref, sem.at[16])]
        start_all(stored)
        scale = math.sqrt(2.0 / math.pi)
        for flip in range(8):
            start = pl.multiple_of((me_ref[0] ^ flip) * block, block)
            place = flip // 2
            lanes = pl.ds(place * block, block)
            weights = w_up[:, pl.ds(start, block)]
            u = dot_nn(both_ref[:rows], weights)
            square = u * u
            bent = jnp.tanh(scale * (u + 0.044715 * (square * u)))
            half_up = 0.5 * (1.0 + bent)
            target = send_ref if flip % 2 else own_ref
            target[:, lanes] = (u * half_up).astype(bf16)
            where = (flip % 2) * 4 + place
            slope_ref[where] = half_up + (0.5 * u) * (1.0 - bent * bent) * (
                scale * (1.0 + (3.0 * 0.044715) * square)
            )
            stored.append(
                pltpu.make_async_copy(
                    slope_ref.at[where], slope_out.at[where], sem.at[17 + flip]
                )
            )
            stored[-1].start()
            if flip % 2 == 0:
                u = dot_nn(both_ref[rows:], weights)
                bent = jnp.tanh(scale * (u + 0.044715 * (u * u * u)))
                far_ref[:, lanes] = (0.5 * u * (1.0 + bent)).astype(bf16)
        wait_all(stored)

    outs = [
        ((rows, 4 * block), bf16),
        ((rows, 4 * block), bf16),
        ((rows, 4 * block), bf16),
        ((2, rows, width // 2), bf16),
        ((width, 8 * block), bf16),
        ((8, rows, block), f32),
    ]
    scratch = [
        pltpu.VMEM((width, 8 * block), bf16),
        pltpu.VMEM((8, rows, block), f32),
        pltpu.VMEM((2 * rows, width), bf16),
        pltpu.SemaphoreType.DMA((25,)),
    ]
    args = (me, *pieces, h2, sib, order)
    return kernel(body, "climb", outs, args, "s" + PIECES + "vvv", scratch, 26, 2)


def vector_columns(order, mine, other):
    width = order.shape[1]
    half = width // 2

    def body(order_ref, *refs):
        ins, (left, right, rows) = refs[:6], refs[6:]
        chosen = one_hot_columns(order_ref)[:, :half]
        rows[...] = jnp.zeros_like(rows)
        for place in range(3):
            rows[place : place + 1] = ins[place][0:1] + ins[3 + place][0:1]
        columns = rows[...].T.astype(bf16)
        for part in range(2):
            left[part] = chosen[part * half : (part + 1) * half]
            right[part] = columns[part * half : (part + 1) * half]

    outs = [((2, half, half), bf16), ((2, half, 128), bf16)]
    scratch = [pltpu.VMEM((128, width), f32)]
    args = (order, *mine, *other)
    return kernel(body, "vector_columns", outs, args, "v" * 7, scratch)


class View:
    def __init__(self, array, columns=None, first=0, lead=None):
        self.array, self.first, self.lead = array, first, lead
        self.columns = columns or array.shape[-1]

    def value(self):
        array = self.array if self.lead is None else self.array[self.lead]
        return array[:, self.first : self.first + self.columns]

    def read(self, ref, first, columns):
        lanes = pl.ds(self.first + first, columns)
        return ref[:, lanes] if self.lead is None else ref[self.lead, :, lanes]


def outer(name, products, split):
    length = products[0][0].columns // 4
    total = sum(product[1].columns for product in products)
    widths = (split, total - split)
    order = ((2, 3), (1, 3), (0, 1), (0, 2))

    def body(*refs):
        ins, outs = refs[: 4 * len(products)], refs[4 * len(products) :]
        base = 0
        for number, product in enumerate(products):
            reads = [
                functools.partial(view.read, ref)
                for view, ref in zip(product, ins[4 * number : 4 * number + 4])
            ]
            columns = product[1].columns
            step = min(768, columns)
            for start in range(0, columns, step):
                for first in range(0, 4 * length, 384):
                    value = dot_tn(reads[0](first, 384), reads[1](start, step))
                    value += dot_tn(reads[2](first, 384), reads[3](start, step))
                    for block in range(first // length, (first + 384) // length):
                        part = value[block * length - first : (block + 1) * length - first]
                        for half in range(2):
                            low = max(base + start, half * split)
                            high = min(base + start + step, split + half * (total - split))
                            if high <= low:
                                continue
                            piece = part[:, low - base - start : high - base - start]
                            out_lanes = pl.ds(low - half * split, high - low)
                            for out in (half, 2 + half):
                                if block in order[out]:
                                    outs[out][order[out].index(block), :, out_lanes] = piece.astype(
                                        outs[out].dtype
                                    )
            base += columns

    outs = [
        ((2, length, widths[out % 2]), bf16 if out < 2 else f32) for out in range(4)
    ]
    args = [view.array for product in products for view in product]
    return kernel(body, name, outs, args, "v" * len(args))


def descend(me, pieces, slope, df):
    rows, width = df.shape
    block = slope.shape[2]

    def body(me_ref, *refs):
        blocks, refs = refs[:10], refs[10:]
        slope_in, df_ref, du_ref, down_ref, w_down, slope_ref, sem = refs
        copies = [[] for _ in range(8)]
        for flip, side, part in each_block(blocks):
            lanes = pl.ds(side * (width // 2), width // 2)
            place = (flip % 2) * 4 + flip // 2
            target = w_down.at[pl.ds(place * block, block), lanes]
            copies[place].append(
                pltpu.make_async_copy(part, target, sem.at[place * 2 + side])
            )
        for place, pair in enumerate(copies):
            pair.append(
                pltpu.make_async_copy(
                    slope_in.at[place], slope_ref.at[place], sem.at[17 + place]
                )
            )
            start_all(pair)
        for place in range(8):
            wait_all(copies[place])
            flip = place % 4 * 2 + place // 4
            start = pl.multiple_of((me_ref[0] ^ flip) * block, block)
            dg = dot_nt(df_ref[...], w_down[pl.ds(place * block, block)])
            du_ref[:, pl.ds(start, block)] = (dg * slope_ref[place]).astype(bf16)
        stored = pltpu.make_async_copy(w_down, down_ref, sem.at[16])
        stored.start()
        stored.wait()

    outs = [((rows, 8 * block), bf16), ((8 * block, width), bf16)]
    scratch = [
        pltpu.VMEM((8 * block, width), bf16),
        pltpu.VMEM((8, rows, block), f32),
        pltpu.SemaphoreType.DMA((25,)),
    ]
    args = (me, *pieces, slope, df)
    return kernel(body, "descend", outs, args, "s" + PIECES + "av", scratch, 24, 1)


def unclimb(w_up, du, picked, added, gate, back_rows, vec):
    rows, width = picked.shape

    def body(up_ref, du_ref, x_ref, add_ref, gate_ref, dy_ref, vec_ref, dm_ref, da_ref, dg_ref):
        dh = dot_nt(du_ref[...], up_ref[...])
        middle = x_ref[...].astype(f32) + add_ref[...]
        inverse = lax.rsqrt(mean_last(middle * middle) + norm_eps)
        unit = middle * inverse
        dg_ref[...] = jnp.broadcast_to(sum_rows(dh * unit), dg_ref.shape)
        scaled = dh * vec_ref[1:2]
        dm = inverse * (scaled - unit * mean_last(scaled * unit))
        dm_ref[...] = dm
        da_ref[...] = (gate_ref[:, 0:1] * dy_ref[...].astype(f32) + dm).astype(bf16)

    outs = [((rows, width), f32), ((rows, width), bf16), ((8, width), f32)]
    args = (w_up, du, picked, added, gate, back_rows, vec)
    return kernel(body, "unclimb", outs, args, "v" * 7)


def unattend(w_out, da, qkv, probs):
    rows, width = da.shape
    top = probs.shape[2]
    seqs, pairs = rows // top, width // PAIR

    def body(out_ref, da_ref, qkv_ref, prob_ref, dqkv_ref, do_ref):
        do_ref[...] = dot_nt(da_ref[...], out_ref[...]).astype(bf16)
        masks, masks_f = head_masks(bf16), head_masks(f32)
        for seq in range(seqs):
            here = pl.ds(seq * top, top)
            for pair in range(pairs):
                lanes = [pl.ds(part * width + pair * PAIR, PAIR) for part in range(3)]
                q, k, v = (qkv_ref[here, part] for part in lanes)
                do = two_heads(do_ref[here, pl.ds(pair * PAIR, PAIR)], masks)
                probs = prob_ref[seq * pairs + pair]
                dprobs = dot_nt(do, v)
                dscores = probs * (dprobs - jnp.sum(dprobs * probs, axis=-1, keepdims=True))
                dscores = dscores.astype(bf16)
                dq = one_pair(dot_nn(dscores, k), masks_f) * head_scale
                dk = dot_tn(dscores, two_heads(q, masks)) * head_scale
                dv = dot_tn(probs.astype(bf16), do)
                for part, value in zip(lanes, (dq, dk, dv)):
                    dqkv_ref[here, part] = value.astype(bf16)

    scratch = [pltpu.VMEM((rows, width), bf16)]
    outs = [((rows, 3 * width), bf16)]
    return kernel(body, "unattend", outs, (w_out, da, qkv, probs), "vvvv", scratch)[0]


def finish_mlp(w_down, own, send, picked, added, gate, back_rows):
    rows, width = picked.shape
    half = w_down.shape[0] // 2

    def body(down_ref, own_ref, send_ref, x_ref, add_ref, gate_ref, dy_ref, *outs):
        new_ref, dlogit_ref, dr_ref = outs
        out = dot_nn(own_ref[:, :half], down_ref[:half])
        out += dot_nn(send_ref[:, :half], down_ref[half:])
        both = add_ref[...] + out
        x = x_ref[...].astype(f32)
        gate = gate_ref[:, 0:1]
        new_ref[...] = (x + gate * both).astype(bf16)
        dlogit = jnp.sum(dy_ref[...].astype(f32) * both, axis=-1, keepdims=True)
        dlogit = dlogit * gate * (1.0 - gate)
        dlogit_ref[...] = jnp.broadcast_to(dlogit, dlogit_ref.shape)
        dr_ref[...] = jnp.broadcast_to(sum_rows(dlogit * x), dr_ref.shape)

    outs = [((rows, width), bf16), ((rows, 128), f32), ((8, width), f32)]
    args = (w_down, own, send, picked, added, gate, back_rows)
    return kernel(body, "finish_mlp", outs, args, "v" * 7)


def finish_rows(w_qkv, dqkv, picked, back_rows, dmiddle, dlogit, vec):
    rows, width = picked.shape

    def body(all_ref, dqkv_ref, x_ref, dy_ref, dm_ref, dlogit_ref, vec_ref, grad_ref, dg_ref):
        dh = dot_nt(dqkv_ref[...], all_ref[...])
        x = x_ref[...].astype(f32)
        inverse = lax.rsqrt(mean_last(x * x) + norm_eps)
        unit = x * inverse
        dg_ref[...] = jnp.broadcast_to(sum_rows(dh * unit), dg_ref.shape)
        scaled = dh * vec_ref[0:1]
        dx = inverse * (scaled - unit * mean_last(scaled * unit))
        grad = dy_ref[...].astype(f32) + dm_ref[...] + dx + dlogit_ref[:, 0:1] * vec_ref[2:3]
        grad_ref[...] = grad.astype(bf16)

    outs = [((rows, width), bf16), ((8, width), f32)]
    args = (w_qkv, dqkv, picked, back_rows, dmiddle, dlogit, vec)
    return kernel(body, "finish_rows", outs, args, "v" * 7)


def stack_all(*groups):
    counts = [len(group) for group in groups]

    def body(*refs):
        ins, outs = refs[: sum(counts)], refs[sum(counts) :]
        for out, count in zip(outs, counts):
            for place in range(count):
                out[place] = ins[place][...]
            ins = ins[count:]

    outs = [((len(group), *group[0].shape), group[0].dtype) for group in groups]
    args = [array for group in groups for array in group]
    return kernel(body, "stack_all", outs, args, "v" * len(args))


def pick_flip(refs, flip):
    if flip == 0 or len(refs) == 4:
        return refs[flip]
    return refs[1] if flip == 2 else refs[2].at[flip // 2]


def join_z(z, own, others, split):
    rows, width = own.shape
    count = 1 + len(others)

    def body(z_ref, *refs):
        ins, (left_ref, right_ref, total) = refs[:count], refs[count:]
        for flip in range(4):
            start = pl.multiple_of((z_ref[0] ^ flip) * rows, rows)
            total[pl.ds(start, rows)] = pick_flip(ins, flip)[...].astype(f32)
        left_ref[...] = total[:, :split].astype(bf16)
        right_ref[...] = total[:, split:].astype(bf16)

    outs = [((4 * rows, split), bf16), ((4 * rows, width - split), bf16)]
    scratch = [pltpu.VMEM((4 * rows, width), f32)]
    return kernel(body, "join_z", outs, (z, own, *others), "s" + "v" * count, scratch)


def join_z_pairs(z, mine, others):
    _, rows, width = mine.shape

    def body(z_ref, *refs):
        ins, outs = refs[:3], refs[3:]
        for flip in range(4):
            start = pl.ds(pl.multiple_of((z_ref[0] ^ flip) * rows, rows), rows)
            block = pick_flip(ins, flip)
            for place in range(4):
                outs[place][start] = block[place]

    outs = [((4 * rows, width), bf16)] * 4
    return kernel(body, "join_z_pairs", outs, (z, mine, *others), "svvv")


def add_z_pairs(z, keep_l, keep_r, other_l, other_r):
    pair, rows, width = keep_l.shape
    part = rows // 4

    def body(z_ref, keep_l, keep_r, other_l, other_r, mine, send, total):
        for half, (keep, other) in enumerate(((keep_l, other_l), (keep_r, other_r))):
            for place in range(pair):
                total[half * pair + place] = keep[place] + other[place].astype(f32)
        for flip in range(4):
            start = pl.multiple_of((z_ref[0] ^ flip) * part, part)
            out = (mine, send)[flip % 2]
            out[flip // 2] = total[:, pl.ds(start, part)].astype(out.dtype)

    outs = [((2, 4, part, width), f32), ((2, 4, part, width), bf16)]
    scratch = [pltpu.VMEM((4, rows, width), f32)]
    args = (z, keep_l, keep_r, other_l, other_r)
    return kernel(body, "add_z_pairs", outs, args, "svvvv", scratch)


def add_four(mine, other):
    def body(mine, other, send_l, send_r, keep):
        def total(place):
            return mine[place] + other[place].astype(f32)

        width = mine.shape[2]
        keep[:, :width] = total(0)
        keep[:, width:] = total(2)
        send_l[...] = total(1).astype(bf16)
        send_r[...] = total(3).astype(bf16)

    _, rows, width = mine.shape
    outs = [((rows, width), bf16)] * 2 + [((rows, 2 * width), f32)]
    return kernel(body, "add_four", outs, (mine, other), "vv")


def add_pairs(keep_l, keep_r, other_l, other_r):
    def body(keep_l, keep_r, other_l, other_r, send_l, send_r, left, right):
        for keep, other, send, mine in (
            (keep_l, other_l, send_l, left),
            (keep_r, other_r, send_r, right),
        ):
            send[...] = (keep[1] + other[1].astype(f32)).astype(bf16)
            mine[...] = keep[0] + other[0].astype(f32)

    shapes = [keep_l.shape[1:], keep_r.shape[1:]]
    outs = [(shape, kind) for kind in (bf16, f32) for shape in shapes]
    return kernel(body, "add_pairs", outs, (keep_l, keep_r, other_l, other_r), "vvvv")


def add_split(z, keep_l, keep_r, other_l, other_r):
    rows, split = keep_l.shape
    width = split + keep_r.shape[1]
    part = rows // 4

    def body(z_ref, keep_l, keep_r, other_l, other_r, mine, send, total):
        total[:, :split] = keep_l[...] + other_l[...].astype(f32)
        total[:, split:] = keep_r[...] + other_r[...].astype(f32)
        for flip in range(4):
            start = pl.multiple_of((z_ref[0] ^ flip) * part, part)
            out = (mine, send)[flip % 2]
            out[flip // 2] = total[pl.ds(start, part)].astype(out.dtype)

    outs = [((2, part, width), f32), ((2, part, width), bf16)]
    scratch = [pltpu.VMEM((rows, width), f32)]
    args = (z, keep_l, keep_r, other_l, other_r)
    return kernel(body, "add_split", outs, args, "svvvv", scratch)


def add_next(keep, other):
    def body(keep, other, mine, send):
        mine[...] = keep[0] + other[0].astype(f32)
        send[...] = (keep[1] + other[1].astype(f32)).astype(bf16)

    shape = keep.shape[1:]
    return kernel(body, "add_next", [(shape, f32), (shape, bf16)], (keep, other), "vv")


def settle_halves(keep, other_l, other_r):
    def body(keep, other_l, other_r, grad, square):
        width = other_l.shape[1]
        total = None
        for half, other in enumerate((other_l, other_r)):
            lanes = pl.ds(half * width, width)
            value = keep[:, lanes] + other[...].astype(f32)
            grad[:, lanes] = value
            part = jnp.sum(value * value)
            total = part if total is None else total + part
        square[...] = jnp.full(square.shape, total)

    outs = [(keep.shape, f32), ((8, 128), f32)]
    return kernel(body, "settle_halves", outs, (keep, other_l, other_r), "vvv")


def settle_z(mine, other):
    rows, width = mine.shape

    def body(mine, other, grad, square, last, turned):
        value = mine[...] + other[...].astype(f32)
        grad[...] = value
        square[...] = jnp.full(square.shape, jnp.sum(value * value))
        turned[...] = jnp.zeros_like(turned)
        turned[:rows] = value[:, width - 128 :]
        last[...] = turned[...].T[:8]

    outs = [(mine.shape, f32), ((8, 128), f32), ((8, 128), f32)]
    scratch = [pltpu.VMEM((128, 128), f32)]
    return kernel(body, "settle_z", outs, (mine, other), "vv", scratch)


def update(squares, limit, grads, states, vec_grad, vec_states):
    count = len(grads)

    def body(square_ref, *refs):
        grad_refs, refs = refs[:count], refs[count:]
        state_refs, refs = refs[: 3 * count], refs[3 * count :]
        vec_ref, vec_m, vec_v, norm_ref, out_refs = *refs[:4], refs[4:]
        norm = jnp.sqrt(jnp.sum(square_ref[...], axis=0, keepdims=True)[:, 0:1])
        norm_ref[...] = jnp.broadcast_to(norm, norm_ref.shape)
        factor = jnp.minimum(1.0, limit / (norm + 1e-06))
        for place in range(count):
            w, m, v = (ref[...] for ref in state_refs[3 * place : 3 * place + 3])
            grad = grads[place].read(grad_refs[place], 0, grads[place].columns) * factor
            for ref, value in zip(out_refs[3 * place :], adam_update(w, grad, m, v)):
                ref[...] = value
        grad = vec_ref[:3, : vec_m.shape[1]] * factor
        first, second = moment_update(grad, vec_m[...], vec_v[...])
        out_refs[-2][...] = first
        out_refs[-1][...] = second

    flat = [array for state in states for array in state]
    outs = [((8, 128), f32)] + [(array.shape, f32) for array in (*flat, *vec_states)]
    args = (squares, *(grad.array for grad in grads), *flat, vec_grad, *vec_states)
    return kernel(body, "update", outs, args, "v" * len(args), (), 32)


class Steps:
    def __init__(self, chain):
        self.chain = chain
        self.result = None
        self.launch(next(chain))

    def launch(self, step):
        self.flips = [flip for _, flip in step]
        self.given = [array for array, _ in step]

    def advance(self, arrays):
        try:
            self.launch(self.chain.send(arrays))
        except StopIteration as stop:
            self.flips, self.given, self.result = (), (), stop.value


def slot(chains, value):
    arrays = [
        [swap(array, flip) for array, flip in zip(chain.given, chain.flips)] for chain in chains
    ]
    arrays, value = lax.optimization_barrier((arrays, value))
    for chain, array in zip(chains, arrays):
        chain.advance(array)
    return value


def ready(chains, value):
    arrays, value = lax.optimization_barrier(([chain.given for chain in chains], value))
    for chain, array in zip(chains, arrays):
        chain.given = array
    return value


def swap(array, bit):
    count = lax.axis_size("wide") * lax.axis_size("narrow")
    return lax.ppermute(array, AXES, [(i, i ^ bit) for i in range(count)])


def exchange(*arrays):
    return (yield [(array, 4) for array in arrays])


def around_z(shard, at_once):
    if at_once:
        return (yield [(shard, flip) for flip in (1, 2, 3)])
    (two,) = yield [(shard, 2)]
    (both,) = yield [(stack_all((shard, two))[0], 1)]
    return two, both


def gather(shard, z, split, at_once):
    others = yield from around_z(shard, at_once)
    left, right = join_z(z, shard, others, split)
    near_l, near_r = yield [(left, 8), (right, 16)]
    return (yield from spread(left, near_l, right, near_r))


def gather_pairs(shard, z):
    half = shard.shape[1] // 2
    left, right = shard[:, :half], shard[:, half:]
    near_l, near_r = yield [(left, 8), (right, 16)]
    mine = jnp.stack([left, near_l, right, near_r])
    others = yield from around_z(mine, False)
    return (yield from spread(*join_z_pairs(z, mine, others)))


def spread(left, near_l, right, near_r):
    keep_l, keep_r = stack_all((left, near_l), (right, near_r))
    far_l, far_r, *near = yield [(keep_l, 16), (keep_r, 8), (keep_l, 4), (keep_r, 4)]
    far = yield [(far_l, 4), (far_r, 4)]
    return (left, near_l, right, near_r, far_l, far_r, *near, *far)


def scatter(z, send_l, send_r, keep_l, keep_r):
    other_l, other_r = yield [(send_l, 16), (send_r, 8)]
    send_l, send_r, left, right = add_pairs(keep_l, keep_r, other_l, other_r)
    other_l, other_r = yield [(send_l, 8), (send_r, 16)]
    mine, send = add_split(z, left, right, other_l, other_r)
    (other,) = yield [(send, 1)]
    mine, send = add_next(mine, other)
    (other,) = yield [(send, 2)]
    return settle_z(mine, other)


def scatter_pairs(z, send_l, send_r, keep_l, keep_r):
    other_l, other_r = yield [(send_l, 16), (send_r, 8)]
    mine, send = add_z_pairs(z, keep_l, keep_r, other_l, other_r)
    (other,) = yield [(send, 1)]
    mine, send = add_next(mine, other)
    (other,) = yield [(send, 2)]
    send_l, send_r, keep = add_four(mine, other)
    other_l, other_r = yield [(send_l, 8), (send_r, 16)]
    return settle_halves(keep, other_l, other_r)


def cut(whole, split):
    blocks = whole.reshape(8, whole.shape[0] // 8, whole.shape[1])
    sides = (blocks[..., :split], blocks[..., split:])
    groups = [
        [sides[flip[2]][flip[0] * 4 + flip[1] * 2 + core] for flip in flips]
        for core in range(2)
        for flips in GROUPS
    ]
    return (*groups[0], *groups[1], *(jnp.stack(group) for group in groups[2:]))


def uncut(own, send):
    parts = jnp.stack([array.reshape(array.shape[0], 4, -1) for array in (own, send)], axis=2)
    return parts.reshape(own.shape[0], -1)


def per_device(
    paired,
    tokens,
    cotangent,
    segments,
    picks,
    w_qkv,
    w_out,
    w_up,
    w_down,
    vectors,
    m_qkv,
    m_out,
    m_up,
    m_down,
    m_vectors,
    v_qkv,
    v_out,
    v_up,
    v_down,
    v_vectors,
):
    devices_all = lax.axis_size("wide") * lax.axis_size("narrow")
    lane = lax.axis_index(AXES)
    seq_count, top_count = picks.shape
    seq_len = segments.shape[1]
    model_width = tokens.shape[1]
    qkv_width = w_qkv.shape[1]
    ff_width = w_up.shape[1]
    shard_width = vectors.shape[1]
    split_a, split_b, split_c = 2 * model_width, ff_width // 2, model_width // 2
    z = (lane & 3).reshape(1)
    me = (lane >> 2).reshape(1) if paired else jnp.zeros((1,), jnp.int32)

    chunk_a = gather_input(w_qkv, w_out, vectors)
    chunk_b = w_up.astype(bf16)
    chunk_c = w_down.astype(bf16)

    def start(chain, *args):
        return Steps(chain(*args)) if paired else None

    def tick(chains, value):
        return slot(chains, value) if paired else value

    def stage(chains, value):
        return ready(chains, value) if paired else value

    def whole(take, chunk, split):
        if paired:
            return take.result
        return cut(lax.all_gather(chunk, AXES, axis=0, tiled=True), split)

    hot = picks[:, :, None] == jnp.arange(seq_len, dtype=jnp.int32)[None, None, :]
    hot_low = hot.astype(bf16)
    tok_blocks = tokens.reshape(seq_count, seq_len, model_width)
    back_blocks = cotangent.reshape(seq_count, seq_len, model_width)

    def pick(blocks):
        rows = jnp.einsum("skl,sld->skd", hot_low, blocks, preferred_element_type=f32)
        return rows.astype(bf16).reshape(-1, model_width)

    def place(blocks, rows):
        rows = rows.reshape(seq_count, top_count, model_width)
        spread = jnp.einsum("skl,skd->sld", hot_low, rows, preferred_element_type=f32).astype(bf16)
        taken = jnp.any(hot, axis=1)
        return jnp.where(taken[:, :, None], spread, blocks).reshape(-1, model_width)

    take_a = start(gather, chunk_a, z, split_a, True)
    take_c = start(gather_pairs, chunk_c, z)
    picked = pick(tok_blocks)
    back_rows = pick(back_blocks)
    seg_sel = jnp.sum(jnp.where(hot, segments[:, None, :], 0), axis=-1)
    seg_row, seg_col = seg_sel[:, None, :], seg_sel[:, :, None]
    spot = jnp.arange(model_width, dtype=jnp.int32)
    half, eighth = model_width // 2, model_width // 8
    flip = spot % half // eighth * 2 + spot // half
    order = ((me[0] ^ flip) * eighth + spot % eighth)[None]
    inputs = (picked, back_rows, seg_row, seg_col, order, chunk_b)
    inputs = tick([take_a, take_c], inputs)
    take_b = start(gather, inputs[-1], z, split_b, False)
    inputs = tick([take_a], inputs[:-1])
    inputs = tick([take_b], inputs)
    inputs = tick([take_b, take_c], inputs)
    inputs = tick([take_a, take_b], inputs)
    inputs = tick([take_a], inputs)

    all_a = whole(take_a, chunk_a, split_a)
    picked, back_rows = inputs[:2]
    order = inputs[4]
    state = attend(me, all_a, *inputs)
    state = tick([take_b, take_c], state)
    own, send, df, gate, vec, added, h2, all_qkv, all_out, qkv, probs = state
    early = start(exchange, send)
    h2 = stage([take_c], h2)
    h2 = tick([take_b, early], h2)
    (sib,) = early.result if paired else (send,)
    all_b = whole(take_b, chunk_b, split_b)
    g_own, g_send, g_sib, h2_pair, all_up, slope = climb(me, all_b, h2, sib, order)

    def give(chain, name, products, split):
        if paired:
            return Steps(chain(z, *outer(name, products, split)))
        grads = [dot_tn(uncut(one.value(), far.value()), two.value()) for one, two, far, _ in products]
        grad = jnp.concatenate(grads, axis=1)
        grad = lax.psum_scatter(grad, AXES, scatter_dimension=0, tiled=True)
        return grad, jnp.full((8, 128), jnp.sum(grad * grad))

    df_sib = jnp.concatenate([sib[2], sib[3]], axis=1)
    left_c = View(g_sib) if paired else View(g_send)
    give_c = give(
        scatter_pairs, "outer_c", [(View(g_own), View(df), left_c, View(df_sib))], split_c
    )
    slope = stage([give_c], slope)
    slope = tick([take_c], slope)
    slope = tick([take_c], slope)
    all_c = whole(take_c, chunk_c, split_c)
    du, all_down = descend(me, all_c, slope, df)
    dmiddle, da, dg2 = unclimb(all_up, du, picked, added, gate, back_rows, vec)
    new_rows, dlogit, dr = finish_mlp(
        all_down, g_own, g_send, picked, added, gate, back_rows
    )
    du, da, dmiddle, new_rows, dlogit = tick([give_c], (du, da, dmiddle, new_rows, dlogit))
    late_u = start(exchange, du)
    dqkv = unattend(all_out, da, qkv, probs)
    dqkv = tick([late_u], dqkv)
    (du_sib,) = late_u.result if paired else (du,)
    late_q = start(exchange, dqkv, da)
    views = [View(h2_pair, lead=place) for place in range(2)]
    if not paired:
        cols = h2.reshape(h2.shape[0], 4, 2, -1)
        views = [View(cols[:, :, core].reshape(h2.shape[0], -1)) for core in range(2)]
    give_b = give(
        scatter_pairs, "outer_b", [(views[0], View(du), views[1], View(du_sib))], split_b
    )
    dqkv = stage([give_b, give_c], dqkv)
    grad_rows, dg1 = finish_rows(all_qkv, dqkv, picked, back_rows, dmiddle, dlogit, vec)
    late_v = start(exchange, dg1, dg2, dr)
    dqkv = stage([late_v], dqkv)
    dqkv = tick([late_q, late_v], dqkv)
    dqkv_sib, da_sib = late_q.result if paired else (dqkv, da)
    products = [
        (View(own, lead=0), View(dqkv), View(sib, lead=0), View(dqkv_sib)),
        (View(own, lead=1), View(da), View(sib, lead=1), View(da_sib)),
    ]
    if paired:
        left, right = vector_columns(order, (dg1, dg2, dr), late_v.result)
        products.append(tuple(View(array, lead=part) for part in range(2) for array in (left, right)))
    give_a = give(scatter, "outer_a", products, split_a)
    grad_rows = stage([give_a], grad_rows)
    grad_rows = tick([give_b, give_c], grad_rows)
    grad_rows, new_rows = stage([give_b, give_c], (grad_rows, new_rows))
    mixed_rows = place(tok_blocks, new_rows)
    grad_rows, mixed_rows = tick([give_a], (grad_rows, mixed_rows))
    grad_rows = stage([give_a], grad_rows)
    grad_rows = tick([give_b, give_c], grad_rows)
    grad_rows = stage([give_b, give_c], grad_rows)
    grad_rows = tick([give_a, give_c], grad_rows)
    grad_rows = stage([give_a], grad_rows)
    input_grad = place(back_blocks, grad_rows)
    input_grad = tick([give_a, give_b], input_grad)
    input_grad = stage([give_a, give_b], input_grad)
    input_grad = tick([give_a, give_b], input_grad)
    if paired:
        give_a, give_b, give_c = give_a.result, give_b.result, give_c.result
        vec_grad = give_a[2]
        local_sq = give_a[1] + give_b[1] + give_c[1]
    else:
        rows = jnp.stack([dg1[0], dg2[0], dr[0]], axis=0)
        rows = lax.psum_scatter(rows, AXES, scatter_dimension=1, tiled=True)
        vec_grad = jnp.pad(rows, ((0, 5), (0, 128 - shard_width)))
        local_sq = give_a[1] + give_b[1] + give_c[1] + jnp.sum(rows * rows)
    squares = jnp.broadcast_to(local_sq[:1], (devices_all, 128))
    squares = lax.all_to_all(squares, AXES, 0, 0, tiled=True)
    params_all = 4 * model_width * model_width + 2 * model_width * ff_width + 3 * model_width
    selected_all = seq_count * top_count * devices_all
    clip_limit = limit_scale * math.sqrt(params_all * selected_all)
    norm, *news = update(
        squares,
        clip_limit,
        [
            View(give_a[0], qkv_width),
            View(give_a[0], model_width, qkv_width),
            View(give_b[0]),
            View(give_c[0]),
        ],
        [
            (w_qkv, m_qkv, v_qkv),
            (w_out, m_out, v_out),
            (w_up, m_up, v_up),
            (w_down, m_down, v_down),
        ],
        vec_grad,
        (m_vectors, v_vectors),
    )
    return (
        mixed_rows,
        input_grad,
        norm[0, 0],
        *news[0:12:3],
        *news[1:12:3],
        news[12],
        *news[2:12:3],
        news[13],
    )


def solution(mesh):
    placed = (
        P(("wide", "narrow"), None),
        P(("wide", "narrow"), None),
        P(("wide", "narrow"), None),
        P(("wide", "narrow"), None),
        P(("wide", "narrow"), None),
        P(("wide", "narrow"), None),
        P(("wide", "narrow"), None),
        P(("wide", "narrow"), None),
        P(None, ("wide", "narrow")),
        P(("wide", "narrow"), None),
        P(("wide", "narrow"), None),
        P(("wide", "narrow"), None),
        P(("wide", "narrow"), None),
        P(None, ("wide", "narrow")),
        P(("wide", "narrow"), None),
        P(("wide", "narrow"), None),
        P(("wide", "narrow"), None),
        P(("wide", "narrow"), None),
        P(None, ("wide", "narrow")),
    )
    paired = mesh.shape["wide"] == 8 and mesh.shape["narrow"] == 4
    return jax.shard_map(
        functools.partial(per_device, paired),
        mesh=mesh,
        in_specs=placed,
        out_specs=(
            P(("wide", "narrow"), None),
            P(("wide", "narrow"), None),
            P(),
            P(("wide", "narrow"), None),
            P(("wide", "narrow"), None),
            P(("wide", "narrow"), None),
            P(("wide", "narrow"), None),
            P(("wide", "narrow"), None),
            P(("wide", "narrow"), None),
            P(("wide", "narrow"), None),
            P(("wide", "narrow"), None),
            P(None, ("wide", "narrow")),
            P(("wide", "narrow"), None),
            P(("wide", "narrow"), None),
            P(("wide", "narrow"), None),
            P(("wide", "narrow"), None),
            P(None, ("wide", "narrow")),
        ),
        check_vma=False,
    )
```

```python
import functools
import math

import jax
import jax.numpy as jnp
from jax import lax
from jax.experimental import pallas as pl
from jax.experimental.pallas import tpu as pltpu
from jax.sharding import PartitionSpec as P

HEAD_DIM = 64


norm_eps = 1e-06
beta_one = 0.9
beta_two = 0.999
adam_eps = 1e-08
learn_rate = 0.03
decay_rate = 0.1
adam_step = 10
limit_scale = 0.01
masked_out = -1e30
AXES = ("wide", "narrow")


def moment_update(grad_part, first, second):
    first_new = beta_one * first + (1.0 - beta_one) * grad_part
    second_new = beta_two * second + (1.0 - beta_two) * grad_part * grad_part
    return (first_new, second_new)


def adam_update(master, grad_part, first, second):
    first_new, second_new = moment_update(grad_part, first, second)
    first_hat = first_new / (1.0 - beta_one**adam_step)
    second_hat = second_new / (1.0 - beta_two**adam_step)
    master_new = master - learn_rate * (
        first_hat / (jnp.sqrt(second_hat) + adam_eps) + decay_rate * master
    )
    return (master_new, first_new, second_new)


f32, bf16 = jnp.float32, jnp.bfloat16
PAIR = 2 * HEAD_DIM
head_scale = HEAD_DIM ** (-0.5)
KEEP_L = ((0, 0, 0), (0, 1, 0))
KEEP_R = ((0, 0, 1), (1, 0, 1))
FAR_L = ((1, 0, 0), (1, 1, 0))
FAR_R = ((0, 1, 1), (1, 1, 1))
GROUPS = (KEEP_L, KEEP_R, FAR_L, FAR_R)


def kernel(body, name, outs, args, kinds, scratch=(), limit=24, loose=0):
    spaces = {"s": pltpu.SMEM, "v": pltpu.VMEM, "h": pltpu.VMEM, "a": pltpu.HBM}
    held = len(outs) - loose
    return pl.pallas_call(
        body,
        out_shape=[
            jax.ShapeDtypeStruct(*out) if place < held else pltpu.HBM(*out)
            for place, out in enumerate(outs)
        ],
        in_specs=[pl.BlockSpec(memory_space=spaces[kind]) for kind in kinds],
        out_specs=[
            pl.BlockSpec(memory_space=pltpu.VMEM if place < held else pltpu.HBM)
            for place in range(len(outs))
        ],
        scratch_shapes=list(scratch),
        compiler_params=pltpu.CompilerParams(vmem_limit_bytes=limit << 20),
        cost_estimate=pl.CostEstimate(flops=1, bytes_accessed=1, transcendentals=0),
        name=name,
    )(
        *(
            pltpu.with_memory_space_constraint(arg, pltpu.HBM) if kind in "ah" else arg
            for arg, kind in zip(args, kinds)
        )
    )


def each_block(pieces):
    for core in range(2):
        for group, flips in enumerate(GROUPS):
            for place, flip in enumerate(flips):
                yield flip[0] * 4 + flip[1] * 2 + core, flip[2], pieces[core * 4 + group].at[place]


def start_all(copies):
    for copy in copies:
        copy.start()


def wait_all(copies):
    for copy in copies:
        copy.wait()


def fetch(pieces, me, sem, base, left, right):
    copies = []
    for flip, half, block in each_block(pieces):
        rows = block.shape[0]
        start = pl.multiple_of((me ^ flip) * rows, rows)
        for target, column, out_column, width in (left, right)[half]:
            copies.append(
                pltpu.make_async_copy(
                    block.at[:, pl.ds(column, width)],
                    target.at[pl.ds(start, rows), pl.ds(out_column, width)],
                    sem.at[base + len(copies)],
                )
            )
    return copies


def dot_nt(left, right):
    return lax.dot_general(left, right, (((1,), (1,)), ((), ())), preferred_element_type=f32)


def dot_tn(left, right):
    return lax.dot_general(left, right, (((0,), (0,)), ((), ())), preferred_element_type=f32)


def dot_nn(left, right):
    return jnp.dot(left, right, preferred_element_type=f32)


def mean_last(array):
    return jnp.mean(array, axis=-1, keepdims=True)


def sum_rows(array):
    return jnp.sum(array, axis=0, keepdims=True)


def head_masks(dtype):
    lanes = lax.broadcasted_iota(jnp.int32, (1, PAIR), 1)
    first = (lanes < HEAD_DIM).astype(f32).astype(dtype)
    return first, (1 - first).astype(dtype)


def two_heads(pair, masks):
    return jnp.concatenate([pair * masks[0], pair * masks[1]], axis=0)


def one_pair(stacked, masks):
    rows = stacked.shape[0] // 2
    return stacked[:rows] * masks[0] + stacked[rows:] * masks[1]


def gather_input(w_qkv, w_out, vectors):
    rows, first = w_qkv.shape
    second = w_out.shape[1]

    def body(qkv_ref, out_ref, vec_ref, chunk_ref, turned):
        chunk_ref[:, :first] = qkv_ref[...].astype(bf16)
        chunk_ref[:, first : first + second] = out_ref[...].astype(bf16)
        turned[...] = jnp.zeros_like(turned)
        turned[:3] = vec_ref[...]
        same = lax.broadcasted_iota(jnp.int32, (rows, rows), 0) == lax.broadcasted_iota(
            jnp.int32, (rows, rows), 1
        )
        columns = dot_nt(same.astype(f32).astype(bf16), turned[...].astype(bf16))
        chunk_ref[:, first + second :] = columns.astype(bf16)

    outs = [((rows, first + second + 128), bf16)]
    scratch = [pltpu.VMEM((128, rows), f32)]
    return kernel(body, "gather_input", outs, (w_qkv, w_out, vectors), "hhh", scratch)[0]


def attend(me, pieces, picked, back_rows, seg_row, seg_col, order):
    rows, width = picked.shape
    seqs = seg_row.shape[0]
    top = rows // seqs
    pairs = width // PAIR
    first = pieces[0].shape[2]
    rest = 3 * width - first
    spare = pieces[1].shape[2] - rest - width

    def body(me_ref, *refs):
        blocks, refs = refs[:8], refs[8:]
        x_ref, dy_ref, seg_row_ref, seg_col_ref, order_ref = refs[:5]
        own_ref, send_ref, df_ref, gate_ref, vec_ref, add_ref, h2_ref = refs[5:12]
        all_ref, out_ref, qkv_out, prob_out = refs[12:16]
        w_qkv, w_out, w_vec, qkv_ref, prob_ref, att_ref, sem = refs[16:]
        vec_copies = fetch(blocks, me_ref[0], sem, 0, (), ((w_vec, rest + width, 0, spare),))
        left = fetch(blocks, me_ref[0], sem, 8, ((w_qkv, 0, 0, first),), ())
        right = fetch(blocks, me_ref[0], sem, 16, (), ((w_qkv, 0, first, rest),))
        out_copies = fetch(blocks, me_ref[0], sem, 24, (), ((w_out, rest, 0, width),))
        start_all(vec_copies + left + right + out_copies)
        wait_all(vec_copies)
        vec = w_vec[...].astype(f32).T[:8]
        vec_ref[...] = vec
        x = x_ref[...].astype(f32)
        h1 = (x * lax.rsqrt(mean_last(x * x) + norm_eps) * vec[0:1]).astype(bf16)
        for copies, start, count in ((left, 0, first), (right, first, rest)):
            wait_all(copies)
            for part in range(start, start + count, 384):
                lanes = pl.ds(part, 384)
                qkv_ref[:, lanes] = dot_nn(h1, w_qkv[:, lanes]).astype(bf16)
        stored = [
            pltpu.make_async_copy(w_qkv, all_ref, sem.at[32]),
            pltpu.make_async_copy(qkv_ref, qkv_out, sem.at[33]),
            pltpu.make_async_copy(w_out, out_ref, sem.at[34]),
        ]
        wait_all(out_copies)
        start_all(stored)
        masks, masks_f = head_masks(bf16), head_masks(f32)
        ordered_pairs = lax.broadcasted_iota(jnp.int32, (top, top), 1) <= lax.broadcasted_iota(
            jnp.int32, (top, top), 0
        )
        for seq in range(seqs):
            here = pl.ds(seq * top, top)
            seen = ordered_pairs & (seg_col_ref[seq] == seg_row_ref[seq])
            hidden = jnp.where(seen, 0.0, masked_out)
            hidden = jnp.concatenate([hidden, hidden], axis=0)
            for pair in range(pairs):
                q, k, v = (
                    qkv_ref[here, pl.ds(part * width + pair * PAIR, PAIR)] for part in range(3)
                )
                scores = dot_nt(two_heads(q, masks), k) * head_scale
                scores = jnp.where(hidden < 0.0, masked_out, scores)
                power = jnp.exp(scores - jnp.max(scores, axis=-1, keepdims=True))
                probs = power / jnp.sum(power, axis=-1, keepdims=True)
                prob_ref[seq * pairs + pair] = probs
                mixed = one_pair(dot_nn(probs.astype(bf16), v), masks_f)
                att_ref[here, pl.ds(pair * PAIR, PAIR)] = mixed.astype(bf16)
            group = pl.ds(seq * pairs, pairs)
            stored.append(
                pltpu.make_async_copy(prob_ref.at[group], prob_out.at[group], sem.at[35 + seq])
            )
            stored[-1].start()
        gate = jax.nn.sigmoid(jnp.sum(x * vec[2:3], axis=-1, keepdims=True))
        gate_ref[...] = jnp.broadcast_to(gate, gate_ref.shape)
        df = (gate * dy_ref[...].astype(f32)).astype(bf16)
        df_ref[...] = df
        added = dot_nn(att_ref[...], w_out[...])
        add_ref[...] = added
        middle = x + added
        h2 = (middle * lax.rsqrt(mean_last(middle * middle) + norm_eps) * vec[1:2]).astype(bf16)
        h2_ref[...] = h2
        for half in range(2):
            lanes = slice(half * (width // 2), (half + 1) * (width // 2))
            send_ref[2 + half] = df[:, lanes]
            send_ref[4 + half] = h2[:, lanes]
        chosen = one_hot_columns(order_ref)
        for place, array in enumerate((h1, att_ref[...])):
            parted = dot_nn(array, chosen).astype(bf16)
            own_ref[place] = parted[:, : width // 2]
            send_ref[place] = parted[:, width // 2 :]
        wait_all(stored)

    outs = [
        ((2, rows, width // 2), bf16),
        ((6, rows, width // 2), bf16),
        ((rows, width), bf16),
        ((rows, 128), f32),
        ((8, width), f32),
        ((rows, width), f32),
        ((rows, width), bf16),
        ((width, 3 * width), bf16),
        ((width, width), bf16),
        ((rows, 3 * width), bf16),
        ((seqs * pairs, 2 * top, top), f32),
    ]
    scratch = [
        pltpu.VMEM((width, 3 * width), bf16),
        pltpu.VMEM((width, width), bf16),
        pltpu.VMEM((width, spare), bf16),
        pltpu.VMEM((rows, 3 * width), bf16),
        pltpu.VMEM((seqs * pairs, 2 * top, top), f32),
        pltpu.VMEM((rows, width), bf16),
        pltpu.SemaphoreType.DMA((35 + seqs,)),
    ]
    args = (me, *pieces, picked, back_rows, seg_row, seg_col, order)
    return kernel(body, "attend", outs, args, "s" + "a" * 6 + "vv" + "vvvvv", scratch, 26, 4)


def one_hot_columns(order_ref):
    width = order_ref.shape[1]
    chosen = lax.broadcasted_iota(jnp.int32, (width, width), 0) == order_ref[...]
    return chosen.astype(f32).astype(bf16)


def climb(me, pieces, h2, sib, order):
    rows, width = h2.shape
    first = pieces[0].shape[2]
    block = 2 * first // 8

    def body(me_ref, *refs):
        blocks, refs = refs[:8], refs[8:]
        h2_ref, sib_ref, order_ref = refs[:3]
        own_ref, send_ref, far_ref, pair_ref, up_ref, slope_out = refs[3:9]
        w_up, slope_ref, both_ref, sem = refs[9:]
        copies = fetch(
            blocks, me_ref[0], sem, 0, ((w_up, 0, 0, first),), ((w_up, 0, first, first),)
        )
        start_all(copies)
        both_ref[:rows] = h2_ref[...]
        for half in range(2):
            lanes = pl.ds(half * (width // 2), width // 2)
            both_ref[rows:, lanes] = sib_ref[4 + half]
        chosen = one_hot_columns(order_ref)[:, : width // 2]
        parted = dot_nn(both_ref[...], chosen).astype(bf16)
        pair_ref[0] = parted[:rows]
        pair_ref[1] = parted[rows:]
        wait_all(copies)
        stored = [pltpu.make_async_copy(w_up, up_ref, sem.at[16])]
        start_all(stored)
        scale = math.sqrt(2.0 / math.pi)
        for flip in range(8):
            start = pl.multiple_of((me_ref[0] ^ flip) * block, block)
            place = flip // 2
            lanes = pl.ds(place * block, block)
            weights = w_up[:, pl.ds(start, block)]
            u = dot_nn(both_ref[:rows], weights)
            square = u * u
            bent = jnp.tanh(scale * (u + 0.044715 * (square * u)))
            half_up = 0.5 * (1.0 + bent)
            target = send_ref if flip % 2 else own_ref
            target[:, lanes] = (u * half_up).astype(bf16)
            where = (flip % 2) * 4 + place
            slope_ref[where] = half_up + (0.5 * u) * (1.0 - bent * bent) * (
                scale * (1.0 + (3.0 * 0.044715) * square)
            )
            stored.append(
                pltpu.make_async_copy(
                    slope_ref.at[where], slope_out.at[where], sem.at[17 + flip]
                )
            )
            stored[-1].start()
            if flip % 2 == 0:
                u = dot_nn(both_ref[rows:], weights)
                bent = jnp.tanh(scale * (u + 0.044715 * (u * u * u)))
                far_ref[:, lanes] = (0.5 * u * (1.0 + bent)).astype(bf16)
        wait_all(stored)

    outs = [
        ((rows, 4 * block), bf16),
        ((rows, 4 * block), bf16),
        ((rows, 4 * block), bf16),
        ((2, rows, width // 2), bf16),
        ((width, 8 * block), bf16),
        ((8, rows, block), f32),
    ]
    scratch = [
        pltpu.VMEM((width, 8 * block), bf16),
        pltpu.VMEM((8, rows, block), f32),
        pltpu.VMEM((2 * rows, width), bf16),
        pltpu.SemaphoreType.DMA((25,)),
    ]
    args = (me, *pieces, h2, sib, order)
    return kernel(body, "climb", outs, args, "s" + "a" * 6 + "vv" + "vvv", scratch, 26, 2)


def vector_columns(order, mine, other):
    width = order.shape[1]
    half = width // 2

    def body(order_ref, *refs):
        ins, (left, right, rows) = refs[:6], refs[6:]
        chosen = one_hot_columns(order_ref)[:, :half]
        rows[...] = jnp.zeros_like(rows)
        for place in range(3):
            rows[place : place + 1] = ins[place][0:1] + ins[3 + place][0:1]
        columns = rows[...].T.astype(bf16)
        for part in range(2):
            left[part] = chosen[part * half : (part + 1) * half]
            right[part] = columns[part * half : (part + 1) * half]

    outs = [((2, half, half), bf16), ((2, half, 128), bf16)]
    scratch = [pltpu.VMEM((128, width), f32)]
    args = (order, *mine, *other)
    return kernel(body, "vector_columns", outs, args, "v" * 7, scratch)


class View:
    def __init__(self, array, columns=None, first=0, lead=None):
        self.array, self.first, self.lead = array, first, lead
        self.columns = columns or array.shape[-1]

    def value(self):
        array = self.array if self.lead is None else self.array[self.lead]
        return array[:, self.first : self.first + self.columns]

    def read(self, ref, first, columns):
        lanes = pl.ds(self.first + first, columns)
        return ref[:, lanes] if self.lead is None else ref[self.lead, :, lanes]


def outer(name, products, split):
    length = products[0][0].columns // 4
    total = sum(product[1].columns for product in products)
    widths = (split, total - split)
    order = ((2, 3), (1, 3), (0, 1), (0, 2))

    def body(*refs):
        ins, outs = refs[: 4 * len(products)], refs[4 * len(products) :]
        base = 0
        for number, product in enumerate(products):
            reads = [
                functools.partial(view.read, ref)
                for view, ref in zip(product, ins[4 * number : 4 * number + 4])
            ]
            columns = product[1].columns
            step = min(768, columns)
            for start in range(0, columns, step):
                for first in range(0, 4 * length, 384):
                    value = dot_tn(reads[0](first, 384), reads[1](start, step))
                    value += dot_tn(reads[2](first, 384), reads[3](start, step))
                    for block in range(first // length, (first + 384) // length):
                        part = value[block * length - first : (block + 1) * length - first]
                        for half in range(2):
                            low = max(base + start, half * split)
                            high = min(base + start + step, split + half * (total - split))
                            if high <= low:
                                continue
                            piece = part[:, low - base - start : high - base - start]
                            out_lanes = pl.ds(low - half * split, high - low)
                            for out in (half, 2 + half):
                                if block in order[out]:
                                    outs[out][order[out].index(block), :, out_lanes] = piece.astype(
                                        outs[out].dtype
                                    )
            base += columns

    outs = [
        ((2, length, widths[out % 2]), bf16 if out < 2 else f32) for out in range(4)
    ]
    args = [view.array for product in products for view in product]
    return kernel(body, name, outs, args, "v" * len(args))


def descend(me, pieces, slope, df):
    rows, width = df.shape
    block = slope.shape[2]

    def body(me_ref, *refs):
        blocks, refs = refs[:8], refs[8:]
        slope_in, df_ref, du_ref, down_ref, w_down, slope_ref, sem = refs
        copies = [[] for _ in range(8)]
        for flip, side, part in each_block(blocks):
            lanes = pl.ds(side * (width // 2), width // 2)
            place = (flip % 2) * 4 + flip // 2
            target = w_down.at[pl.ds(place * block, block), lanes]
            copies[place].append(
                pltpu.make_async_copy(part, target, sem.at[place * 2 + side])
            )
        for place, pair in enumerate(copies):
            pair.append(
                pltpu.make_async_copy(
                    slope_in.at[place], slope_ref.at[place], sem.at[17 + place]
                )
            )
            start_all(pair)
        for place in range(8):
            wait_all(copies[place])
            flip = place % 4 * 2 + place // 4
            start = pl.multiple_of((me_ref[0] ^ flip) * block, block)
            dg = dot_nt(df_ref[...], w_down[pl.ds(place * block, block)])
            du_ref[:, pl.ds(start, block)] = (dg * slope_ref[place]).astype(bf16)
        stored = pltpu.make_async_copy(w_down, down_ref, sem.at[16])
        stored.start()
        stored.wait()

    outs = [((rows, 8 * block), bf16), ((8 * block, width), bf16)]
    scratch = [
        pltpu.VMEM((8 * block, width), bf16),
        pltpu.VMEM((8, rows, block), f32),
        pltpu.SemaphoreType.DMA((25,)),
    ]
    args = (me, *pieces, slope, df)
    return kernel(body, "descend", outs, args, "s" + "a" * 6 + "vvav", scratch, 24, 1)


def unclimb(w_up, du, picked, added, gate, back_rows, vec):
    rows, width = picked.shape

    def body(up_ref, du_ref, x_ref, add_ref, gate_ref, dy_ref, vec_ref, dm_ref, da_ref, dg_ref):
        dh = dot_nt(du_ref[...], up_ref[...])
        middle = x_ref[...].astype(f32) + add_ref[...]
        inverse = lax.rsqrt(mean_last(middle * middle) + norm_eps)
        unit = middle * inverse
        dg_ref[...] = jnp.broadcast_to(sum_rows(dh * unit), dg_ref.shape)
        scaled = dh * vec_ref[1:2]
        dm = inverse * (scaled - unit * mean_last(scaled * unit))
        dm_ref[...] = dm
        da_ref[...] = (gate_ref[:, 0:1] * dy_ref[...].astype(f32) + dm).astype(bf16)

    outs = [((rows, width), f32), ((rows, width), bf16), ((8, width), f32)]
    args = (w_up, du, picked, added, gate, back_rows, vec)
    return kernel(body, "unclimb", outs, args, "v" * 7)


def unattend(w_out, da, qkv, probs):
    rows, width = da.shape
    top = probs.shape[2]
    seqs, pairs = rows // top, width // PAIR

    def body(out_ref, da_ref, qkv_ref, prob_ref, dqkv_ref, do_ref):
        do_ref[...] = dot_nt(da_ref[...], out_ref[...]).astype(bf16)
        masks, masks_f = head_masks(bf16), head_masks(f32)
        for seq in range(seqs):
            here = pl.ds(seq * top, top)
            for pair in range(pairs):
                lanes = [pl.ds(part * width + pair * PAIR, PAIR) for part in range(3)]
                q, k, v = (qkv_ref[here, part] for part in lanes)
                do = two_heads(do_ref[here, pl.ds(pair * PAIR, PAIR)], masks)
                probs = prob_ref[seq * pairs + pair]
                dprobs = dot_nt(do, v)
                dscores = probs * (dprobs - jnp.sum(dprobs * probs, axis=-1, keepdims=True))
                dscores = dscores.astype(bf16)
                dq = one_pair(dot_nn(dscores, k), masks_f) * head_scale
                dk = dot_tn(dscores, two_heads(q, masks)) * head_scale
                dv = dot_tn(probs.astype(bf16), do)
                for part, value in zip(lanes, (dq, dk, dv)):
                    dqkv_ref[here, part] = value.astype(bf16)

    scratch = [pltpu.VMEM((rows, width), bf16)]
    outs = [((rows, 3 * width), bf16)]
    return kernel(body, "unattend", outs, (w_out, da, qkv, probs), "vvvv", scratch)[0]


def finish_mlp(w_down, own, send, picked, added, gate, back_rows):
    rows, width = picked.shape
    half = w_down.shape[0] // 2

    def body(down_ref, own_ref, send_ref, x_ref, add_ref, gate_ref, dy_ref, *outs):
        new_ref, dlogit_ref, dr_ref = outs
        out = dot_nn(own_ref[:, :half], down_ref[:half])
        out += dot_nn(send_ref[:, :half], down_ref[half:])
        both = add_ref[...] + out
        x = x_ref[...].astype(f32)
        gate = gate_ref[:, 0:1]
        new_ref[...] = (x + gate * both).astype(bf16)
        dlogit = jnp.sum(dy_ref[...].astype(f32) * both, axis=-1, keepdims=True)
        dlogit = dlogit * gate * (1.0 - gate)
        dlogit_ref[...] = jnp.broadcast_to(dlogit, dlogit_ref.shape)
        dr_ref[...] = jnp.broadcast_to(sum_rows(dlogit * x), dr_ref.shape)

    outs = [((rows, width), bf16), ((rows, 128), f32), ((8, width), f32)]
    args = (w_down, own, send, picked, added, gate, back_rows)
    return kernel(body, "finish_mlp", outs, args, "v" * 7)


def finish_rows(w_qkv, dqkv, picked, back_rows, dmiddle, dlogit, vec):
    rows, width = picked.shape

    def body(all_ref, dqkv_ref, x_ref, dy_ref, dm_ref, dlogit_ref, vec_ref, grad_ref, dg_ref):
        dh = dot_nt(dqkv_ref[...], all_ref[...])
        x = x_ref[...].astype(f32)
        inverse = lax.rsqrt(mean_last(x * x) + norm_eps)
        unit = x * inverse
        dg_ref[...] = jnp.broadcast_to(sum_rows(dh * unit), dg_ref.shape)
        scaled = dh * vec_ref[0:1]
        dx = inverse * (scaled - unit * mean_last(scaled * unit))
        grad = dy_ref[...].astype(f32) + dm_ref[...] + dx + dlogit_ref[:, 0:1] * vec_ref[2:3]
        grad_ref[...] = grad.astype(bf16)

    outs = [((rows, width), bf16), ((8, width), f32)]
    args = (w_qkv, dqkv, picked, back_rows, dmiddle, dlogit, vec)
    return kernel(body, "finish_rows", outs, args, "v" * 7)


def join_z(z, own, others, split):
    rows, width = own.shape

    def body(z_ref, *refs):
        ins, left_ref, right_ref, total = refs[:4], *refs[4:]
        for flip, block in enumerate(ins):
            start = pl.multiple_of((z_ref[0] ^ flip) * rows, rows)
            total[pl.ds(start, rows)] = block[...].astype(f32)
        left_ref[...] = total[:, :split].astype(bf16)
        right_ref[...] = total[:, split:].astype(bf16)

    outs = [((4 * rows, split), bf16), ((4 * rows, width - split), bf16)]
    scratch = [pltpu.VMEM((4 * rows, width), f32)]
    return kernel(body, "join_z", outs, (z, own, *others), "svvvv", scratch)


def join_z_pairs(z, left, right, near_l, near_r, others):
    rows, width = left.shape

    def body(z_ref, *refs):
        mine, others, outs = refs[:4], refs[4:7], refs[7:]
        for flip in range(4):
            start = pl.ds(pl.multiple_of((z_ref[0] ^ flip) * rows, rows), rows)
            for place in range(4):
                block = others[flip - 1][place] if flip else mine[place][...]
                outs[place // 2][place % 2, start] = block

    outs = [((2, 4 * rows, width), bf16)] * 2
    args = (z, left, near_l, right, near_r, *others)
    return kernel(body, "join_z_pairs", outs, args, "svvvvvvv")


def add_z_pairs(z, keep_l, keep_r, other_l, other_r):
    pair, rows, width = keep_l.shape
    part = rows // 4

    def body(z_ref, keep_l, keep_r, other_l, other_r, mine, send, total):
        for half, (keep, other) in enumerate(((keep_l, other_l), (keep_r, other_r))):
            for place in range(pair):
                total[half * pair + place] = keep[place] + other[place].astype(f32)
        for flip in range(4):
            start = pl.multiple_of((z_ref[0] ^ flip) * part, part)
            out = (mine, send)[flip % 2]
            out[flip // 2] = total[:, pl.ds(start, part)].astype(out.dtype)

    outs = [((2, 4, part, width), f32), ((2, 4, part, width), bf16)]
    scratch = [pltpu.VMEM((4, rows, width), f32)]
    args = (z, keep_l, keep_r, other_l, other_r)
    return kernel(body, "add_z_pairs", outs, args, "svvvv", scratch)


def add_four(mine, other):
    def body(mine, other, send_l, send_r, keep):
        def total(place):
            return mine[place] + other[place].astype(f32)

        width = mine.shape[2]
        keep[:, :width] = total(0)
        keep[:, width:] = total(2)
        send_l[...] = total(1).astype(bf16)
        send_r[...] = total(3).astype(bf16)

    _, rows, width = mine.shape
    outs = [((rows, width), bf16)] * 2 + [((rows, 2 * width), f32)]
    return kernel(body, "add_four", outs, (mine, other), "vv")


def add_pairs(keep_l, keep_r, other_l, other_r):
    def body(keep_l, keep_r, other_l, other_r, send_l, send_r, left, right):
        for keep, other, send, mine in (
            (keep_l, other_l, send_l, left),
            (keep_r, other_r, send_r, right),
        ):
            send[...] = (keep[1] + other[1].astype(f32)).astype(bf16)
            mine[...] = keep[0] + other[0].astype(f32)

    shapes = [keep_l.shape[1:], keep_r.shape[1:]]
    outs = [(shape, kind) for kind in (bf16, f32) for shape in shapes]
    return kernel(body, "add_pairs", outs, (keep_l, keep_r, other_l, other_r), "vvvv")


def add_split(z, keep_l, keep_r, other_l, other_r):
    rows, split = keep_l.shape
    width = split + keep_r.shape[1]
    part = rows // 4

    def body(z_ref, keep_l, keep_r, other_l, other_r, mine, send, total):
        total[:, :split] = keep_l[...] + other_l[...].astype(f32)
        total[:, split:] = keep_r[...] + other_r[...].astype(f32)
        for flip in range(4):
            start = pl.multiple_of((z_ref[0] ^ flip) * part, part)
            out = (mine, send)[flip % 2]
            out[flip // 2] = total[pl.ds(start, part)].astype(out.dtype)

    outs = [((2, part, width), f32), ((2, part, width), bf16)]
    scratch = [pltpu.VMEM((rows, width), f32)]
    args = (z, keep_l, keep_r, other_l, other_r)
    return kernel(body, "add_split", outs, args, "svvvv", scratch)


def add_next(keep, other):
    def body(keep, other, mine, send):
        mine[...] = keep[0] + other[0].astype(f32)
        send[...] = (keep[1] + other[1].astype(f32)).astype(bf16)

    shape = keep.shape[1:]
    return kernel(body, "add_next", [(shape, f32), (shape, bf16)], (keep, other), "vv")


def settle_halves(keep, other_l, other_r):
    def body(keep, other_l, other_r, grad, square):
        width = other_l.shape[1]
        total = None
        for half, other in enumerate((other_l, other_r)):
            lanes = pl.ds(half * width, width)
            value = keep[:, lanes] + other[...].astype(f32)
            grad[:, lanes] = value
            part = jnp.sum(value * value)
            total = part if total is None else total + part
        square[...] = jnp.full(square.shape, total)

    outs = [(keep.shape, f32), ((8, 128), f32)]
    return kernel(body, "settle_halves", outs, (keep, other_l, other_r), "vvv")


def settle_z(mine, other):
    rows, width = mine.shape

    def body(mine, other, grad, square, last, turned):
        value = mine[...] + other[...].astype(f32)
        grad[...] = value
        square[...] = jnp.full(square.shape, jnp.sum(value * value))
        turned[...] = jnp.zeros_like(turned)
        turned[:rows] = value[:, width - 128 :]
        last[...] = turned[...].T[:8]

    outs = [(mine.shape, f32), ((8, 128), f32), ((8, 128), f32)]
    scratch = [pltpu.VMEM((128, 128), f32)]
    return kernel(body, "settle_z", outs, (mine, other), "vv", scratch)


def update(squares, limit, grads, states, vec_grad, vec_states):
    count = len(grads)

    def body(square_ref, *refs):
        grad_refs, refs = refs[:count], refs[count:]
        state_refs, refs = refs[: 3 * count], refs[3 * count :]
        vec_ref, vec_m, vec_v, norm_ref, out_refs = *refs[:4], refs[4:]
        norm = jnp.sqrt(jnp.sum(square_ref[...], axis=0, keepdims=True)[:, 0:1])
        norm_ref[...] = jnp.broadcast_to(norm, norm_ref.shape)
        factor = jnp.minimum(1.0, limit / (norm + 1e-06))
        for place in range(count):
            w, m, v = (ref[...] for ref in state_refs[3 * place : 3 * place + 3])
            grad = grads[place].read(grad_refs[place], 0, grads[place].columns) * factor
            for ref, value in zip(out_refs[3 * place :], adam_update(w, grad, m, v)):
                ref[...] = value
        grad = vec_ref[:3, : vec_m.shape[1]] * factor
        first, second = moment_update(grad, vec_m[...], vec_v[...])
        out_refs[-2][...] = first
        out_refs[-1][...] = second

    flat = [array for state in states for array in state]
    outs = [((8, 128), f32)] + [(array.shape, f32) for array in (*flat, *vec_states)]
    args = (squares, *(grad.array for grad in grads), *flat, vec_grad, *vec_states)
    return kernel(body, "update", outs, args, "v" * len(args), (), 32)


class Steps:
    def __init__(self, chain):
        self.chain = chain
        self.result = None
        self.launch(next(chain))

    def launch(self, step):
        self.flips = [flip for _, flip in step]
        self.given = [array for array, _ in step]

    def advance(self, arrays):
        try:
            self.launch(self.chain.send(arrays))
        except StopIteration as stop:
            self.flips, self.given, self.result = (), (), stop.value


def slot(chains, value):
    arrays = [
        [swap(array, flip) for array, flip in zip(chain.given, chain.flips)] for chain in chains
    ]
    arrays, value = lax.optimization_barrier((arrays, value))
    for chain, array in zip(chains, arrays):
        chain.advance(array)
    return value


def ready(chains, value):
    arrays, value = lax.optimization_barrier(([chain.given for chain in chains], value))
    for chain, array in zip(chains, arrays):
        chain.given = array
    return value


def swap(array, bit):
    count = lax.axis_size("wide") * lax.axis_size("narrow")
    return lax.ppermute(array, AXES, [(i, i ^ bit) for i in range(count)])


def exchange(*arrays):
    return (yield [(array, 4) for array in arrays])


def around_z(shard, at_once):
    if at_once:
        return (yield [(shard, flip) for flip in (1, 2, 3)])
    (two,) = yield [(shard, 2)]
    (both,) = yield [(jnp.stack([shard, two]), 1)]
    return both[0], two, both[1]


def gather(shard, z, split, at_once):
    others = yield from around_z(shard, at_once)
    left, right = join_z(z, shard, others, split)
    near_l, near_r = yield [(left, 8), (right, 16)]
    return (yield from spread(jnp.stack([left, near_l]), jnp.stack([right, near_r])))


def gather_pairs(shard, z):
    half = shard.shape[1] // 2
    left, right = shard[:, :half], shard[:, half:]
    near_l, near_r = yield [(left, 8), (right, 16)]
    others = yield from around_z(jnp.stack([left, near_l, right, near_r]), False)
    keep_l, keep_r = join_z_pairs(z, left, right, near_l, near_r, others)
    return (yield from spread(keep_l, keep_r))


def spread(keep_l, keep_r):
    far_l, far_r, *near = yield [(keep_l, 16), (keep_r, 8), (keep_l, 4), (keep_r, 4)]
    far = yield [(far_l, 4), (far_r, 4)]
    return (keep_l, keep_r, far_l, far_r, *near, *far)


def scatter(z, send_l, send_r, keep_l, keep_r):
    other_l, other_r = yield [(send_l, 16), (send_r, 8)]
    send_l, send_r, left, right = add_pairs(keep_l, keep_r, other_l, other_r)
    other_l, other_r = yield [(send_l, 8), (send_r, 16)]
    mine, send = add_split(z, left, right, other_l, other_r)
    (other,) = yield [(send, 1)]
    mine, send = add_next(mine, other)
    (other,) = yield [(send, 2)]
    return settle_z(mine, other)


def scatter_pairs(z, send_l, send_r, keep_l, keep_r):
    other_l, other_r = yield [(send_l, 16), (send_r, 8)]
    mine, send = add_z_pairs(z, keep_l, keep_r, other_l, other_r)
    (other,) = yield [(send, 1)]
    mine, send = add_next(mine, other)
    (other,) = yield [(send, 2)]
    send_l, send_r, keep = add_four(mine, other)
    other_l, other_r = yield [(send_l, 8), (send_r, 16)]
    return settle_halves(keep, other_l, other_r)


def cut(whole, split):
    blocks = whole.reshape(8, whole.shape[0] // 8, whole.shape[1])
    sides = (blocks[..., :split], blocks[..., split:])
    return tuple(
        jnp.stack([sides[flip[2]][flip[0] * 4 + flip[1] * 2 + core] for flip in flips])
        for core in range(2)
        for flips in GROUPS
    )


def uncut(own, send):
    parts = jnp.stack([array.reshape(array.shape[0], 4, -1) for array in (own, send)], axis=2)
    return parts.reshape(own.shape[0], -1)


def per_device(
    paired,
    tokens,
    cotangent,
    segments,
    picks,
    w_qkv,
    w_out,
    w_up,
    w_down,
    vectors,
    m_qkv,
    m_out,
    m_up,
    m_down,
    m_vectors,
    v_qkv,
    v_out,
    v_up,
    v_down,
    v_vectors,
):
    devices_all = lax.axis_size("wide") * lax.axis_size("narrow")
    lane = lax.axis_index(AXES)
    seq_count, top_count = picks.shape
    seq_len = segments.shape[1]
    model_width = tokens.shape[1]
    qkv_width = w_qkv.shape[1]
    ff_width = w_up.shape[1]
    shard_width = vectors.shape[1]
    split_a, split_b, split_c = 2 * model_width, ff_width // 2, model_width // 2
    z = (lane & 3).reshape(1)
    me = (lane >> 2).reshape(1) if paired else jnp.zeros((1,), jnp.int32)

    chunk_a = gather_input(w_qkv, w_out, vectors)
    chunk_b = w_up.astype(bf16)
    chunk_c = w_down.astype(bf16)

    def start(chain, *args):
        return Steps(chain(*args)) if paired else None

    def tick(chains, value):
        return slot(chains, value) if paired else value

    def stage(chains, value):
        return ready(chains, value) if paired else value

    def whole(take, chunk, split):
        if paired:
            return take.result
        return cut(lax.all_gather(chunk, AXES, axis=0, tiled=True), split)

    hot = picks[:, :, None] == jnp.arange(seq_len, dtype=jnp.int32)[None, None, :]
    hot_low = hot.astype(bf16)
    tok_blocks = tokens.reshape(seq_count, seq_len, model_width)
    back_blocks = cotangent.reshape(seq_count, seq_len, model_width)

    def pick(blocks):
        rows = jnp.einsum("skl,sld->skd", hot_low, blocks, preferred_element_type=f32)
        return rows.astype(bf16).reshape(-1, model_width)

    def place(blocks, rows):
        rows = rows.reshape(seq_count, top_count, model_width)
        spread = jnp.einsum("skl,skd->sld", hot_low, rows, preferred_element_type=f32).astype(bf16)
        taken = jnp.any(hot, axis=1)
        return jnp.where(taken[:, :, None], spread, blocks).reshape(-1, model_width)

    take_a = start(gather, chunk_a, z, split_a, True)
    take_c = start(gather_pairs, chunk_c, z)
    picked = pick(tok_blocks)
    back_rows = pick(back_blocks)
    seg_sel = jnp.sum(jnp.where(hot, segments[:, None, :], 0), axis=-1)
    seg_row, seg_col = seg_sel[:, None, :], seg_sel[:, :, None]
    spot = jnp.arange(model_width, dtype=jnp.int32)
    half, eighth = model_width // 2, model_width // 8
    flip = spot % half // eighth * 2 + spot // half
    order = ((me[0] ^ flip) * eighth + spot % eighth)[None]
    inputs = (picked, back_rows, seg_row, seg_col, order, chunk_b)
    inputs = tick([take_a], inputs)
    take_b = start(gather, inputs[-1], z, split_b, False)
    inputs = tick([take_a, take_b, take_c], inputs[:-1])
    inputs = tick([take_a, take_b], inputs)
    inputs = tick([take_a, take_b, take_c], inputs)

    all_a = whole(take_a, chunk_a, split_a)
    picked, back_rows = inputs[:2]
    order = inputs[4]
    state = attend(me, all_a, *inputs)
    state = tick([take_b, take_c], state)
    own, send, df, gate, vec, added, h2, all_qkv, all_out, qkv, probs = state
    early = start(exchange, send)
    h2 = stage([take_c], h2)
    h2 = tick([take_b, early], h2)
    (sib,) = early.result if paired else (send,)
    all_b = whole(take_b, chunk_b, split_b)
    g_own, g_send, g_sib, h2_pair, all_up, slope = climb(me, all_b, h2, sib, order)

    def give(chain, name, products, split):
        if paired:
            return Steps(chain(z, *outer(name, products, split)))
        grads = [dot_tn(uncut(one.value(), far.value()), two.value()) for one, two, far, _ in products]
        grad = jnp.concatenate(grads, axis=1)
        grad = lax.psum_scatter(grad, AXES, scatter_dimension=0, tiled=True)
        return grad, jnp.full((8, 128), jnp.sum(grad * grad))

    df_sib = jnp.concatenate([sib[2], sib[3]], axis=1)
    left_c = View(g_sib) if paired else View(g_send)
    give_c = give(
        scatter_pairs, "outer_c", [(View(g_own), View(df), left_c, View(df_sib))], split_c
    )
    slope = stage([give_c], slope)
    slope = tick([take_c], slope)
    slope = tick([take_c], slope)
    all_c = whole(take_c, chunk_c, split_c)
    du, all_down = descend(me, all_c, slope, df)
    dmiddle, da, dg2 = unclimb(all_up, du, picked, added, gate, back_rows, vec)
    new_rows, dlogit, dr = finish_mlp(
        all_down, g_own, g_send, picked, added, gate, back_rows
    )
    du, da, dmiddle, new_rows, dlogit = tick([give_c], (du, da, dmiddle, new_rows, dlogit))
    late_u = start(exchange, du)
    dqkv = unattend(all_out, da, qkv, probs)
    dqkv = tick([late_u], dqkv)
    (du_sib,) = late_u.result if paired else (du,)
    late_q = start(exchange, dqkv, da)
    views = [View(h2_pair, lead=place) for place in range(2)]
    if not paired:
        cols = h2.reshape(h2.shape[0], 4, 2, -1)
        views = [View(cols[:, :, core].reshape(h2.shape[0], -1)) for core in range(2)]
    give_b = give(
        scatter_pairs, "outer_b", [(views[0], View(du), views[1], View(du_sib))], split_b
    )
    dqkv = stage([give_b, give_c], dqkv)
    grad_rows, dg1 = finish_rows(all_qkv, dqkv, picked, back_rows, dmiddle, dlogit, vec)
    late_v = start(exchange, dg1, dg2, dr)
    dqkv = stage([late_v], dqkv)
    dqkv = tick([late_q, late_v], dqkv)
    dqkv_sib, da_sib = late_q.result if paired else (dqkv, da)
    products = [
        (View(own, lead=0), View(dqkv), View(sib, lead=0), View(dqkv_sib)),
        (View(own, lead=1), View(da), View(sib, lead=1), View(da_sib)),
    ]
    if paired:
        left, right = vector_columns(order, (dg1, dg2, dr), late_v.result)
        products.append(tuple(View(array, lead=part) for part in range(2) for array in (left, right)))
    give_a = give(scatter, "outer_a", products, split_a)
    grad_rows = stage([give_a], grad_rows)
    grad_rows = tick([give_b, give_c], grad_rows)
    grad_rows, new_rows = stage([give_b, give_c], (grad_rows, new_rows))
    mixed_rows = place(tok_blocks, new_rows)
    grad_rows, mixed_rows = tick([give_a], (grad_rows, mixed_rows))
    grad_rows = stage([give_a], grad_rows)
    grad_rows = tick([give_b, give_c], grad_rows)
    grad_rows = stage([give_b, give_c], grad_rows)
    grad_rows = tick([give_a, give_c], grad_rows)
    grad_rows = stage([give_a], grad_rows)
    input_grad = place(back_blocks, grad_rows)
    input_grad = tick([give_a, give_b], input_grad)
    input_grad = stage([give_a, give_b], input_grad)
    input_grad = tick([give_a, give_b], input_grad)
    if paired:
        give_a, give_b, give_c = give_a.result, give_b.result, give_c.result
        vec_grad = give_a[2]
        local_sq = give_a[1] + give_b[1] + give_c[1]
    else:
        rows = jnp.stack([dg1[0], dg2[0], dr[0]], axis=0)
        rows = lax.psum_scatter(rows, AXES, scatter_dimension=1, tiled=True)
        vec_grad = jnp.pad(rows, ((0, 5), (0, 128 - shard_width)))
        local_sq = give_a[1] + give_b[1] + give_c[1] + jnp.sum(rows * rows)
    squares = jnp.broadcast_to(local_sq[:1], (devices_all, 128))
    squares = lax.all_to_all(squares, AXES, 0, 0, tiled=True)
    params_all = 4 * model_width * model_width + 2 * model_width * ff_width + 3 * model_width
    selected_all = seq_count * top_count * devices_all
    clip_limit = limit_scale * math.sqrt(params_all * selected_all)
    norm, *news = update(
        squares,
        clip_limit,
        [
            View(give_a[0], qkv_width),
            View(give_a[0], model_width, qkv_width),
            View(give_b[0]),
            View(give_c[0]),
        ],
        [
            (w_qkv, m_qkv, v_qkv),
            (w_out, m_out, v_out),
            (w_up, m_up, v_up),
            (w_down, m_down, v_down),
        ],
        vec_grad,
        (m_vectors, v_vectors),
    )
    return (
        mixed_rows,
        input_grad,
        norm[0, 0],
        *news[0:12:3],
        *news[1:12:3],
        news[12],
        *news[2:12:3],
        news[13],
    )


def solution(mesh):
    placed = (
        P(("wide", "narrow"), None),
        P(("wide", "narrow"), None),
        P(("wide", "narrow"), None),
        P(("wide", "narrow"), None),
        P(("wide", "narrow"), None),
        P(("wide", "narrow"), None),
        P(("wide", "narrow"), None),
        P(("wide", "narrow"), None),
        P(None, ("wide", "narrow")),
        P(("wide", "narrow"), None),
        P(("wide", "narrow"), None),
        P(("wide", "narrow"), None),
        P(("wide", "narrow"), None),
        P(None, ("wide", "narrow")),
        P(("wide", "narrow"), None),
        P(("wide", "narrow"), None),
        P(("wide", "narrow"), None),
        P(("wide", "narrow"), None),
        P(None, ("wide", "narrow")),
    )
    paired = mesh.shape["wide"] == 8 and mesh.shape["narrow"] == 4
    return jax.shard_map(
        functools.partial(per_device, paired),
        mesh=mesh,
        in_specs=placed,
        out_specs=(
            P(("wide", "narrow"), None),
            P(("wide", "narrow"), None),
            P(),
            P(("wide", "narrow"), None),
            P(("wide", "narrow"), None),
            P(("wide", "narrow"), None),
            P(("wide", "narrow"), None),
            P(("wide", "narrow"), None),
            P(("wide", "narrow"), None),
            P(("wide", "narrow"), None),
            P(("wide", "narrow"), None),
            P(None, ("wide", "narrow")),
            P(("wide", "narrow"), None),
            P(("wide", "narrow"), None),
            P(("wide", "narrow"), None),
            P(("wide", "narrow"), None),
            P(None, ("wide", "narrow")),
        ),
        check_vma=False,
    )
```

```python
import functools
import math

import jax
import jax.numpy as jnp
from jax import lax
from jax.experimental import pallas as pl
from jax.experimental.pallas import tpu as pltpu
from jax.sharding import PartitionSpec as P

HEAD_DIM = 64


norm_eps = 1e-06
beta_one = 0.9
beta_two = 0.999
adam_eps = 1e-08
learn_rate = 0.03
decay_rate = 0.1
adam_step = 10
limit_scale = 0.01
masked_out = -1e30
AXES = ("wide", "narrow")


def moment_update(grad_part, first, second):
    first_new = beta_one * first + (1.0 - beta_one) * grad_part
    second_new = beta_two * second + (1.0 - beta_two) * grad_part * grad_part
    return (first_new, second_new)


def adam_update(master, grad_part, first, second):
    first_new, second_new = moment_update(grad_part, first, second)
    first_hat = first_new / (1.0 - beta_one**adam_step)
    second_hat = second_new / (1.0 - beta_two**adam_step)
    master_new = master - learn_rate * (
        first_hat / (jnp.sqrt(second_hat) + adam_eps) + decay_rate * master
    )
    return (master_new, first_new, second_new)


f32, bf16 = jnp.float32, jnp.bfloat16
PAIR = 2 * HEAD_DIM
head_scale = HEAD_DIM ** (-0.5)
KEEP_L = ((0, 0, 0), (0, 1, 0))
KEEP_R = ((0, 0, 1), (1, 0, 1))
FAR_L = ((1, 0, 0), (1, 1, 0))
FAR_R = ((0, 1, 1), (1, 1, 1))
GROUPS = (KEEP_L, KEEP_R, FAR_L, FAR_R)


def kernel(body, name, outs, args, kinds, scratch=(), limit=24, loose=0):
    spaces = {"s": pltpu.SMEM, "v": pltpu.VMEM, "h": pltpu.VMEM, "a": pltpu.HBM}
    held = len(outs) - loose
    return pl.pallas_call(
        body,
        out_shape=[
            jax.ShapeDtypeStruct(*out) if place < held else pltpu.HBM(*out)
            for place, out in enumerate(outs)
        ],
        in_specs=[pl.BlockSpec(memory_space=spaces[kind]) for kind in kinds],
        out_specs=[
            pl.BlockSpec(memory_space=pltpu.VMEM if place < held else pltpu.HBM)
            for place in range(len(outs))
        ],
        scratch_shapes=list(scratch),
        compiler_params=pltpu.CompilerParams(vmem_limit_bytes=limit << 20),
        cost_estimate=pl.CostEstimate(flops=1, bytes_accessed=1, transcendentals=0),
        name=name,
    )(
        *(
            pltpu.with_memory_space_constraint(arg, pltpu.HBM) if kind in "ah" else arg
            for arg, kind in zip(args, kinds)
        )
    )


def each_block(pieces):
    for core in range(2):
        for group, flips in enumerate(GROUPS):
            for place, flip in enumerate(flips):
                yield flip[0] * 4 + flip[1] * 2 + core, flip[2], pieces[core * 4 + group].at[place]


def start_all(copies):
    for copy in copies:
        copy.start()


def wait_all(copies):
    for copy in copies:
        copy.wait()


def fetch(pieces, me, sem, base, left, right):
    copies = []
    for flip, half, block in each_block(pieces):
        rows = block.shape[0]
        start = pl.multiple_of((me ^ flip) * rows, rows)
        for target, column, out_column, width in (left, right)[half]:
            copies.append(
                pltpu.make_async_copy(
                    block.at[:, pl.ds(column, width)],
                    target.at[pl.ds(start, rows), pl.ds(out_column, width)],
                    sem.at[base + len(copies)],
                )
            )
    return copies


def dot_nt(left, right):
    return lax.dot_general(left, right, (((1,), (1,)), ((), ())), preferred_element_type=f32)


def dot_tn(left, right):
    return lax.dot_general(left, right, (((0,), (0,)), ((), ())), preferred_element_type=f32)


def dot_nn(left, right):
    return jnp.dot(left, right, preferred_element_type=f32)


def mean_last(array):
    return jnp.mean(array, axis=-1, keepdims=True)


def sum_rows(array):
    return jnp.sum(array, axis=0, keepdims=True)


def head_masks(dtype):
    lanes = lax.broadcasted_iota(jnp.int32, (1, PAIR), 1)
    first = (lanes < HEAD_DIM).astype(f32).astype(dtype)
    return first, (1 - first).astype(dtype)


def two_heads(pair, masks):
    return jnp.concatenate([pair * masks[0], pair * masks[1]], axis=0)


def one_pair(stacked, masks):
    rows = stacked.shape[0] // 2
    return stacked[:rows] * masks[0] + stacked[rows:] * masks[1]


def gather_input(w_qkv, w_out, vectors):
    rows, first = w_qkv.shape
    second = w_out.shape[1]

    def body(qkv_ref, out_ref, vec_ref, chunk_ref, turned):
        chunk_ref[:, :first] = qkv_ref[...].astype(bf16)
        chunk_ref[:, first : first + second] = out_ref[...].astype(bf16)
        turned[...] = jnp.zeros_like(turned)
        turned[:3] = vec_ref[...]
        same = lax.broadcasted_iota(jnp.int32, (rows, rows), 0) == lax.broadcasted_iota(
            jnp.int32, (rows, rows), 1
        )
        columns = dot_nt(same.astype(f32).astype(bf16), turned[...].astype(bf16))
        chunk_ref[:, first + second :] = columns.astype(bf16)

    outs = [((rows, first + second + 128), bf16)]
    scratch = [pltpu.VMEM((128, rows), f32)]
    return kernel(body, "gather_input", outs, (w_qkv, w_out, vectors), "hhh", scratch)[0]


def attend(me, pieces, picked, back_rows, seg_row, seg_col, order):
    rows, width = picked.shape
    seqs = seg_row.shape[0]
    top = rows // seqs
    pairs = width // PAIR
    first = pieces[0].shape[2]
    rest = 3 * width - first
    spare = pieces[1].shape[2] - rest - width

    def body(me_ref, *refs):
        blocks, refs = refs[:8], refs[8:]
        x_ref, dy_ref, seg_row_ref, seg_col_ref, order_ref = refs[:5]
        own_ref, send_ref, df_ref, gate_ref, vec_ref, add_ref, h2_ref = refs[5:12]
        all_ref, out_ref, qkv_out, prob_out = refs[12:16]
        w_qkv, w_out, w_vec, qkv_ref, prob_ref, att_ref, sem = refs[16:]
        vec_copies = fetch(blocks, me_ref[0], sem, 0, (), ((w_vec, rest + width, 0, spare),))
        left = fetch(blocks, me_ref[0], sem, 8, ((w_qkv, 0, 0, first),), ())
        right = fetch(blocks, me_ref[0], sem, 16, (), ((w_qkv, 0, first, rest),))
        out_copies = fetch(blocks, me_ref[0], sem, 24, (), ((w_out, rest, 0, width),))
        start_all(vec_copies + left + right + out_copies)
        wait_all(vec_copies)
        vec = w_vec[...].astype(f32).T[:8]
        vec_ref[...] = vec
        x = x_ref[...].astype(f32)
        h1 = (x * lax.rsqrt(mean_last(x * x) + norm_eps) * vec[0:1]).astype(bf16)
        for copies, start, count in ((left, 0, first), (right, first, rest)):
            wait_all(copies)
            for part in range(start, start + count, 384):
                lanes = pl.ds(part, 384)
                qkv_ref[:, lanes] = dot_nn(h1, w_qkv[:, lanes]).astype(bf16)
        stored = [
            pltpu.make_async_copy(w_qkv, all_ref, sem.at[32]),
            pltpu.make_async_copy(qkv_ref, qkv_out, sem.at[33]),
            pltpu.make_async_copy(w_out, out_ref, sem.at[34]),
        ]
        wait_all(out_copies)
        start_all(stored)
        masks, masks_f = head_masks(bf16), head_masks(f32)
        ordered_pairs = lax.broadcasted_iota(jnp.int32, (top, top), 1) <= lax.broadcasted_iota(
            jnp.int32, (top, top), 0
        )
        for seq in range(seqs):
            here = pl.ds(seq * top, top)
            seen = ordered_pairs & (seg_col_ref[seq] == seg_row_ref[seq])
            hidden = jnp.where(seen, 0.0, masked_out)
            hidden = jnp.concatenate([hidden, hidden], axis=0)
            for pair in range(pairs):
                q, k, v = (
                    qkv_ref[here, pl.ds(part * width + pair * PAIR, PAIR)] for part in range(3)
                )
                scores = dot_nt(two_heads(q, masks), k) * head_scale
                scores = jnp.where(hidden < 0.0, masked_out, scores)
                power = jnp.exp(scores - jnp.max(scores, axis=-1, keepdims=True))
                probs = power / jnp.sum(power, axis=-1, keepdims=True)
                prob_ref[seq * pairs + pair] = probs
                mixed = one_pair(dot_nn(probs.astype(bf16), v), masks_f)
                att_ref[here, pl.ds(pair * PAIR, PAIR)] = mixed.astype(bf16)
            group = pl.ds(seq * pairs, pairs)
            stored.append(
                pltpu.make_async_copy(prob_ref.at[group], prob_out.at[group], sem.at[35 + seq])
            )
            stored[-1].start()
        gate = jax.nn.sigmoid(jnp.sum(x * vec[2:3], axis=-1, keepdims=True))
        gate_ref[...] = jnp.broadcast_to(gate, gate_ref.shape)
        df = (gate * dy_ref[...].astype(f32)).astype(bf16)
        df_ref[...] = df
        added = dot_nn(att_ref[...], w_out[...])
        add_ref[...] = added
        middle = x + added
        h2 = (middle * lax.rsqrt(mean_last(middle * middle) + norm_eps) * vec[1:2]).astype(bf16)
        h2_ref[...] = h2
        for half in range(2):
            lanes = slice(half * (width // 2), (half + 1) * (width // 2))
            send_ref[2 + half] = df[:, lanes]
            send_ref[4 + half] = h2[:, lanes]
        chosen = one_hot_columns(order_ref)
        for place, array in enumerate((h1, att_ref[...])):
            parted = dot_nn(array, chosen).astype(bf16)
            own_ref[place] = parted[:, : width // 2]
            send_ref[place] = parted[:, width // 2 :]
        wait_all(stored)

    outs = [
        ((2, rows, width // 2), bf16),
        ((6, rows, width // 2), bf16),
        ((rows, width), bf16),
        ((rows, 128), f32),
        ((8, width), f32),
        ((rows, width), f32),
        ((rows, width), bf16),
        ((width, 3 * width), bf16),
        ((width, width), bf16),
        ((rows, 3 * width), bf16),
        ((seqs * pairs, 2 * top, top), f32),
    ]
    scratch = [
        pltpu.VMEM((width, 3 * width), bf16),
        pltpu.VMEM((width, width), bf16),
        pltpu.VMEM((width, spare), bf16),
        pltpu.VMEM((rows, 3 * width), bf16),
        pltpu.VMEM((seqs * pairs, 2 * top, top), f32),
        pltpu.VMEM((rows, width), bf16),
        pltpu.SemaphoreType.DMA((35 + seqs,)),
    ]
    args = (me, *pieces, picked, back_rows, seg_row, seg_col, order)
    return kernel(body, "attend", outs, args, "s" + "a" * 8 + "vvvvv", scratch, 26, 4)


def one_hot_columns(order_ref):
    width = order_ref.shape[1]
    chosen = lax.broadcasted_iota(jnp.int32, (width, width), 0) == order_ref[...]
    return chosen.astype(f32).astype(bf16)


def climb(me, pieces, h2, sib, order):
    rows, width = h2.shape
    first = pieces[0].shape[2]
    block = 2 * first // 8

    def body(me_ref, *refs):
        blocks, refs = refs[:8], refs[8:]
        h2_ref, sib_ref, order_ref = refs[:3]
        own_ref, send_ref, far_ref, pair_ref, up_ref, slope_out = refs[3:9]
        w_up, slope_ref, both_ref, sem = refs[9:]
        copies = fetch(
            blocks, me_ref[0], sem, 0, ((w_up, 0, 0, first),), ((w_up, 0, first, first),)
        )
        start_all(copies)
        both_ref[:rows] = h2_ref[...]
        for half in range(2):
            lanes = pl.ds(half * (width // 2), width // 2)
            both_ref[rows:, lanes] = sib_ref[4 + half]
        chosen = one_hot_columns(order_ref)[:, : width // 2]
        parted = dot_nn(both_ref[...], chosen).astype(bf16)
        pair_ref[0] = parted[:rows]
        pair_ref[1] = parted[rows:]
        wait_all(copies)
        stored = [pltpu.make_async_copy(w_up, up_ref, sem.at[16])]
        start_all(stored)
        scale = math.sqrt(2.0 / math.pi)
        for flip in range(8):
            start = pl.multiple_of((me_ref[0] ^ flip) * block, block)
            place = flip // 2
            lanes = pl.ds(place * block, block)
            weights = w_up[:, pl.ds(start, block)]
            u = dot_nn(both_ref[:rows], weights)
            square = u * u
            bent = jnp.tanh(scale * (u + 0.044715 * (square * u)))
            half_up = 0.5 * (1.0 + bent)
            target = send_ref if flip % 2 else own_ref
            target[:, lanes] = (u * half_up).astype(bf16)
            where = (flip % 2) * 4 + place
            slope_ref[where] = half_up + (0.5 * u) * (1.0 - bent * bent) * (
                scale * (1.0 + (3.0 * 0.044715) * square)
            )
            stored.append(
                pltpu.make_async_copy(
                    slope_ref.at[where], slope_out.at[where], sem.at[17 + flip]
                )
            )
            stored[-1].start()
            if flip % 2 == 0:
                u = dot_nn(both_ref[rows:], weights)
                bent = jnp.tanh(scale * (u + 0.044715 * (u * u * u)))
                far_ref[:, lanes] = (0.5 * u * (1.0 + bent)).astype(bf16)
        wait_all(stored)

    outs = [
        ((rows, 4 * block), bf16),
        ((rows, 4 * block), bf16),
        ((rows, 4 * block), bf16),
        ((2, rows, width // 2), bf16),
        ((width, 8 * block), bf16),
        ((8, rows, block), f32),
    ]
    scratch = [
        pltpu.VMEM((width, 8 * block), bf16),
        pltpu.VMEM((8, rows, block), f32),
        pltpu.VMEM((2 * rows, width), bf16),
        pltpu.SemaphoreType.DMA((25,)),
    ]
    args = (me, *pieces, h2, sib, order)
    return kernel(body, "climb", outs, args, "s" + "a" * 8 + "vvv", scratch, 26, 2)


def vector_columns(order, mine, other):
    width = order.shape[1]
    half = width // 2

    def body(order_ref, *refs):
        ins, (left, right, rows) = refs[:6], refs[6:]
        chosen = one_hot_columns(order_ref)[:, :half]
        rows[...] = jnp.zeros_like(rows)
        for place in range(3):
            rows[place : place + 1] = ins[place][0:1] + ins[3 + place][0:1]
        columns = rows[...].T.astype(bf16)
        for part in range(2):
            left[part] = chosen[part * half : (part + 1) * half]
            right[part] = columns[part * half : (part + 1) * half]

    outs = [((2, half, half), bf16), ((2, half, 128), bf16)]
    scratch = [pltpu.VMEM((128, width), f32)]
    args = (order, *mine, *other)
    return kernel(body, "vector_columns", outs, args, "v" * 7, scratch)


class View:
    def __init__(self, array, columns=None, first=0, lead=None):
        self.array, self.first, self.lead = array, first, lead
        self.columns = columns or array.shape[-1]

    def value(self):
        array = self.array if self.lead is None else self.array[self.lead]
        return array[:, self.first : self.first + self.columns]

    def read(self, ref, first, columns):
        lanes = pl.ds(self.first + first, columns)
        return ref[:, lanes] if self.lead is None else ref[self.lead, :, lanes]


def outer(name, products, split):
    length = products[0][0].columns // 4
    total = sum(product[1].columns for product in products)
    widths = (split, total - split)
    order = ((2, 3), (1, 3), (0, 1), (0, 2))

    def body(*refs):
        ins, outs = refs[: 4 * len(products)], refs[4 * len(products) :]
        base = 0
        for number, product in enumerate(products):
            reads = [
                functools.partial(view.read, ref)
                for view, ref in zip(product, ins[4 * number : 4 * number + 4])
            ]
            columns = product[1].columns
            step = min(768, columns)
            for start in range(0, columns, step):
                for first in range(0, 4 * length, 384):
                    value = dot_tn(reads[0](first, 384), reads[1](start, step))
                    value += dot_tn(reads[2](first, 384), reads[3](start, step))
                    for block in range(first // length, (first + 384) // length):
                        part = value[block * length - first : (block + 1) * length - first]
                        for half in range(2):
                            low = max(base + start, half * split)
                            high = min(base + start + step, split + half * (total - split))
                            if high <= low:
                                continue
                            piece = part[:, low - base - start : high - base - start]
                            out_lanes = pl.ds(low - half * split, high - low)
                            for out in (half, 2 + half):
                                if block in order[out]:
                                    outs[out][order[out].index(block), :, out_lanes] = piece.astype(
                                        outs[out].dtype
                                    )
            base += columns

    outs = [
        ((2, length, widths[out % 2]), bf16 if out < 2 else f32) for out in range(4)
    ]
    args = [view.array for product in products for view in product]
    return kernel(body, name, outs, args, "v" * len(args))


def descend(me, pieces, slope, df):
    rows, width = df.shape
    block = slope.shape[2]

    def body(me_ref, *refs):
        blocks, refs = refs[:8], refs[8:]
        slope_in, df_ref, du_ref, down_ref, w_down, slope_ref, sem = refs
        copies = [[] for _ in range(8)]
        for flip, side, part in each_block(blocks):
            lanes = pl.ds(side * (width // 2), width // 2)
            place = (flip % 2) * 4 + flip // 2
            target = w_down.at[pl.ds(place * block, block), lanes]
            copies[place].append(
                pltpu.make_async_copy(part, target, sem.at[place * 2 + side])
            )
        for place, pair in enumerate(copies):
            pair.append(
                pltpu.make_async_copy(
                    slope_in.at[place], slope_ref.at[place], sem.at[17 + place]
                )
            )
            start_all(pair)
        for place in range(8):
            wait_all(copies[place])
            flip = place % 4 * 2 + place // 4
            start = pl.multiple_of((me_ref[0] ^ flip) * block, block)
            dg = dot_nt(df_ref[...], w_down[pl.ds(place * block, block)])
            du_ref[:, pl.ds(start, block)] = (dg * slope_ref[place]).astype(bf16)
        stored = pltpu.make_async_copy(w_down, down_ref, sem.at[16])
        stored.start()
        stored.wait()

    outs = [((rows, 8 * block), bf16), ((8 * block, width), bf16)]
    scratch = [
        pltpu.VMEM((8 * block, width), bf16),
        pltpu.VMEM((8, rows, block), f32),
        pltpu.SemaphoreType.DMA((25,)),
    ]
    args = (me, *pieces, slope, df)
    return kernel(body, "descend", outs, args, "s" + "a" * 9 + "v", scratch, 24, 1)


def unclimb(w_up, du, picked, added, gate, back_rows, vec):
    rows, width = picked.shape

    def body(up_ref, du_ref, x_ref, add_ref, gate_ref, dy_ref, vec_ref, dm_ref, da_ref, dg_ref):
        dh = dot_nt(du_ref[...], up_ref[...])
        middle = x_ref[...].astype(f32) + add_ref[...]
        inverse = lax.rsqrt(mean_last(middle * middle) + norm_eps)
        unit = middle * inverse
        dg_ref[...] = jnp.broadcast_to(sum_rows(dh * unit), dg_ref.shape)
        scaled = dh * vec_ref[1:2]
        dm = inverse * (scaled - unit * mean_last(scaled * unit))
        dm_ref[...] = dm
        da_ref[...] = (gate_ref[:, 0:1] * dy_ref[...].astype(f32) + dm).astype(bf16)

    outs = [((rows, width), f32), ((rows, width), bf16), ((8, width), f32)]
    args = (w_up, du, picked, added, gate, back_rows, vec)
    return kernel(body, "unclimb", outs, args, "v" * 7)


def unattend(w_out, da, qkv, probs):
    rows, width = da.shape
    top = probs.shape[2]
    seqs, pairs = rows // top, width // PAIR

    def body(out_ref, da_ref, qkv_ref, prob_ref, dqkv_ref, do_ref):
        do_ref[...] = dot_nt(da_ref[...], out_ref[...]).astype(bf16)
        masks, masks_f = head_masks(bf16), head_masks(f32)
        for seq in range(seqs):
            here = pl.ds(seq * top, top)
            for pair in range(pairs):
                lanes = [pl.ds(part * width + pair * PAIR, PAIR) for part in range(3)]
                q, k, v = (qkv_ref[here, part] for part in lanes)
                do = two_heads(do_ref[here, pl.ds(pair * PAIR, PAIR)], masks)
                probs = prob_ref[seq * pairs + pair]
                dprobs = dot_nt(do, v)
                dscores = probs * (dprobs - jnp.sum(dprobs * probs, axis=-1, keepdims=True))
                dscores = dscores.astype(bf16)
                dq = one_pair(dot_nn(dscores, k), masks_f) * head_scale
                dk = dot_tn(dscores, two_heads(q, masks)) * head_scale
                dv = dot_tn(probs.astype(bf16), do)
                for part, value in zip(lanes, (dq, dk, dv)):
                    dqkv_ref[here, part] = value.astype(bf16)

    scratch = [pltpu.VMEM((rows, width), bf16)]
    outs = [((rows, 3 * width), bf16)]
    return kernel(body, "unattend", outs, (w_out, da, qkv, probs), "vvvv", scratch)[0]


def finish_mlp(w_down, own, send, picked, added, gate, back_rows):
    rows, width = picked.shape
    half = w_down.shape[0] // 2

    def body(down_ref, own_ref, send_ref, x_ref, add_ref, gate_ref, dy_ref, *outs):
        new_ref, dlogit_ref, dr_ref = outs
        out = dot_nn(own_ref[:, :half], down_ref[:half])
        out += dot_nn(send_ref[:, :half], down_ref[half:])
        both = add_ref[...] + out
        x = x_ref[...].astype(f32)
        gate = gate_ref[:, 0:1]
        new_ref[...] = (x + gate * both).astype(bf16)
        dlogit = jnp.sum(dy_ref[...].astype(f32) * both, axis=-1, keepdims=True)
        dlogit = dlogit * gate * (1.0 - gate)
        dlogit_ref[...] = jnp.broadcast_to(dlogit, dlogit_ref.shape)
        dr_ref[...] = jnp.broadcast_to(sum_rows(dlogit * x), dr_ref.shape)

    outs = [((rows, width), bf16), ((rows, 128), f32), ((8, width), f32)]
    args = (w_down, own, send, picked, added, gate, back_rows)
    return kernel(body, "finish_mlp", outs, args, "v" * 7)


def finish_rows(w_qkv, dqkv, picked, back_rows, dmiddle, dlogit, vec):
    rows, width = picked.shape

    def body(all_ref, dqkv_ref, x_ref, dy_ref, dm_ref, dlogit_ref, vec_ref, grad_ref, dg_ref):
        dh = dot_nt(dqkv_ref[...], all_ref[...])
        x = x_ref[...].astype(f32)
        inverse = lax.rsqrt(mean_last(x * x) + norm_eps)
        unit = x * inverse
        dg_ref[...] = jnp.broadcast_to(sum_rows(dh * unit), dg_ref.shape)
        scaled = dh * vec_ref[0:1]
        dx = inverse * (scaled - unit * mean_last(scaled * unit))
        grad = dy_ref[...].astype(f32) + dm_ref[...] + dx + dlogit_ref[:, 0:1] * vec_ref[2:3]
        grad_ref[...] = grad.astype(bf16)

    outs = [((rows, width), bf16), ((8, width), f32)]
    args = (w_qkv, dqkv, picked, back_rows, dmiddle, dlogit, vec)
    return kernel(body, "finish_rows", outs, args, "v" * 7)


def join_z(z, own, others, split):
    rows, width = own.shape

    def body(z_ref, *refs):
        ins, left_ref, right_ref, total = refs[:4], *refs[4:]
        for flip, block in enumerate(ins):
            start = pl.multiple_of((z_ref[0] ^ flip) * rows, rows)
            total[pl.ds(start, rows)] = block[...].astype(f32)
        left_ref[...] = total[:, :split].astype(bf16)
        right_ref[...] = total[:, split:].astype(bf16)

    outs = [((4 * rows, split), bf16), ((4 * rows, width - split), bf16)]
    scratch = [pltpu.VMEM((4 * rows, width), f32)]
    return kernel(body, "join_z", outs, (z, own, *others), "svvvv", scratch)


def join_z_pairs(z, left, right, near_l, near_r, others):
    rows, width = left.shape

    def body(z_ref, *refs):
        mine, others, outs = refs[:4], refs[4:7], refs[7:]
        for flip in range(4):
            start = pl.ds(pl.multiple_of((z_ref[0] ^ flip) * rows, rows), rows)
            for place in range(4):
                block = others[flip - 1][place] if flip else mine[place][...]
                outs[place // 2][place % 2, start] = block

    outs = [((2, 4 * rows, width), bf16)] * 2
    args = (z, left, near_l, right, near_r, *others)
    return kernel(body, "join_z_pairs", outs, args, "svvvvvvv")


def add_z_pairs(z, keep_l, keep_r, other_l, other_r):
    pair, rows, width = keep_l.shape
    part = rows // 4

    def body(z_ref, keep_l, keep_r, other_l, other_r, mine, send, total):
        for half, (keep, other) in enumerate(((keep_l, other_l), (keep_r, other_r))):
            for place in range(pair):
                total[half * pair + place] = keep[place] + other[place].astype(f32)
        for flip in range(4):
            start = pl.multiple_of((z_ref[0] ^ flip) * part, part)
            out = (mine, send)[flip % 2]
            out[flip // 2] = total[:, pl.ds(start, part)].astype(out.dtype)

    outs = [((2, 4, part, width), f32), ((2, 4, part, width), bf16)]
    scratch = [pltpu.VMEM((4, rows, width), f32)]
    args = (z, keep_l, keep_r, other_l, other_r)
    return kernel(body, "add_z_pairs", outs, args, "svvvv", scratch)


def add_four(mine, other):
    def body(mine, other, send_l, send_r, keep):
        def total(place):
            return mine[place] + other[place].astype(f32)

        width = mine.shape[2]
        keep[:, :width] = total(0)
        keep[:, width:] = total(2)
        send_l[...] = total(1).astype(bf16)
        send_r[...] = total(3).astype(bf16)

    _, rows, width = mine.shape
    outs = [((rows, width), bf16)] * 2 + [((rows, 2 * width), f32)]
    return kernel(body, "add_four", outs, (mine, other), "vv")


def add_pairs(keep_l, keep_r, other_l, other_r):
    def body(keep_l, keep_r, other_l, other_r, send_l, send_r, left, right):
        for keep, other, send, mine in (
            (keep_l, other_l, send_l, left),
            (keep_r, other_r, send_r, right),
        ):
            send[...] = (keep[1] + other[1].astype(f32)).astype(bf16)
            mine[...] = keep[0] + other[0].astype(f32)

    shapes = [keep_l.shape[1:], keep_r.shape[1:]]
    outs = [(shape, kind) for kind in (bf16, f32) for shape in shapes]
    return kernel(body, "add_pairs", outs, (keep_l, keep_r, other_l, other_r), "vvvv")


def add_split(z, keep_l, keep_r, other_l, other_r):
    rows, split = keep_l.shape
    width = split + keep_r.shape[1]
    part = rows // 4

    def body(z_ref, keep_l, keep_r, other_l, other_r, mine, send, total):
        total[:, :split] = keep_l[...] + other_l[...].astype(f32)
        total[:, split:] = keep_r[...] + other_r[...].astype(f32)
        for flip in range(4):
            start = pl.multiple_of((z_ref[0] ^ flip) * part, part)
            out = (mine, send)[flip % 2]
            out[flip // 2] = total[pl.ds(start, part)].astype(out.dtype)

    outs = [((2, part, width), f32), ((2, part, width), bf16)]
    scratch = [pltpu.VMEM((rows, width), f32)]
    args = (z, keep_l, keep_r, other_l, other_r)
    return kernel(body, "add_split", outs, args, "svvvv", scratch)


def add_next(keep, other):
    def body(keep, other, mine, send):
        mine[...] = keep[0] + other[0].astype(f32)
        send[...] = (keep[1] + other[1].astype(f32)).astype(bf16)

    shape = keep.shape[1:]
    return kernel(body, "add_next", [(shape, f32), (shape, bf16)], (keep, other), "vv")


def settle_halves(keep, other_l, other_r):
    def body(keep, other_l, other_r, grad, square):
        width = other_l.shape[1]
        total = None
        for half, other in enumerate((other_l, other_r)):
            lanes = pl.ds(half * width, width)
            value = keep[:, lanes] + other[...].astype(f32)
            grad[:, lanes] = value
            part = jnp.sum(value * value)
            total = part if total is None else total + part
        square[...] = jnp.full(square.shape, total)

    outs = [(keep.shape, f32), ((8, 128), f32)]
    return kernel(body, "settle_halves", outs, (keep, other_l, other_r), "vvv")


def settle_z(mine, other, squares, devices):
    rows, width = mine.shape

    def body(mine, other, *refs):
        more, (grad, square, last, turned) = refs[: len(squares)], refs[len(squares) :]
        value = mine[...] + other[...].astype(f32)
        grad[...] = value
        total = jnp.sum(value * value)
        for ref in more:
            total = total + ref[0:1, :]
        square[...] = jnp.broadcast_to(total, square.shape)
        turned[...] = jnp.zeros_like(turned)
        turned[:rows] = value[:, width - 128 :]
        last[...] = turned[...].T[:8]

    outs = [(mine.shape, f32), ((devices, 128), f32), ((8, 128), f32)]
    scratch = [pltpu.VMEM((128, 128), f32)]
    args = (mine, other, *squares)
    return kernel(body, "settle_z", outs, args, "v" * len(args), scratch)


def update(squares, limit, grads, states, vec_grad, vec_states):
    count = len(grads)

    def body(square_ref, *refs):
        grad_refs, refs = refs[:count], refs[count:]
        state_refs, refs = refs[: 3 * count], refs[3 * count :]
        vec_ref, vec_m, vec_v, norm_ref, out_refs = *refs[:4], refs[4:]
        norm = jnp.sqrt(jnp.sum(square_ref[...], axis=0, keepdims=True)[:, 0:1])
        norm_ref[...] = norm
        factor = jnp.minimum(1.0, limit / (norm + 1e-06))
        for place in range(count):
            w, m, v = (ref[...] for ref in state_refs[3 * place : 3 * place + 3])
            grad = grads[place].read(grad_refs[place], 0, grads[place].columns) * factor
            for ref, value in zip(out_refs[3 * place :], adam_update(w, grad, m, v)):
                ref[...] = value
        grad = vec_ref[:3, : vec_m.shape[1]] * factor
        first, second = moment_update(grad, vec_m[...], vec_v[...])
        out_refs[-2][...] = first
        out_refs[-1][...] = second

    flat = [array for state in states for array in state]
    outs = [((1, 1), f32)] + [(array.shape, f32) for array in (*flat, *vec_states)]
    args = (squares, *(grad.array for grad in grads), *flat, vec_grad, *vec_states)
    return kernel(body, "update", outs, args, "v" * len(args), (), 32)


class Steps:
    def __init__(self, chain):
        self.chain = chain
        self.result = None
        self.launch(next(chain))

    def launch(self, step):
        self.flips = [flip for _, flip in step]
        self.given = [array for array, _ in step]

    def advance(self, arrays):
        try:
            self.launch(self.chain.send(arrays))
        except StopIteration as stop:
            self.flips, self.given, self.result = (), (), stop.value


def slot(chains, value):
    arrays = [
        [swap(array, flip) for array, flip in zip(chain.given, chain.flips)] for chain in chains
    ]
    arrays, value = lax.optimization_barrier((arrays, value))
    for chain, array in zip(chains, arrays):
        chain.advance(array)
    return value


def ready(chains, value):
    arrays, value = lax.optimization_barrier(([chain.given for chain in chains], value))
    for chain, array in zip(chains, arrays):
        chain.given = array
    return value


def swap(array, bit):
    count = lax.axis_size("wide") * lax.axis_size("narrow")
    return lax.ppermute(array, AXES, [(i, i ^ bit) for i in range(count)])


def exchange(*arrays):
    return (yield [(array, 4) for array in arrays])


def around_z(shard, at_once):
    if at_once:
        return (yield [(shard, flip) for flip in (1, 2, 3)])
    (two,) = yield [(shard, 2)]
    (both,) = yield [(jnp.stack([shard, two]), 1)]
    return both[0], two, both[1]


def gather(shard, z, split, at_once):
    others = yield from around_z(shard, at_once)
    left, right = join_z(z, shard, others, split)
    near_l, near_r = yield [(left, 8), (right, 16)]
    return (yield from spread(jnp.stack([left, near_l]), jnp.stack([right, near_r])))


def gather_pairs(shard, z):
    half = shard.shape[1] // 2
    left, right = shard[:, :half], shard[:, half:]
    near_l, near_r = yield [(left, 8), (right, 16)]
    others = yield from around_z(jnp.stack([left, near_l, right, near_r]), False)
    keep_l, keep_r = join_z_pairs(z, left, right, near_l, near_r, others)
    return (yield from spread(keep_l, keep_r))


def spread(keep_l, keep_r):
    far_l, far_r, *near = yield [(keep_l, 16), (keep_r, 8), (keep_l, 4), (keep_r, 4)]
    far = yield [(far_l, 4), (far_r, 4)]
    return (keep_l, keep_r, far_l, far_r, *near, *far)


def scatter(z, send_l, send_r, keep_l, keep_r):
    other_l, other_r = yield [(send_l, 16), (send_r, 8)]
    send_l, send_r, left, right = add_pairs(keep_l, keep_r, other_l, other_r)
    other_l, other_r = yield [(send_l, 8), (send_r, 16)]
    mine, send = add_split(z, left, right, other_l, other_r)
    (other,) = yield [(send, 1)]
    mine, send = add_next(mine, other)
    (other,) = yield [(send, 2)]
    return mine, other


def scatter_pairs(z, send_l, send_r, keep_l, keep_r):
    other_l, other_r = yield [(send_l, 16), (send_r, 8)]
    mine, send = add_z_pairs(z, keep_l, keep_r, other_l, other_r)
    (other,) = yield [(send, 1)]
    mine, send = add_next(mine, other)
    (other,) = yield [(send, 2)]
    send_l, send_r, keep = add_four(mine, other)
    other_l, other_r = yield [(send_l, 8), (send_r, 16)]
    return settle_halves(keep, other_l, other_r)


def cut(whole, split):
    blocks = whole.reshape(8, whole.shape[0] // 8, whole.shape[1])
    sides = (blocks[..., :split], blocks[..., split:])
    return tuple(
        jnp.stack([sides[flip[2]][flip[0] * 4 + flip[1] * 2 + core] for flip in flips])
        for core in range(2)
        for flips in GROUPS
    )


def uncut(own, send):
    parts = jnp.stack([array.reshape(array.shape[0], 4, -1) for array in (own, send)], axis=2)
    return parts.reshape(own.shape[0], -1)


def per_device(
    paired,
    tokens,
    cotangent,
    segments,
    picks,
    w_qkv,
    w_out,
    w_up,
    w_down,
    vectors,
    m_qkv,
    m_out,
    m_up,
    m_down,
    m_vectors,
    v_qkv,
    v_out,
    v_up,
    v_down,
    v_vectors,
):
    devices_all = lax.axis_size("wide") * lax.axis_size("narrow")
    lane = lax.axis_index(AXES)
    seq_count, top_count = picks.shape
    seq_len = segments.shape[1]
    model_width = tokens.shape[1]
    qkv_width = w_qkv.shape[1]
    ff_width = w_up.shape[1]
    shard_width = vectors.shape[1]
    split_a, split_b, split_c = 2 * model_width, ff_width // 2, model_width // 2
    z = (lane & 3).reshape(1)
    me = (lane >> 2).reshape(1) if paired else jnp.zeros((1,), jnp.int32)

    chunk_a = gather_input(w_qkv, w_out, vectors)
    chunk_b = w_up.astype(bf16)
    chunk_c = w_down.astype(bf16)

    def start(chain, *args):
        return Steps(chain(*args)) if paired else None

    def tick(chains, value):
        return slot(chains, value) if paired else value

    def stage(chains, value):
        return ready(chains, value) if paired else value

    def whole(take, chunk, split):
        if paired:
            return take.result
        return cut(lax.all_gather(chunk, AXES, axis=0, tiled=True), split)

    hot = picks[:, :, None] == jnp.arange(seq_len, dtype=jnp.int32)[None, None, :]
    hot_low = hot.astype(bf16)
    tok_blocks = tokens.reshape(seq_count, seq_len, model_width)
    back_blocks = cotangent.reshape(seq_count, seq_len, model_width)

    def pick(blocks):
        rows = jnp.einsum("skl,sld->skd", hot_low, blocks, preferred_element_type=f32)
        return rows.astype(bf16).reshape(-1, model_width)

    def place(blocks, rows):
        rows = rows.reshape(seq_count, top_count, model_width)
        spread = jnp.einsum("skl,skd->sld", hot_low, rows, preferred_element_type=f32).astype(bf16)
        taken = jnp.any(hot, axis=1)
        return jnp.where(taken[:, :, None], spread, blocks).reshape(-1, model_width)

    take_a = start(gather, chunk_a, z, split_a, True)
    take_c = start(gather_pairs, chunk_c, z)
    picked = pick(tok_blocks)
    back_rows = pick(back_blocks)
    seg_sel = jnp.sum(jnp.where(hot, segments[:, None, :], 0), axis=-1)
    seg_row, seg_col = seg_sel[:, None, :], seg_sel[:, :, None]
    spot = jnp.arange(model_width, dtype=jnp.int32)
    half, eighth = model_width // 2, model_width // 8
    flip = spot % half // eighth * 2 + spot // half
    order = ((me[0] ^ flip) * eighth + spot % eighth)[None]
    inputs = (picked, back_rows, seg_row, seg_col, order, chunk_b)
    inputs = tick([take_a], inputs)
    take_b = start(gather, inputs[-1], z, split_b, False)
    inputs = tick([take_a, take_b, take_c], inputs[:-1])
    inputs = tick([take_a, take_b], inputs)
    inputs = tick([take_a, take_b, take_c], inputs)

    all_a = whole(take_a, chunk_a, split_a)
    picked, back_rows = inputs[:2]
    order = inputs[4]
    state = attend(me, all_a, *inputs)
    state = tick([take_b, take_c], state)
    own, send, df, gate, vec, added, h2, all_qkv, all_out, qkv, probs = state
    early = start(exchange, send)
    h2 = stage([take_c], h2)
    h2 = tick([take_b, early], h2)
    (sib,) = early.result if paired else (send,)
    all_b = whole(take_b, chunk_b, split_b)
    g_own, g_send, g_sib, h2_pair, all_up, slope = climb(me, all_b, h2, sib, order)

    def give(chain, name, products, split):
        if paired:
            return Steps(chain(z, *outer(name, products, split)))
        grads = [dot_tn(uncut(one.value(), far.value()), two.value()) for one, two, far, _ in products]
        grad = jnp.concatenate(grads, axis=1)
        grad = lax.psum_scatter(grad, AXES, scatter_dimension=0, tiled=True)
        return grad, jnp.full((8, 128), jnp.sum(grad * grad))

    df_sib = jnp.concatenate([sib[2], sib[3]], axis=1)
    left_c = View(g_sib) if paired else View(g_send)
    give_c = give(
        scatter_pairs, "outer_c", [(View(g_own), View(df), left_c, View(df_sib))], split_c
    )
    slope = stage([give_c], slope)
    slope = tick([take_c], slope)
    slope = tick([take_c], slope)
    all_c = whole(take_c, chunk_c, split_c)
    du, all_down = descend(me, all_c, slope, df)
    dmiddle, da, dg2 = unclimb(all_up, du, picked, added, gate, back_rows, vec)
    new_rows, dlogit, dr = finish_mlp(
        all_down, g_own, g_send, picked, added, gate, back_rows
    )
    du, da, dmiddle, new_rows, dlogit = tick([give_c], (du, da, dmiddle, new_rows, dlogit))
    late_u = start(exchange, du)
    dqkv = unattend(all_out, da, qkv, probs)
    dqkv = tick([late_u], dqkv)
    (du_sib,) = late_u.result if paired else (du,)
    late_q = start(exchange, dqkv, da)
    views = [View(h2_pair, lead=place) for place in range(2)]
    if not paired:
        cols = h2.reshape(h2.shape[0], 4, 2, -1)
        views = [View(cols[:, :, core].reshape(h2.shape[0], -1)) for core in range(2)]
    give_b = give(
        scatter_pairs, "outer_b", [(views[0], View(du), views[1], View(du_sib))], split_b
    )
    dqkv = stage([give_b, give_c], dqkv)
    grad_rows, dg1 = finish_rows(all_qkv, dqkv, picked, back_rows, dmiddle, dlogit, vec)
    late_v = start(exchange, dg1, dg2, dr)
    dqkv = stage([late_v], dqkv)
    dqkv = tick([late_q, late_v], dqkv)
    dqkv_sib, da_sib = late_q.result if paired else (dqkv, da)
    products = [
        (View(own, lead=0), View(dqkv), View(sib, lead=0), View(dqkv_sib)),
        (View(own, lead=1), View(da), View(sib, lead=1), View(da_sib)),
    ]
    if paired:
        left, right = vector_columns(order, (dg1, dg2, dr), late_v.result)
        products.append(tuple(View(array, lead=part) for part in range(2) for array in (left, right)))
    give_a = give(scatter, "outer_a", products, split_a)
    grad_rows = stage([give_a], grad_rows)
    grad_rows = tick([give_b, give_c], grad_rows)
    grad_rows, new_rows = stage([give_b, give_c], (grad_rows, new_rows))
    mixed_rows = place(tok_blocks, new_rows)
    grad_rows, mixed_rows = tick([give_a], (grad_rows, mixed_rows))
    grad_rows = stage([give_a], grad_rows)
    grad_rows = tick([give_b, give_c], grad_rows)
    grad_rows = stage([give_b, give_c], grad_rows)
    grad_rows = tick([give_a, give_c], grad_rows)
    grad_rows = stage([give_a], grad_rows)
    input_grad = place(back_blocks, grad_rows)
    input_grad = tick([give_a, give_b], input_grad)
    input_grad = stage([give_a, give_b], input_grad)
    input_grad = tick([give_a, give_b], input_grad)
    if paired:
        (grad_b, square_b), (grad_c, square_c) = give_b.result, give_c.result
        grad_a, squares, vec_grad = settle_z(*give_a.result, (square_b, square_c), devices_all)
    else:
        rows = jnp.stack([dg1[0], dg2[0], dr[0]], axis=0)
        rows = lax.psum_scatter(rows, AXES, scatter_dimension=1, tiled=True)
        vec_grad = jnp.pad(rows, ((0, 5), (0, 128 - shard_width)))
        (grad_a, square_a), (grad_b, square_b), (grad_c, square_c) = give_a, give_b, give_c
        local_sq = square_a + square_b + square_c + jnp.sum(rows * rows)
        squares = jnp.broadcast_to(local_sq[:1], (devices_all, 128))
    squares = lax.all_to_all(squares, AXES, 0, 0, tiled=True)
    params_all = 4 * model_width * model_width + 2 * model_width * ff_width + 3 * model_width
    selected_all = seq_count * top_count * devices_all
    clip_limit = limit_scale * math.sqrt(params_all * selected_all)
    norm, *news = update(
        squares,
        clip_limit,
        [
            View(grad_a, qkv_width),
            View(grad_a, model_width, qkv_width),
            View(grad_b),
            View(grad_c),
        ],
        [
            (w_qkv, m_qkv, v_qkv),
            (w_out, m_out, v_out),
            (w_up, m_up, v_up),
            (w_down, m_down, v_down),
        ],
        vec_grad,
        (m_vectors, v_vectors),
    )
    return (
        mixed_rows,
        input_grad,
        norm[0, 0],
        *news[0:12:3],
        *news[1:12:3],
        news[12],
        *news[2:12:3],
        news[13],
    )


def solution(mesh):
    placed = (
        P(("wide", "narrow"), None),
        P(("wide", "narrow"), None),
        P(("wide", "narrow"), None),
        P(("wide", "narrow"), None),
        P(("wide", "narrow"), None),
        P(("wide", "narrow"), None),
        P(("wide", "narrow"), None),
        P(("wide", "narrow"), None),
        P(None, ("wide", "narrow")),
        P(("wide", "narrow"), None),
        P(("wide", "narrow"), None),
        P(("wide", "narrow"), None),
        P(("wide", "narrow"), None),
        P(None, ("wide", "narrow")),
        P(("wide", "narrow"), None),
        P(("wide", "narrow"), None),
        P(("wide", "narrow"), None),
        P(("wide", "narrow"), None),
        P(None, ("wide", "narrow")),
    )
    paired = mesh.shape["wide"] == 8 and mesh.shape["narrow"] == 4
    return jax.shard_map(
        functools.partial(per_device, paired),
        mesh=mesh,
        in_specs=placed,
        out_specs=(
            P(("wide", "narrow"), None),
            P(("wide", "narrow"), None),
            P(),
            P(("wide", "narrow"), None),
            P(("wide", "narrow"), None),
            P(("wide", "narrow"), None),
            P(("wide", "narrow"), None),
            P(("wide", "narrow"), None),
            P(("wide", "narrow"), None),
            P(("wide", "narrow"), None),
            P(("wide", "narrow"), None),
            P(None, ("wide", "narrow")),
            P(("wide", "narrow"), None),
            P(("wide", "narrow"), None),
            P(("wide", "narrow"), None),
            P(("wide", "narrow"), None),
            P(None, ("wide", "narrow")),
        ),
        check_vma=False,
    )
```
